128 devices in a mesh: wide: 16 (over z_hi, x, core), narrow: 8 (over z_lo, y).
Axes of the slice: x: 4, y: 4, z: 4 (z_hi: 2, z_lo: 2; z = z_hi * 2 + z_lo), core: 2. Of those that a mesh axis runs over, the one named last changes fastest.
Arguments:
- root_front: float32 [6, 16, 128, 12, 8, 128], P(None, 'wide', None, None, 'narrow'), may hold values from -1 to 67.88225, as said below
- child_update: float32 [16, 3, 16, 64, 12, 8, 64], P('wide', None, None, None, None, 'narrow'), may hold values from -0.5 to 1.5, as said below
- child_map: int32 [8, 6144], replicated, may hold values from 0 to 12287, as said below
Outputs:
- factored: float32 [6, 16, 128, 12, 8, 128], P(None, 'wide', None, None, 'narrow')
The draws below stay inside these ranges and needn't reach their ends.
Inputs may be any that keep to these rules, and one draw needn't show every extreme that they name: `child_map`: row g lists 6144 distinct root indices in increasing order, exactly 64 of them in each aligned block of 128 root indices; rows 2h and 2h + 1 together hold every root index once. Read as a matrix, root_front is symmetric with a positive diagonal larger than its other entries. `child_update`: each S_g is symmetric with a positive diagonal.
All inputs are finite; a program needn't handle non-finite values.
Results may differ from the reference program's by a relative error of at most 0.0001.
Values sent between devices are 32-bit elements; how exact they have to be, the bound alone decides.
A program may use at most 192 MiB of HBM per device.

```python
import jax
import jax.numpy as jnp
from jax import lax

ROOT = 12288
CHILDREN = 8
BLOCK = 128
PANEL = 256
PANELS = 2
CHILD = 6144
HALF = 64
SPLIT = 2
ROW_BLOCKS = 6
COL_BLOCKS = 12
PAIR_BLOCKS = 3
N_WIDE = 16
N_NARROW = 8


def draw_root_front(key, part):
    key = jax.random.fold_in(key, 11)
    first_key, second_key = jax.random.split(key, 2)
    raw_values = jax.random.uniform(first_key, (ROOT, ROOT), jnp.float32, -1.0, 1.0)
    diag_scale = jax.random.uniform(second_key, (ROOT,), jnp.float32, 1.5, 3.0)
    mixed_values = 0.5 * (raw_values + raw_values.T)
    id_values = jnp.arange(ROOT)
    diag_values = (2.0 * PANEL) ** 0.5 * diag_scale
    matrix = jnp.where(id_values[:, None] == id_values[None, :], diag_values[:, None], mixed_values)
    return matrix.reshape(ROW_BLOCKS, N_WIDE, BLOCK, COL_BLOCKS, N_NARROW, BLOCK).astype(jnp.float32)


def draw_child_update(key, part):
    key = jax.random.fold_in(key, 17)
    group_keys = jax.random.split(key, CHILDREN)

    def draw_group(group_key):
        first_key, second_key = jax.random.split(group_key, 2)
        raw_values = jax.random.uniform(first_key, (CHILD, CHILD), jnp.float32, -0.5, 0.5)
        diag_values = jax.random.uniform(second_key, (CHILD,), jnp.float32, 0.5, 1.5)
        mixed_values = 0.5 * (raw_values + raw_values.T)
        id_values = jnp.arange(CHILD)
        return jnp.where(id_values[:, None] == id_values[None, :], diag_values[:, None], mixed_values)
    blocks_full = lax.map(draw_group, group_keys)
    shaped = blocks_full.reshape(CHILDREN, PAIR_BLOCKS, SPLIT, N_WIDE, HALF, COL_BLOCKS, N_NARROW, HALF)
    shaped = shaped.transpose(0, 2, 1, 3, 4, 5, 6, 7)
    return shaped.reshape(N_WIDE, PAIR_BLOCKS, N_WIDE, HALF, COL_BLOCKS, N_NARROW, HALF).astype(jnp.float32)


def draw_child_map(key, part):
    key = jax.random.fold_in(key, 29)
    pair_count = CHILDREN // 2
    blocks_all = ROOT // BLOCK
    scores = jax.random.randint(key, (pair_count, blocks_all, BLOCK), 0, 1 << 20, dtype=jnp.int32) * BLOCK + jnp.arange(BLOCK, dtype=jnp.int32)
    order_perm = jnp.argsort(scores, axis=-1).astype(jnp.int32)
    first_half = jnp.sort(order_perm[..., :HALF], axis=-1)
    second_half = jnp.sort(order_perm[..., HALF:], axis=-1)
    starts = (jnp.arange(blocks_all, dtype=jnp.int32) * BLOCK)[None, :, None]
    both_halves = jnp.stack([first_half + starts, second_half + starts], axis=1)
    return both_halves.reshape(CHILDREN, CHILD).astype(jnp.int32)


def setup_inputs(seed: int = 0) -> dict:
    seeds = jax.random.split(jax.random.key(seed), 4)
    return {
        "root_front": draw_root_front(jax.random.fold_in(seeds[3], 71), 0),
        "child_update": draw_child_update(jax.random.fold_in(seeds[3], 71), 0),
        "child_map": draw_child_map(jax.random.fold_in(seeds[3], 71), 0),
    }


def reference(root_front, child_update, child_map):
    front_now = root_front.reshape(ROOT, ROOT)
    for group_id in range(CHILDREN):
        block_part = child_update[group_id * SPLIT:(group_id + 1) * SPLIT]
        update = jnp.transpose(block_part, (1, 0, 2, 3, 4, 5, 6)).reshape(CHILD, CHILD)
        places = child_map[group_id].astype(jnp.int32)
        front_now = front_now.at[places[:, None], places[None, :]].add(update)
    row_ids = jnp.arange(ROOT, dtype=jnp.int32)
    panel_ids = jnp.arange(PANEL, dtype=jnp.int32)
    factor_parts = []
    for panel_step in range(PANELS):
        first_col = panel_step * PANEL
        diagonal = front_now[first_col:first_col + PANEL, first_col:first_col + PANEL]
        factor = jnp.linalg.cholesky(diagonal)
        solved = lax.linalg.triangular_solve(factor, front_now[:, first_col:first_col + PANEL], left_side=False, lower=True, transpose_a=True)
        keep_mask = row_ids[:, None] - first_col >= panel_ids[None, :]
        factor_rows = jnp.where(keep_mask, solved, 0.0)
        trimmed = jnp.where((row_ids >= first_col + PANEL)[:, None], factor_rows, 0.0)
        front_now = front_now - jnp.dot(trimmed, trimmed.T, precision=lax.Precision.HIGHEST)
        factor_parts.append(factor_rows)
    span_cols = PANELS * PANEL
    lower_all = jnp.concatenate(factor_parts, axis=1)
    span_ids = jnp.arange(span_cols, dtype=jnp.int32)
    left_side = jnp.where(row_ids[:, None] >= span_ids[None, :], lower_all, front_now[:, :span_cols])
    front_now = front_now.at[:, :span_cols].set(left_side)
    top_side = jnp.where(span_ids[:, None] < row_ids[None, :], lower_all.T, front_now[:span_cols, :])
    front_now = front_now.at[:span_cols, :].set(top_side)
    return front_now.reshape(root_front.shape)
```

```python
import functools

import jax
import jax.numpy as jnp
from jax import lax
from jax.experimental import pallas as pl
from jax.experimental.pallas import tpu as pltpu
from jax.sharding import PartitionSpec as P

BLOCK = 128
HALF = 64
ROW_BLOCKS = 6
COL_BLOCKS = 12
CHILDREN = 8
N_WIDE = 16
N_NARROW = 8
SPAN = 512
CHUNK = HALF * COL_BLOCKS
MESH = pl.DeviceIdType.MESH
F32 = jnp.float32
BF16 = jnp.bfloat16


def mod(value, n):
    return lax.rem(value, n)


def shift_of(p, q):
    return p // 8 + (mod(p, 8) > q).astype(jnp.int32)


def halves(value):
    high = value.astype(BF16)
    low = (value - high.astype(F32)).astype(BF16)
    return high, low


def dot3(a, b, dims):
    ah, al = halves(a)
    bh, bl = halves(b)
    spec = (dims, ((), ()))
    total = lax.dot_general(ah, bh, spec, preferred_element_type=F32)
    total += lax.dot_general(ah, bl, spec, preferred_element_type=F32)
    total += lax.dot_general(al, bh, spec, preferred_element_type=F32)
    return total


def dot_full(a, b, dims):
    return lax.dot_general(
        a, b, (dims, ((), ())), precision=lax.Precision.HIGHEST, preferred_element_type=F32
    )


def thirds(value):
    high = value.astype(BF16).astype(F32)
    rest = value - high
    mid = rest.astype(BF16).astype(F32)
    low = rest - mid
    return high, mid, low


def factor_128(pair):
    lane = lax.broadcasted_iota(jnp.int32, (8, 128), 1)
    sub = lax.broadcasted_iota(jnp.int32, (8, 128), 0)

    def step(b, carry):
        first = pl.multiple_of(b * 8, 8)
        rows = pair[pl.ds(first, 8), :]
        rows_a = rows[:, :128]
        rows_b = rows[:, 128:]
        turned = pltpu.roll(rows_a, mod(128 - first, 128), 1)
        cols = [jnp.broadcast_to(turned[:, j : j + 1], (8, 128)) for j in range(8)]
        e = {}
        for a in range(8):
            for j in range(a + 1):
                e[a, j] = jnp.broadcast_to(cols[j][a : a + 1, :], (8, 128))
        inv = []
        low = {}
        for j in range(8):
            d = e[j, j]
            r = lax.rsqrt(d)
            r = r * (1.5 - 0.5 * d * r * r)
            inv.append(r)
            for a in range(j + 1, 8):
                low[a, j] = e[a, j] * r
            for a in range(j + 1, 8):
                for c in range(j + 1, a + 1):
                    e[a, c] = e[a, c] - low[a, j] * low[c, j]
        ups_a = []
        ups_b = []
        out_a = jnp.zeros((8, 128), F32)
        out_b = jnp.zeros((8, 128), F32)
        for a in range(8):
            row_a = jnp.broadcast_to(rows_a[a : a + 1, :], (8, 128))
            row_b = jnp.broadcast_to(rows_b[a : a + 1, :], (8, 128))
            for j in range(a):
                row_a = row_a - low[a, j] * ups_a[j]
                row_b = row_b - low[a, j] * ups_b[j]
            row_a = row_a * inv[a]
            row_b = row_b * inv[a]
            ups_a.append(row_a)
            ups_b.append(row_b)
            out_a = jnp.where(sub == a, row_a, out_a)
            out_b = jnp.where(sub == a, row_b, out_b)
        done = jnp.concatenate([out_a, out_b], axis=1)
        pair[pl.ds(first, 8), :] = done
        mult = jnp.where(lane >= first + 8, out_a, 0.0)
        mh, mm, ml = thirds(mult)
        uh, um, ul = thirds(done)
        left = jnp.concatenate([mh, mh, mm, mh, ml, mm], axis=0).astype(BF16)
        right = jnp.concatenate([uh, um, uh, ul, uh, um], axis=0).astype(BF16)
        gone = lax.dot_general(
            left, right, (((0,), (0,)), ((), ())), preferred_element_type=F32
        )
        pair[...] = pair[...] - gone
        return carry

    lax.fori_loop(0, 16, step, 0)


def factor_block(jb, work, pair):
    at = jb * 128
    eye = (
        lax.broadcasted_iota(jnp.int32, (128, 128), 0)
        == lax.broadcasted_iota(jnp.int32, (128, 128), 1)
    ).astype(F32)
    pair[:, 0:128] = work[at : at + 128, at : at + 128]
    pair[:, 128:256] = eye
    factor_128(pair)
    inverse = pair[:, 128:256]
    if jb:
        work[at : at + 128, SPAN : SPAN + at] = dot_full(
            inverse, work[at : at + 128, SPAN : SPAN + at], ((1,), (0,))
        )
    work[at : at + 128, SPAN + at : SPAN + at + 128] = inverse
    if jb < 3:
        rest = at + 128
        above = dot_full(inverse, work[at : at + 128, rest:SPAN], ((1,), (0,)))
        work[rest:SPAN, rest:SPAN] -= dot_full(above, above, ((0,), (0,)))
        work[rest:SPAN, SPAN : SPAN + rest] -= dot_full(
            above, work[at : at + 128, SPAN : SPAN + rest], ((0,), (0,))
        )


def kernel(
    child_map, child, root, out,
    marks, row_offs, col_places, chunk_buf, front, bulk_out, bulk_in, unit_in, front_out, front_in, cols, diag, rows, work,
    pair, wide_buf, pick, rows_f, rows_h, rows_l, cols_h, cols_l,
    s_marks, s_chunk, s_front, s_out, bulk_s, bulk_r, unit_s, unit_r, front_s, front_r,
    cols_s, cols_r, hand_s, dz_s, dz_r, dy_s, dy_r, r1_s, r1_r, rz_s, rz_r, ry_s, ry_r,
):
    p = lax.axis_index("wide")
    q = lax.axis_index("narrow")
    core = mod(p, 2)
    chip = p // 2
    ph = p // 8
    pl8 = mod(p, 8)
    zl = q // 4
    y = mod(q, 4)
    own = pl8 == q
    shift = shift_of(p, q)
    q_other = mod(q + 4, 8)

    def remote(src, dst, ssem, rsem, wide, narrow):
        return pltpu.make_async_remote_copy(
            src_ref=src, dst_ref=dst, send_sem=ssem, recv_sem=rsem,
            device_id=(wide, narrow), device_id_type=MESH,
        )

    def local(src, dst, sem):
        return pltpu.make_async_copy(src, dst, sem)

    def chunk_of(n):
        k = n // 16
        late = jnp.where(n < 4, n, 4 + mod(p + n, 12))
        dest = jnp.where(n < 16, late, mod(p + n, 16))
        return k, dest

    def chunk_copy(n):
        k, dest = chunk_of(n)
        at = pl.multiple_of((k * 16 + dest) * CHUNK, CHUNK)
        slot = mod(n, 4)
        to = pl.multiple_of(slot * CHUNK, CHUNK)
        return local(child.at[pl.ds(at, CHUNK)], chunk_buf.at[pl.ds(to, CHUNK)], s_chunk.at[slot])

    for n in range(4):
        chunk_copy(jnp.int32(n)).start()
    marks_load = local(child_map, marks, s_marks.at[0])
    marks_load.start()
    front_load = local(root, front, s_front.at[0])
    front_load.start()

    barrier = pltpu.get_barrier_semaphore()

    def greet(wide, narrow):
        pl.semaphore_signal(barrier, inc=1, device_id=(wide, narrow), device_id_type=MESH)

    def greet_wide(i, carry):
        greet(mod(p + i, 16), q)
        return carry

    lax.fori_loop(1, 16, greet_wide, 0)
    for i in range(1, 4):
        greet(p, zl * 4 + mod(y + i, 4))
    greet(p, q_other)
    pl.semaphore_wait(barrier, 19)

    def packed(n, la, lb):
        base = mod(n, 4) * CHUNK
        xa = chunk_buf[pl.ds(base + la, HALF, stride=COL_BLOCKS), :]
        xb = chunk_buf[pl.ds(base + lb, HALF, stride=COL_BLOCKS), :]
        return jnp.concatenate([xa, xb], axis=1)

    def next_chunk(n):
        @pl.when(n + 4 < 48)
        def _():
            chunk_copy(n + 4).start()

    def unit_copy(u):
        slot = u // 8
        owner = mod(u, 8) * 2 + (slot > 0).astype(jnp.int32)
        return owner, remote(
            bulk_out.at[mod(u, 4) * 3, u // 4], unit_in.at[slot * 8 + chip], unit_s.at[u], unit_r.at[slot * 8 + chip],
            owner, q,
        )

    def front_copy(m):
        u = m * 4 + p
        slot = u // 8
        owner = mod(u, 8) * 2 + (slot > 0).astype(jnp.int32)
        return owner, slot, remote(
            front_out.at[m], front_in.at[slot], front_s.at[m], front_r.at[slot], owner, q
        )

    def bulk_copy(k, dest):
        kk = 2 * k + core
        return remote(
            bulk_out.at[dest * 3 + k], bulk_in.at[kk * 8 + chip],
            bulk_s.at[dest * 3 + k], bulk_r.at[kk * 8 + chip], dest, q,
        )

    def panel_row(kk, dest):
        return jnp.logical_and(kk == 0, dest < 4)

    def pack(n, carry):
        chunk_copy(n).wait()
        k, dest = chunk_of(n)

        def one(m, c):
            bulk_out[dest * 3 + k, m] = packed(n, 2 * m, 2 * m + 1)
            return c

        lax.fori_loop(0, 6, one, 0)

        @pl.when(panel_row(2 * k + core, dest))
        def _():
            def unit(m, c):
                u = m * 4 + dest
                owner, copy = unit_copy(u)

                @pl.when(owner != p)
                def _():
                    copy.start()

                @pl.when(owner == p)
                def _():
                    unit_in[(u // 8) * 8 + chip] = bulk_out[dest * 3, m]
                return c

            lax.fori_loop(0, 6, unit, 0)
        next_chunk(n)
        return carry

    def fire(n, carry):
        k, dest = chunk_of(n)
        kk = 2 * k + core

        @pl.when(jnp.logical_not(panel_row(kk, dest)))
        def _():
            @pl.when(dest != p)
            def _():
                bulk_copy(k, dest).start()

            @pl.when(dest == p)
            def _():
                bulk_in[kk * 8 + chip] = bulk_out[dest * 3 + k]
        return carry

    lax.fori_loop(0, 4, pack, 0)
    front_load.wait()

    @pl.when(p < 4)
    def _():
        def one(m, c):
            for h in range(2):
                front_out[m, :, h * 128 : h * 128 + 128] = front[
                    pl.ds(2 * m + h, BLOCK, stride=COL_BLOCKS), :
                ]
            owner, slot, copy = front_copy(m)

            @pl.when(owner != p)
            def _():
                copy.start()

            @pl.when(owner == p)
            def _():
                front_in[slot] = front_out[m]
            return c

        lax.fori_loop(0, 6, one, 0)

    level = lax.broadcasted_iota(jnp.int32, (128, 128), 0)

    def set_pick(row):
        for j in range(4):
            table = jnp.where(row_offs[row, j : j + 1, :] == level, 1.0, 0.0).astype(BF16)
            pick[:, j * 128 : j * 128 + 128] = table
            pick[:, 512 + j * 128 : 640 + j * 128] = table

    def assemble(source, m):
        for g in range(CHILDREN):
            value = source(g)
            for h in range(2):
                place = jnp.broadcast_to(col_places[2 * m + h, g : g + 1, :], (HALF, 128))
                taken = jnp.take_along_axis(
                    value, jnp.maximum(place, 0), axis=1, mode="promise_in_bounds"
                )
                high, low = halves(jnp.where(place >= 0, taken, 0.0))
                wide_buf[g * 64 : g * 64 + 64, h * 128 : h * 128 + 128] = high
                wide_buf[512 + g * 64 : 576 + g * 64, h * 128 : h * 128 + 128] = low
        return jnp.dot(pick[...], wide_buf[...], preferred_element_type=F32)

    def cols_at(u):
        return cols.at[u // 4, pl.ds(pl.multiple_of(mod(u, 4) * 128, 128), 128), :]

    def cols_copy(u, dc):
        return remote(
            cols_at(u), cols_at(u), cols_s.at[(u // 8) * 8 + dc], cols_r.at[u],
            mod(chip + dc, 8) * 2 + core, q,
        )

    def hand_copy(u):
        return remote(cols_at(u), cols_at(u), hand_s.at[u], cols_r.at[u], chip * 2 + 1 - core, q)

    def own_unit(slot, carry):
        u = slot * 8 + chip
        block = mod(u, 4)

        def landed(g, c):
            @pl.when(jnp.logical_or(core == 1, g != chip))
            def _():
                remote(
                    bulk_out.at[0, 0], unit_in.at[slot * 8 + g], unit_s.at[0],
                    unit_r.at[slot * 8 + g], g * 2, q,
                ).wait_recv()
            return c

        lax.fori_loop(0, 8, landed, 0)

        @pl.when(block != p)
        def _():
            remote(
                front_out.at[0], front_in.at[slot], front_s.at[0], front_r.at[slot], block, q
            ).wait_recv()

        set_pick(6)
        total = assemble(lambda g: unit_in[slot * 8 + g], u // 4)
        cols[u // 4, pl.ds(pl.multiple_of(block * 128, 128), 128), :] = total + front_in[slot]

        def send(dc, c):
            cols_copy(u, dc).start()
            return c

        lax.fori_loop(1, 8, send, 0)
        hand_copy(u).start()
        return carry

    def hand_on(u, carry):
        @pl.when(mod(u, 8) != chip)
        def _():
            cols_copy(u, 1).wait_recv()
            hand_copy(u).start()
        return carry

    def taken(u, carry):
        hand_copy(u).wait_recv()
        return carry

    first_slot = core
    last_slot = 1 + 2 * core

    marks_load.wait()
    lanes = lax.broadcasted_iota(jnp.int32, (CHILDREN, 128), 1)

    def block_marks(block):
        at = pl.multiple_of((block // 2) * 128, 128)
        part = marks[:, pl.ds(at, 128)]
        turned = pltpu.roll(part, 64, 1)
        return (
            jnp.where(mod(block, 2) == 0, part, turned) - block * BLOCK,
            jnp.where(mod(block, 2) == 0, turned, part) - block * BLOCK,
        )

    def row_table(i, carry):
        block = jnp.where(i < 6, i * 16 + p, mod(chip, 4))
        first, second = block_marks(block)
        for j in range(4):
            row_offs[i, j : j + 1, :] = jnp.where(
                lanes[0:1] < 64, first[2 * j : 2 * j + 1], second[2 * j + 1 : 2 * j + 2]
            )
        return carry

    lax.fori_loop(0, 7, row_table, 0)
    ranks = lax.broadcasted_iota(jnp.int32, (HALF, 128), 0)
    spots = lax.broadcasted_iota(jnp.int32, (HALF, 128), 1)

    def col_table(l, carry):
        first, _ = block_marks(l * 8 + q)
        tall = first.T
        for g in range(CHILDREN):
            hit = jnp.broadcast_to(tall[0:HALF, g : g + 1], (HALF, 128)) == spots
            place = jnp.where(hit, ranks + mod(l, 2) * HALF, -1)
            col_places[l, g : g + 1, :] = jnp.max(place, axis=0, keepdims=True)
        return carry

    lax.fori_loop(0, 12, col_table, 0)
    lax.fori_loop(4, 16, pack, 0)
    lax.fori_loop(0, 8, fire, 0)
    lax.fori_loop(first_slot, last_slot, own_unit, 0)
    lax.fori_loop(8, 12, fire, 0)
    lax.fori_loop(16, 24, pack, 0)

    @pl.when(core == 0)
    def _():
        lax.fori_loop(0, 4, hand_on, 0)

    @pl.when(core == 1)
    def _():
        lax.fori_loop(0, 4, taken, 0)

    dz = remote(diag.at[y], diag.at[y], dz_s.at[0], dz_r.at[0], p, q_other)

    @pl.when(zl == 0)
    def _():
        diag[y] = cols[0, :, 0:128]
        dz.start()

    @pl.when(zl == 1)
    def _():
        dz.wait_recv()

    def dy(i):
        return remote(diag.at[y], diag.at[y], dy_s.at[i], dy_r.at[y], p, zl * 4 + mod(y + i, 4))

    for i in range(1, 4):
        dy(i).start()

    lax.fori_loop(12, 16, fire, 0)
    lax.fori_loop(24, 48, pack, 0)

    @pl.when(core == 0)
    def _():
        lax.fori_loop(4, 8, hand_on, 0)
        lax.fori_loop(8, 24, taken, 0)

    @pl.when(core == 1)
    def _():
        lax.fori_loop(8, 24, hand_on, 0)
        lax.fori_loop(4, 8, taken, 0)

    def r1(c):
        return remote(
            cols.at[:, pl.ds(c * 128, 128), pl.ds(pl.multiple_of(ph * 128, 128), 128)],
            rows.at[c], r1_s.at[c], r1_r.at[0], p, zl * 4 + c,
        )

    rz = remote(rows.at[y], rows.at[y], rz_s.at[0], rz_r.at[0], p, q_other)

    def ry(i):
        return remote(rows.at[y], rows.at[y], ry_s.at[i], ry_r.at[y], p, zl * 4 + mod(y + i, 4))

    @pl.when(own)
    def _():
        for c in range(4):
            @pl.when(y != c)
            def _():
                r1(c).start()

            @pl.when(y == c)
            def _():
                rows[c] = cols[:, c * 128 : c * 128 + 128, pl.ds(pl.multiple_of(ph * 128, 128), 128)]

    lax.fori_loop(16, 20, fire, 0)

    for i in range(1, 4):
        src = mod(y + i, 4)
        remote(diag.at[src], diag.at[src], dy_s.at[i], dy_r.at[src], p, q_other).wait_recv()

    for c in range(4):
        work[:, c * 128 : c * 128 + 128] = diag[c]
    full = work[:, 0:SPAN]
    work[:, 0:SPAN] = 0.5 * (full + full.T)
    work[:, SPAN:] = jnp.zeros((SPAN, SPAN), F32)

    factor_block(0, work, pair)

    holder = zl == pl8 // 4

    @pl.when(holder)
    def _():
        @pl.when(jnp.logical_not(own))
        def _():
            remote(
                rows.at[y], rows.at[y], r1_s.at[0], r1_r.at[0], p, q_other
            ).wait_recv()
        rz.start()

    lax.fori_loop(20, 26, fire, 0)
    factor_block(1, work, pair)

    @pl.when(jnp.logical_not(holder))
    def _():
        rz.wait_recv()

    for i in range(1, 4):
        ry(i).start()

    lax.fori_loop(26, 48, fire, 0)
    factor_block(2, work, pair)
    factor_block(3, work, pair)

    def sent_unit(slot, carry):
        u = slot * 8 + chip

        def one(dc, c):
            cols_copy(u, dc).wait_send()
            return c

        lax.fori_loop(1, 8, one, 0)
        hand_copy(u).wait_send()
        return carry

    lax.fori_loop(first_slot, last_slot, sent_unit, 0)

    def handed(u, carry):
        @pl.when(mod(u, 8) != chip)
        def _():
            hand_copy(u).wait_send()
        return carry

    @pl.when(core == 0)
    def _():
        lax.fori_loop(0, 8, handed, 0)

    @pl.when(core == 1)
    def _():
        lax.fori_loop(8, 24, handed, 0)

    @pl.when(zl == 0)
    def _():
        dz.wait_send()

    for i in range(1, 4):
        dy(i).wait_send()

    @pl.when(own)
    def _():
        for c in range(4):
            @pl.when(y != c)
            def _():
                r1(c).wait_send()

    @pl.when(holder)
    def _():
        rz.wait_send()

    for i in range(1, 4):
        ry(i).wait_send()

    for i in range(1, 4):
        src = mod(y + i, 4)
        remote(rows.at[src], rows.at[src], ry_s.at[i], ry_r.at[src], p, q_other).wait_recv()

    def solve_rows(kk, carry):
        block = jnp.concatenate([rows[c, kk] for c in range(4)], axis=0)
        turned = dot3(work[:, SPAN:], block, ((1,), (0,))).T
        at = pl.multiple_of(kk * 128, 128)
        high, low = halves(turned)
        rows_h[pl.ds(at, 128), :] = high
        rows_l[pl.ds(at, 128), :] = low
        for c in range(4):
            rows_f[c, pl.ds(at, 128), :] = turned[:, c * 128 : c * 128 + 128]
        return carry

    lax.fori_loop(0, 6, solve_rows, 0)

    def solve_cols(m, carry):
        solved = dot3(work[:, SPAN:], cols[m], ((1,), (0,)))
        high, low = halves(solved)
        cols[m] = solved
        cols_h[m] = high
        cols_l[m] = low
        return carry

    lax.fori_loop(0, 6, solve_cols, 0)

    def store(kk):
        at = pl.multiple_of(kk * (128 * COL_BLOCKS), 128 * COL_BLOCKS)
        span = pl.ds(at, 128 * COL_BLOCKS)
        return local(front.at[span], out.at[span], s_out.at[kk])

    def finish(kk, carry):
        at = pl.multiple_of(kk * 128, 128)
        panel = panel_row(kk, p)

        @pl.when(jnp.logical_not(panel))
        def _():
            def landed(g, c):
                @pl.when(jnp.logical_not(jnp.logical_and(g == chip, mod(kk, 2) == core)))
                def _():
                    remote(
                        bulk_out.at[0], bulk_in.at[kk * 8 + g], bulk_s.at[0],
                        bulk_r.at[kk * 8 + g], g * 2 + mod(kk, 2), q,
                    ).wait_recv()
                return c

            lax.fori_loop(0, 8, landed, 0)
            set_pick(kk)

            def one(m, c):
                total = assemble(lambda g: bulk_in[kk * 8 + g, m], m)
                high = rows_h[pl.ds(at, 128), :]
                total -= jnp.dot(high, cols_h[m], preferred_element_type=F32)
                total -= jnp.dot(high, cols_l[m], preferred_element_type=F32)
                total -= jnp.dot(rows_l[pl.ds(at, 128), :], cols_h[m], preferred_element_type=F32)
                for h in range(2):
                    where = pl.ds(kk * (128 * COL_BLOCKS) + 2 * m + h, BLOCK, stride=COL_BLOCKS)
                    front[where, :] = front[where, :] + total[:, h * 128 : h * 128 + 128]
                return c

            lax.fori_loop(0, 6, one, 0)

        @pl.when(panel)
        def _():
            for l in range(COL_BLOCKS):
                @pl.when(l * 8 + q > p)
                def _():
                    front[pl.ds(l, BLOCK, stride=COL_BLOCKS), :] = cols[
                        l // 2, pl.ds(pl.multiple_of(p * 128, 128), 128),
                        (l % 2) * 128 : (l % 2) * 128 + 128,
                    ]

        @pl.when(jnp.logical_and(q < 4, kk * 16 + p > q))
        def _():
            front[pl.ds(kk * (128 * COL_BLOCKS), BLOCK, stride=COL_BLOCKS), :] = rows_f[
                q, pl.ds(at, 128), :
            ]

        @pl.when(jnp.logical_and(q < 4, kk * 16 + p == q))
        def _():
            tile = rows_f[q, 0:128, :]
            lower = lax.broadcasted_iota(jnp.int32, (128, 128), 0) >= lax.broadcasted_iota(
                jnp.int32, (128, 128), 1
            )
            front[pl.ds(0, BLOCK, stride=COL_BLOCKS), :] = jnp.where(lower, tile, tile.T)

        store(kk).start()
        return carry

    lax.fori_loop(0, 6, finish, 0)

    def sent_bulk(n, carry):
        k, dest = chunk_of(n)

        @pl.when(jnp.logical_not(jnp.logical_or(dest == p, panel_row(2 * k + core, dest))))
        def _():
            bulk_copy(k, dest).wait_send()
        return carry

    lax.fori_loop(0, 48, sent_bulk, 0)

    @pl.when(core == 0)
    def _():
        def one(u, c):
            owner, copy = unit_copy(u)

            @pl.when(owner != p)
            def _():
                copy.wait_send()
            return c

        lax.fori_loop(0, 24, one, 0)

    @pl.when(p < 4)
    def _():
        def one(m, c):
            owner, slot, copy = front_copy(m)

            @pl.when(owner != p)
            def _():
                copy.wait_send()
            return c

        lax.fori_loop(0, 6, one, 0)

    def stored(kk, carry):
        store(kk).wait()
        return carry

    lax.fori_loop(0, 6, stored, 0)


def plain_copy(src, dst):
    dst[...] = src[...]


def body(root_front, child_update, child_map):
    child = child_update.reshape(3 * 16 * CHUNK, HALF)
    root = root_front.reshape(ROW_BLOCKS * BLOCK * COL_BLOCKS, BLOCK)
    vmem = lambda *shape: pltpu.VMEM(shape, F32)
    sems = lambda n: pltpu.SemaphoreType.DMA((n,))
    out = pl.pallas_call(
        kernel,
        out_shape=jax.ShapeDtypeStruct(root.shape, F32),
        in_specs=[pl.BlockSpec(memory_space=pl.ANY)] * 3,
        out_specs=pl.BlockSpec(memory_space=pl.ANY),
        scratch_shapes=[
            pltpu.VMEM((CHILDREN, 6144), jnp.int32),
            pltpu.VMEM((8, 4, 128), jnp.int32),
            pltpu.VMEM((COL_BLOCKS, CHILDREN, 128), jnp.int32),
            vmem(4 * CHUNK, HALF),
            vmem(ROW_BLOCKS * BLOCK * COL_BLOCKS, BLOCK),
            vmem(48, 6, HALF, 128),
            vmem(48, 6, HALF, 128),
            vmem(24, HALF, 128),
            vmem(6, BLOCK, 256),
            vmem(3, BLOCK, 256),
            vmem(6, SPAN, 256),
            vmem(4, SPAN, 128),
            vmem(4, 6, BLOCK, BLOCK),
            vmem(SPAN, 2 * SPAN),
            vmem(BLOCK, 2 * BLOCK),
            pltpu.VMEM((1024, 256), BF16),
            pltpu.VMEM((BLOCK, 1024), BF16),
            vmem(4, 768, BLOCK),
            pltpu.VMEM((768, SPAN), BF16),
            pltpu.VMEM((768, SPAN), BF16),
            pltpu.VMEM((6, SPAN, 256), BF16),
            pltpu.VMEM((6, SPAN, 256), BF16),
            sems(1), sems(4), sems(1), sems(6), sems(48), sems(48), sems(24), sems(24),
            sems(6), sems(3), sems(24), sems(24), sems(24), sems(1), sems(1), sems(4), sems(4),
            sems(4), sems(1), sems(1), sems(1), sems(4), sems(4),
        ],
        compiler_params=pltpu.CompilerParams(
            collective_id=0, has_side_effects=True, vmem_limit_bytes=60 * 2**20
        ),
    )(child_map, child, root)
    part = pl.BlockSpec((BLOCK * COL_BLOCKS, BLOCK), lambda i: (i, 0))
    out = pl.pallas_call(
        plain_copy,
        grid=(ROW_BLOCKS,),
        out_shape=jax.ShapeDtypeStruct(root.shape, F32),
        in_specs=[part],
        out_specs=part,
    )(out)
    return out.reshape(root_front.shape)


def solution(mesh):
    return jax.shard_map(
        body,
        mesh=mesh,
        in_specs=(
            P(None, "wide", None, None, "narrow", None),
            P("wide", None, None, None, None, "narrow", None),
            P(),
        ),
        out_specs=P(None, "wide", None, None, "narrow", None),
        check_vma=False,
    )
```

```python
import functools

import jax
import jax.numpy as jnp
from jax import lax
from jax.experimental import pallas as pl
from jax.experimental.pallas import tpu as pltpu
from jax.sharding import PartitionSpec as P

BLOCK = 128
HALF = 64
ROW_BLOCKS = 6
COL_BLOCKS = 12
CHILDREN = 8
N_WIDE = 16
N_NARROW = 8
SPAN = 512
CHUNK = HALF * COL_BLOCKS
MESH = pl.DeviceIdType.MESH
F32 = jnp.float32
BF16 = jnp.bfloat16


def mod(value, n):
    return lax.rem(value, n)


def shift_of(p, q):
    return p // 8 + (mod(p, 8) > q).astype(jnp.int32)


def halves(value):
    high = value.astype(BF16)
    low = (value - high.astype(F32)).astype(BF16)
    return high, low


def dot_full(a, b, dims):
    return lax.dot_general(
        a, b, (dims, ((), ())), precision=lax.Precision.HIGHEST, preferred_element_type=F32
    )


def thirds(value):
    high = value.astype(BF16).astype(F32)
    rest = value - high
    mid = rest.astype(BF16).astype(F32)
    low = rest - mid
    return high, mid, low


def factor_128(pair):
    lane = lax.broadcasted_iota(jnp.int32, (8, 128), 1)
    sub = lax.broadcasted_iota(jnp.int32, (8, 128), 0)

    def step(b, carry):
        first = pl.multiple_of(b * 8, 8)
        rows = pair[pl.ds(first, 8), :]
        rows_a = rows[:, :128]
        rows_b = rows[:, 128:]
        turned = pltpu.roll(rows_a, mod(128 - first, 128), 1)
        cols = [jnp.broadcast_to(turned[:, j : j + 1], (8, 128)) for j in range(8)]
        e = {}
        for a in range(8):
            for j in range(a + 1):
                e[a, j] = jnp.broadcast_to(cols[j][a : a + 1, :], (8, 128))
        inv = []
        low = {}
        for j in range(8):
            d = e[j, j]
            r = lax.rsqrt(d)
            r = r * (1.5 - 0.5 * d * r * r)
            inv.append(r)
            for a in range(j + 1, 8):
                low[a, j] = e[a, j] * r
            for a in range(j + 1, 8):
                for c in range(j + 1, a + 1):
                    e[a, c] = e[a, c] - low[a, j] * low[c, j]
        ups_a = []
        ups_b = []
        out_a = jnp.zeros((8, 128), F32)
        out_b = jnp.zeros((8, 128), F32)
        for a in range(8):
            row_a = jnp.broadcast_to(rows_a[a : a + 1, :], (8, 128))
            row_b = jnp.broadcast_to(rows_b[a : a + 1, :], (8, 128))
            for j in range(a):
                row_a = row_a - low[a, j] * ups_a[j]
                row_b = row_b - low[a, j] * ups_b[j]
            row_a = row_a * inv[a]
            row_b = row_b * inv[a]
            ups_a.append(row_a)
            ups_b.append(row_b)
            out_a = jnp.where(sub == a, row_a, out_a)
            out_b = jnp.where(sub == a, row_b, out_b)
        done = jnp.concatenate([out_a, out_b], axis=1)
        pair[pl.ds(first, 8), :] = done
        mult = jnp.where(lane >= first + 8, out_a, 0.0)
        mh, mm, ml = thirds(mult)
        uh, um, ul = thirds(done)
        left = jnp.concatenate([mh, mh, mm, mh, ml, mm], axis=0).astype(BF16)
        right = jnp.concatenate([uh, um, uh, ul, uh, um], axis=0).astype(BF16)
        gone = lax.dot_general(
            left, right, (((0,), (0,)), ((), ())), preferred_element_type=F32
        )
        pair[...] = pair[...] - gone
        return carry

    lax.fori_loop(0, 16, step, 0)


def factor_block(jb, work, pair):
    at = jb * 128
    eye = (
        lax.broadcasted_iota(jnp.int32, (128, 128), 0)
        == lax.broadcasted_iota(jnp.int32, (128, 128), 1)
    ).astype(F32)
    pair[:, 0:128] = work[at : at + 128, at : at + 128]
    pair[:, 128:256] = eye
    factor_128(pair)
    inverse = pair[:, 128:256]
    if jb:
        work[at : at + 128, SPAN : SPAN + at] = dot_full(
            inverse, work[at : at + 128, SPAN : SPAN + at], ((1,), (0,))
        )
    work[at : at + 128, SPAN + at : SPAN + at + 128] = inverse
    if jb < 3:
        rest = at + 128
        above = dot_full(inverse, work[at : at + 128, rest:SPAN], ((1,), (0,)))
        work[rest:SPAN, rest:SPAN] -= dot_full(above, above, ((0,), (0,)))
        work[rest:SPAN, SPAN : SPAN + rest] -= dot_full(
            above, work[at : at + 128, SPAN : SPAN + rest], ((0,), (0,))
        )


def kernel(
    child_map, child, root, out, bulk_in, row_out, col_out,
    marks, row_perms, col_places, chunk_buf, front, bulk_out, unit_in, front_out, front_in, cols, diag, rows, work,
    pair, rows_f, rows_h, rows_l, prod, inv_h, inv_l, relay,
    keep_s, tab_s, s_marks, s_chunk, s_front, s_out, relay_s, relay_r, bulk_s, bulk_r, unit_s, unit_r, front_s, front_r,
    cols_s, cols_r, hand_s, dz_s, dz_r, dy_s, dy_r, r1_s, r1_r, rz_s, rz_r, ry_s, ry_r,
):
    p = lax.axis_index("wide")
    q = lax.axis_index("narrow")
    core = mod(p, 2)
    chip = p // 2
    ph = p // 8
    pl8 = mod(p, 8)
    zl = q // 4
    y = mod(q, 4)
    own = pl8 == q
    shift = shift_of(p, q)
    q_other = mod(q + 4, 8)

    def remote(src, dst, ssem, rsem, wide, narrow):
        return pltpu.make_async_remote_copy(
            src_ref=src, dst_ref=dst, send_sem=ssem, recv_sem=rsem,
            device_id=(wide, narrow), device_id_type=MESH,
        )

    def local(src, dst, sem):
        return pltpu.make_async_copy(src, dst, sem)

    def chunk_of(n):
        k = n // 16
        late = jnp.where(n < 4, n, 4 + mod(p + n, 12))
        dest = jnp.where(n < 16, late, mod(p + n, 16))
        return k, dest

    def chunk_copy(n):
        k, dest = chunk_of(n)
        at = pl.multiple_of((k * 16 + dest) * CHUNK, CHUNK)
        slot = mod(n, 4)
        to = pl.multiple_of(slot * CHUNK, CHUNK)
        return local(child.at[pl.ds(at, CHUNK)], chunk_buf.at[pl.ds(to, CHUNK)], s_chunk.at[slot])

    for n in range(4):
        chunk_copy(jnp.int32(n)).start()
    marks_load = local(child_map, marks, s_marks.at[0])
    marks_load.start()
    front_load = local(root, front, s_front.at[0])
    front_load.start()

    barrier = pltpu.get_barrier_semaphore()

    def greet(wide, narrow):
        pl.semaphore_signal(barrier, inc=1, device_id=(wide, narrow), device_id_type=MESH)

    def greet_wide(i, carry):
        greet(mod(p + i, 16), q)
        return carry

    lax.fori_loop(1, 16, greet_wide, 0)
    for i in range(1, 4):
        greet(p, zl * 4 + mod(y + i, 4))

    def greet_plane(i, carry):
        greet(i, q_other)
        return carry

    lax.fori_loop(0, 16, greet_plane, 0)
    pl.semaphore_wait(barrier, 34)

    def packed(n, la, lb):
        base = mod(n, 4) * CHUNK
        xa = chunk_buf[pl.ds(base + la, HALF, stride=COL_BLOCKS), :]
        xb = chunk_buf[pl.ds(base + lb, HALF, stride=COL_BLOCKS), :]
        return jnp.concatenate([xa, xb], axis=1)

    def next_chunk(n):
        @pl.when(n + 4 < 48)
        def _():
            chunk_copy(n + 4).start()

    def unit_copy(u):
        slot = u // 8
        owner = mod(u, 8) * 2 + (slot > 0).astype(jnp.int32)
        return owner, remote(
            bulk_out.at[mod(u, 4) * 3, u // 4], unit_in.at[slot * 8 + chip], unit_s.at[u], unit_r.at[slot * 8 + chip],
            owner, q,
        )

    def front_copy(m):
        u = m * 4 + p
        slot = u // 8
        owner = mod(u, 8) * 2 + (slot > 0).astype(jnp.int32)
        return owner, slot, remote(
            front_out.at[m], front_in.at[slot], front_s.at[m], front_r.at[slot], owner, q
        )

    zh = ph
    xs = mod(chip, 4)

    def bulk_copy(k, dest):
        kk = 2 * k + core
        return remote(
            bulk_out.at[dest * 3 + k], bulk_in.at[kk * 8 + chip],
            bulk_s.at[dest * 3 + k], bulk_r.at[kk * 8 + chip], dest, q,
        )

    def keep_copy(k):
        return local(bulk_out.at[p * 3 + k], bulk_in.at[(2 * k + core) * 8 + chip], keep_s.at[k])

    def first_copy(k, dest):
        xd = mod(dest // 2, 4)
        far = mod(xd - xs + 6, 4) == 0
        xi = jnp.where(far, mod(xd + 1, 4), xd)
        gap = mod(xs - xi + 4, 4)
        way = jnp.where(far, 3, jnp.where(gap == 3, 2, gap))
        zi = jnp.where(mod(core + xs + k, 2) == 0, zh, 1 - zh)
        slot = k * 8 + way * 2 + core
        return remote(
            bulk_out.at[dest * 3 + k], relay.at[slot], bulk_s.at[dest * 3 + k],
            relay_r.at[slot], (zi * 4 + xi) * 2 + mod(dest, 2), q_other,
        )

    def second_copy(k, way, cs):
        slot = k * 8 + way * 2 + cs
        side = jnp.where(jnp.logical_or(way == 1, way == 3), 1, jnp.where(way == 2, 3, 0))
        source_x = mod(xs + side, 4)
        dest_x = jnp.where(way == 3, mod(xs + 3, 4), xs)
        source_z = jnp.where(mod(cs + source_x + k, 2) == 0, zh, 1 - zh)
        dest = ((1 - source_z) * 4 + dest_x) * 2 + core
        place = (2 * k + cs) * 8 + source_z * 4 + source_x
        return dest, remote(
            relay.at[slot], bulk_in.at[place], relay_s.at[slot], bulk_r.at[place], dest, q_other
        )

    def relay_one(i, carry):
        k, way, cs = i // 8, mod(i, 8) // 2, mod(i, 2)
        dest, copy = second_copy(k, way, cs)

        @pl.when(jnp.logical_not(panel_row(2 * k + cs, dest)))
        def _():
            remote(
                bulk_out.at[0], relay.at[i], bulk_s.at[0], relay_r.at[i], p, q_other
            ).wait_recv()
            copy.start()
        return carry

    def panel_row(kk, dest):
        return jnp.logical_and(kk == 0, dest < 4)

    def pack(n, carry):
        chunk_copy(n).wait()
        k, dest = chunk_of(n)

        def one(m, c):
            bulk_out[dest * 3 + k, m] = packed(n, 2 * m, 2 * m + 1)
            return c

        lax.fori_loop(0, 6, one, 0)

        @pl.when(panel_row(2 * k + core, dest))
        def _():
            def unit(m, c):
                u = m * 4 + dest
                owner, copy = unit_copy(u)

                @pl.when(owner != p)
                def _():
                    copy.start()

                @pl.when(owner == p)
                def _():
                    unit_in[(u // 8) * 8 + chip] = bulk_out[dest * 3, m]
                return c

            lax.fori_loop(0, 6, unit, 0)
        next_chunk(n)
        return carry

    def fire(n, carry):
        k, j = n // 16, mod(n, 16)
        crossing = j < 8
        dest = jnp.where(crossing, 1 - zh, zh) * 8 + mod(p + j, 8)
        kk = 2 * k + core

        @pl.when(jnp.logical_not(panel_row(kk, dest)))
        def _():
            @pl.when(crossing)
            def _():
                first_copy(k, dest).start()

            @pl.when(jnp.logical_and(jnp.logical_not(crossing), dest != p))
            def _():
                bulk_copy(k, dest).start()

            @pl.when(dest == p)
            def _():
                keep_copy(k).start()
        return carry

    lax.fori_loop(0, 4, pack, 0)
    front_load.wait()

    @pl.when(p < 4)
    def _():
        def one(m, c):
            for h in range(2):
                front_out[m, :, h * 128 : h * 128 + 128] = front[
                    pl.ds(2 * m + h, BLOCK, stride=COL_BLOCKS), :
                ]
            owner, slot, copy = front_copy(m)

            @pl.when(owner != p)
            def _():
                copy.start()

            @pl.when(owner == p)
            def _():
                front_in[slot] = front_out[m]
            return c

        lax.fori_loop(0, 6, one, 0)

    def assemble(source, m, row):
        sides = []
        for h in range(2):
            total = jnp.zeros((BLOCK, BLOCK), F32)
            for pair_id in range(CHILDREN // 2):
                parts = []
                for g in (2 * pair_id, 2 * pair_id + 1):
                    place = jnp.broadcast_to(col_places[2 * m + h, g : g + 1, :], (HALF, 128))
                    taken = jnp.take_along_axis(
                        source(g), jnp.maximum(place, 0), axis=1, mode="promise_in_bounds"
                    )
                    parts.append(jnp.where(place >= 0, taken, 0.0))
                turned = jnp.concatenate(parts, axis=0).T
                order = jnp.broadcast_to(row_perms[row, pair_id : pair_id + 1, :], (BLOCK, BLOCK))
                total += jnp.take_along_axis(turned, order, axis=1, mode="promise_in_bounds")
            sides.append(total.T)
        return sides

    def cols_at(u):
        return cols.at[u // 4, pl.ds(pl.multiple_of(mod(u, 4) * 128, 128), 128), :]

    def cols_copy(u, dc):
        return remote(
            cols_at(u), cols_at(u), cols_s.at[(u // 8) * 8 + dc], cols_r.at[u],
            mod(chip + dc, 8) * 2 + core, q,
        )

    def hand_copy(u):
        return remote(cols_at(u), cols_at(u), hand_s.at[u], cols_r.at[u], chip * 2 + 1 - core, q)

    def own_unit(slot, carry):
        u = slot * 8 + chip
        block = mod(u, 4)

        def landed(g, c):
            @pl.when(jnp.logical_or(core == 1, g != chip))
            def _():
                remote(
                    bulk_out.at[0, 0], unit_in.at[slot * 8 + g], unit_s.at[0],
                    unit_r.at[slot * 8 + g], g * 2, q,
                ).wait_recv()
            return c

        lax.fori_loop(0, 8, landed, 0)

        @pl.when(block != p)
        def _():
            remote(
                front_out.at[0], front_in.at[slot], front_s.at[0], front_r.at[slot], block, q
            ).wait_recv()

        sides = assemble(lambda g: unit_in[slot * 8 + g], u // 4, 6)
        cols[u // 4, pl.ds(pl.multiple_of(block * 128, 128), 128), :] = (
            jnp.concatenate(sides, axis=1) + front_in[slot]
        )

        def send(dc, c):
            cols_copy(u, dc).start()
            return c

        lax.fori_loop(1, 8, send, 0)
        hand_copy(u).start()
        return carry

    def hand_on(u, carry):
        @pl.when(mod(u, 8) != chip)
        def _():
            cols_copy(u, 1).wait_recv()
            hand_copy(u).start()
        return carry

    def taken(u, carry):
        hand_copy(u).wait_recv()
        return carry

    first_slot = core
    last_slot = 1 + 2 * core

    marks_load.wait()
    ranks = lax.broadcasted_iota(jnp.int32, (HALF, 128), 0)
    spots = lax.broadcasted_iota(jnp.int32, (HALF, 128), 1)

    def places(block):
        at = pl.multiple_of((block // 2) * 128, 128)
        part = marks[:, pl.ds(at, 128)]
        mine = jnp.where(mod(block, 2) == 0, part, pltpu.roll(part, 64, 1)) - block * BLOCK
        tall = mine.T
        found = []
        for g in range(CHILDREN):
            hit = jnp.broadcast_to(tall[0:HALF, g : g + 1], (HALF, 128)) == spots
            found.append(jnp.max(jnp.where(hit, ranks, -1), axis=0, keepdims=True))
        return found

    def row_table(i, carry):
        found = places(jnp.where(i < 6, i * 16 + p, mod(chip, 4)))
        for j in range(4):
            first, second = found[2 * j], found[2 * j + 1]
            row_perms[i, j : j + 1, :] = jnp.where(first >= 0, first, second + HALF)
        return carry

    lax.fori_loop(0, 7, row_table, 0)

    def col_table(l, carry):
        found = places(l * 8 + q)
        for g in range(CHILDREN):
            col_places[l, g : g + 1, :] = jnp.where(
                found[g] >= 0, found[g] + mod(l, 2) * HALF, -1
            )
        return carry

    lax.fori_loop(0, 12, col_table, 0)
    lax.fori_loop(first_slot, last_slot, own_unit, 0)
    lax.fori_loop(4, 16, pack, 0)

    @pl.when(core == 0)
    def _():
        lax.fori_loop(0, 4, hand_on, 0)

    @pl.when(core == 1)
    def _():
        lax.fori_loop(0, 4, taken, 0)

    dz = remote(diag.at[y], diag.at[y], dz_s.at[0], dz_r.at[0], p, q_other)

    @pl.when(zl == 0)
    def _():
        diag[y] = cols[0, :, 0:128]
        dz.start()

    @pl.when(zl == 1)
    def _():
        dz.wait_recv()

    def dy(i):
        return remote(diag.at[y], diag.at[y], dy_s.at[i], dy_r.at[y], p, zl * 4 + mod(y + i, 4))

    for i in range(1, 4):
        dy(i).start()

    lax.fori_loop(0, 16, fire, 0)
    lax.fori_loop(16, 48, pack, 0)

    @pl.when(core == 0)
    def _():
        lax.fori_loop(4, 8, hand_on, 0)
        lax.fori_loop(8, 24, taken, 0)

    @pl.when(core == 1)
    def _():
        lax.fori_loop(8, 24, hand_on, 0)
        lax.fori_loop(4, 8, taken, 0)

    def r1(c):
        return remote(
            cols.at[:, pl.ds(c * 128, 128), pl.ds(pl.multiple_of(ph * 128, 128), 128)],
            rows.at[c], r1_s.at[c], r1_r.at[0], p, zl * 4 + c,
        )

    rz = remote(rows.at[y], rows.at[y], rz_s.at[0], rz_r.at[0], p, q_other)

    def ry(i):
        return remote(rows.at[y], rows.at[y], ry_s.at[i], ry_r.at[y], p, zl * 4 + mod(y + i, 4))

    @pl.when(own)
    def _():
        for c in range(4):
            @pl.when(y != c)
            def _():
                r1(c).start()

            @pl.when(y == c)
            def _():
                rows[c] = cols[:, c * 128 : c * 128 + 128, pl.ds(pl.multiple_of(ph * 128, 128), 128)]


    for i in range(1, 4):
        src = mod(y + i, 4)
        remote(diag.at[src], diag.at[src], dy_s.at[i], dy_r.at[src], p, q_other).wait_recv()

    for c in range(4):
        work[:, c * 128 : c * 128 + 128] = diag[c]
    full = work[:, 0:SPAN]
    work[:, 0:SPAN] = 0.5 * (full + full.T)
    work[:, SPAN:] = jnp.zeros((SPAN, SPAN), F32)

    factor_block(0, work, pair)

    holder = zl == pl8 // 4

    @pl.when(holder)
    def _():
        @pl.when(jnp.logical_not(own))
        def _():
            remote(
                rows.at[y], rows.at[y], r1_s.at[0], r1_r.at[0], p, q_other
            ).wait_recv()
        rz.start()

    lax.fori_loop(16, 24, fire, 0)
    lax.fori_loop(0, 8, relay_one, 0)
    lax.fori_loop(24, 32, fire, 0)
    factor_block(1, work, pair)

    @pl.when(jnp.logical_not(holder))
    def _():
        rz.wait_recv()

    for i in range(1, 4):
        ry(i).start()

    lax.fori_loop(32, 40, fire, 0)
    factor_block(2, work, pair)
    lax.fori_loop(8, 16, relay_one, 0)
    lax.fori_loop(40, 48, fire, 0)
    factor_block(3, work, pair)
    lax.fori_loop(16, 24, relay_one, 0)

    def sent_unit(slot, carry):
        u = slot * 8 + chip

        def one(dc, c):
            cols_copy(u, dc).wait_send()
            return c

        lax.fori_loop(1, 8, one, 0)
        hand_copy(u).wait_send()
        return carry

    lax.fori_loop(first_slot, last_slot, sent_unit, 0)

    def handed(u, carry):
        @pl.when(mod(u, 8) != chip)
        def _():
            hand_copy(u).wait_send()
        return carry

    @pl.when(core == 0)
    def _():
        lax.fori_loop(0, 8, handed, 0)

    @pl.when(core == 1)
    def _():
        lax.fori_loop(8, 24, handed, 0)

    @pl.when(zl == 0)
    def _():
        dz.wait_send()

    for i in range(1, 4):
        dy(i).wait_send()

    @pl.when(own)
    def _():
        for c in range(4):
            @pl.when(y != c)
            def _():
                r1(c).wait_send()

    @pl.when(holder)
    def _():
        rz.wait_send()

    for i in range(1, 4):
        ry(i).wait_send()

    for i in range(1, 4):
        src = mod(y + i, 4)
        remote(rows.at[src], rows.at[src], ry_s.at[i], ry_r.at[src], p, q_other).wait_recv()

    inverse_h, inverse_l = halves(work[:, SPAN:])
    inv_h[...] = inverse_h
    inv_l[...] = inverse_l

    def solve(block):
        high, low = halves(block)
        total = jnp.dot(inv_h[...], high, preferred_element_type=F32)
        total += jnp.dot(inv_h[...], low, preferred_element_type=F32)
        total += jnp.dot(inv_l[...], high, preferred_element_type=F32)
        return total

    def solve_rows(kk, carry):
        block = jnp.concatenate([rows[c, kk] for c in range(4)], axis=0)
        turned = solve(block).T
        at = pl.multiple_of(kk * 128, 128)
        high, low = halves(turned)
        rows_h[pl.ds(at, 128), :] = high
        rows_l[pl.ds(at, 128), :] = low
        for c in range(4):
            rows_f[c, pl.ds(at, 128), :] = turned[:, c * 128 : c * 128 + 128]
        return carry

    lax.fori_loop(0, 6, solve_rows, 0)

    def solve_cols(m, carry):
        solved = solve(cols[m])
        high, low = halves(solved)
        cols[m] = solved
        total = jnp.dot(rows_h[...], high, preferred_element_type=F32)
        total += jnp.dot(rows_h[...], low, preferred_element_type=F32)
        total += jnp.dot(rows_l[...], high, preferred_element_type=F32)
        prod[...] = total

        def less(kk, c):
            at = pl.multiple_of(kk * 128, 128)
            for h in range(2):
                where = pl.ds(kk * (128 * COL_BLOCKS) + 2 * m + h, BLOCK, stride=COL_BLOCKS)
                front[where, :] = (
                    front[where, :] - prod[pl.ds(at, 128), h * 128 : h * 128 + 128]
                )
            return c

        lax.fori_loop(0, 6, less, 0)
        return carry

    lax.fori_loop(0, 6, solve_cols, 0)

    def store(kk):
        at = pl.multiple_of(kk * (128 * COL_BLOCKS), 128 * COL_BLOCKS)
        span = pl.ds(at, 128 * COL_BLOCKS)
        return local(front.at[span], out.at[span], s_out.at[kk])

    @pl.when(p < 4)
    def _():
        for l in range(COL_BLOCKS):
            @pl.when(l * 8 + q > p)
            def _():
                front[pl.ds(l, BLOCK, stride=COL_BLOCKS), :] = cols[
                    l // 2, pl.ds(pl.multiple_of(p * 128, 128), 128),
                    (l % 2) * 128 : (l % 2) * 128 + 128,
                ]

    @pl.when(q < 4)
    def _():
        for kk in range(ROW_BLOCKS):
            @pl.when(kk * 16 + p > q)
            def _():
                front[pl.ds(kk * (128 * COL_BLOCKS), BLOCK, stride=COL_BLOCKS), :] = rows_f[
                    q, kk * 128 : kk * 128 + 128, :
                ]

        @pl.when(p == q)
        def _():
            tile = rows_f[q, 0:128, :]
            lower = lax.broadcasted_iota(jnp.int32, (128, 128), 0) >= lax.broadcasted_iota(
                jnp.int32, (128, 128), 1
            )
            front[pl.ds(0, BLOCK, stride=COL_BLOCKS), :] = jnp.where(lower, tile, tile.T)

    lax.fori_loop(0, 6, lambda kk, c: (store(kk).start(), c)[1], 0)

    def landed(i, carry):
        kk, g = i // 8, mod(i, 8)
        mine = jnp.logical_and(g == chip, mod(kk, 2) == core)

        @pl.when(jnp.logical_not(jnp.logical_or(mine, panel_row(kk, p))))
        def _():
            remote(
                bulk_out.at[0], bulk_in.at[i], bulk_s.at[0], bulk_r.at[i], g * 2 + mod(kk, 2), q
            ).wait_recv()
        return carry

    lax.fori_loop(0, 48, landed, 0)

    def kept(k, carry):
        @pl.when(jnp.logical_not(panel_row(2 * k + core, p)))
        def _():
            keep_copy(k).wait()
        return carry

    lax.fori_loop(0, 3, kept, 0)
    tables = [
        local(row_perms, row_out, tab_s.at[0]), local(col_places, col_out, tab_s.at[1])
    ]
    for copy in tables:
        copy.start()
    for copy in tables:
        copy.wait()

    def sent_bulk(n, carry):
        k, dest = chunk_of(n)

        @pl.when(jnp.logical_not(jnp.logical_or(dest == p, panel_row(2 * k + core, dest))))
        def _():
            bulk_copy(k, dest).wait_send()
        return carry

    lax.fori_loop(0, 48, sent_bulk, 0)

    @pl.when(core == 0)
    def _():
        def one(u, c):
            owner, copy = unit_copy(u)

            @pl.when(owner != p)
            def _():
                copy.wait_send()
            return c

        lax.fori_loop(0, 24, one, 0)

    @pl.when(p < 4)
    def _():
        def one(m, c):
            owner, slot, copy = front_copy(m)

            @pl.when(owner != p)
            def _():
                copy.wait_send()
            return c

        lax.fori_loop(0, 6, one, 0)

    def relayed(i, carry):
        k, way, cs = i // 8, mod(i, 8) // 2, mod(i, 2)
        dest, copy = second_copy(k, way, cs)

        @pl.when(jnp.logical_not(panel_row(2 * k + cs, dest)))
        def _():
            copy.wait_send()
        return carry

    lax.fori_loop(0, 24, relayed, 0)

    def stored(kk, carry):
        store(kk).wait()
        return carry

    lax.fori_loop(0, 6, stored, 0)


def add_children(row_perms, col_places, front, children, out, pick, wide_buf):
    kk = pl.program_id(0)
    p = lax.axis_index("wide")
    q = lax.axis_index("narrow")
    panel = jnp.logical_and(kk == 0, p < 4)

    @pl.when(panel)
    def _():
        out[...] = front[...]

    @pl.when(jnp.logical_not(panel))
    def _():
        level = lax.broadcasted_iota(jnp.int32, (128, 128), 1)
        for j in range(4):
            order = jnp.broadcast_to(row_perms[kk, j : j + 1, :], (128, 128)).T
            table = jnp.where(order == level, 1.0, 0.0).astype(BF16)
            pick[:, j * 128 : j * 128 + 128] = table
            pick[:, 512 + j * 128 : 640 + j * 128] = table

        def one(m, carry):
            for g in range(CHILDREN):
                for h in range(2):
                    place = jnp.broadcast_to(col_places[2 * m + h, g : g + 1, :], (HALF, 128))
                    taken = jnp.take_along_axis(
                        children[g, m], jnp.maximum(place, 0), axis=1, mode="promise_in_bounds"
                    )
                    high, low = halves(jnp.where(place >= 0, taken, 0.0))
                    wide_buf[g * 64 : g * 64 + 64, h * 128 : h * 128 + 128] = high
                    wide_buf[512 + g * 64 : 576 + g * 64, h * 128 : h * 128 + 128] = low
            total = jnp.dot(pick[...], wide_buf[...], preferred_element_type=F32)
            for h in range(2):
                where = pl.ds(2 * m + h, BLOCK, stride=COL_BLOCKS)
                side = total[:, h * 128 : h * 128 + 128]
                if h == 0:
                    side = jnp.where(jnp.logical_and(m == 0, q < 4), 0.0, side)
                out[where, :] = front[where, :] + side
            return carry

        lax.fori_loop(0, 6, one, 0)


def body(root_front, child_update, child_map):
    child = child_update.reshape(3 * 16 * CHUNK, HALF)
    root = root_front.reshape(ROW_BLOCKS * BLOCK * COL_BLOCKS, BLOCK)
    vmem = lambda *shape: pltpu.VMEM(shape, F32)
    sems = lambda n: pltpu.SemaphoreType.DMA((n,))
    front, children, row_perms, col_places = pl.pallas_call(
        kernel,
        out_shape=[
            jax.ShapeDtypeStruct(root.shape, F32),
            jax.ShapeDtypeStruct((48, 6, HALF, 128), F32),
            jax.ShapeDtypeStruct((8, 4, 128), jnp.int32),
            jax.ShapeDtypeStruct((COL_BLOCKS, CHILDREN, 128), jnp.int32),
        ],
        in_specs=[pl.BlockSpec(memory_space=pl.ANY)] * 3,
        out_specs=[pl.BlockSpec(memory_space=pl.ANY)] * 4,
        scratch_shapes=[
            pltpu.VMEM((CHILDREN, 6144), jnp.int32),
            pltpu.VMEM((8, 4, 128), jnp.int32),
            pltpu.VMEM((COL_BLOCKS, CHILDREN, 128), jnp.int32),
            vmem(4 * CHUNK, HALF),
            vmem(ROW_BLOCKS * BLOCK * COL_BLOCKS, BLOCK),
            vmem(48, 6, HALF, 128),
            vmem(24, HALF, 128),
            vmem(6, BLOCK, 256),
            vmem(3, BLOCK, 256),
            vmem(6, SPAN, 256),
            vmem(4, SPAN, 128),
            vmem(4, 6, BLOCK, BLOCK),
            vmem(SPAN, 2 * SPAN),
            vmem(BLOCK, 2 * BLOCK),
            vmem(4, 768, BLOCK),
            pltpu.VMEM((768, SPAN), BF16),
            pltpu.VMEM((768, SPAN), BF16),
            vmem(768, 256),
            pltpu.VMEM((SPAN, SPAN), BF16),
            pltpu.VMEM((SPAN, SPAN), BF16),
            vmem(24, 6, HALF, 128),
            sems(3), sems(2), sems(1), sems(4), sems(1), sems(6), sems(24), sems(24), sems(48), sems(48), sems(24), sems(24),
            sems(6), sems(3), sems(24), sems(24), sems(24), sems(1), sems(1), sems(4), sems(4),
            sems(4), sems(1), sems(1), sems(1), sems(4), sems(4),
        ],
        compiler_params=pltpu.CompilerParams(
            collective_id=0, has_side_effects=True, vmem_limit_bytes=60 * 2**20
        ),
    )(child_map, child, root)
    part = pl.BlockSpec((BLOCK * COL_BLOCKS, BLOCK), lambda i: (i, 0))
    out = pl.pallas_call(
        add_children,
        grid=(ROW_BLOCKS,),
        out_shape=jax.ShapeDtypeStruct(root.shape, F32),
        in_specs=[
            pl.BlockSpec((8, 4, 128), lambda i: (0, 0, 0)),
            pl.BlockSpec((COL_BLOCKS, CHILDREN, 128), lambda i: (0, 0, 0)),
            part,
            pl.BlockSpec((CHILDREN, 6, HALF, 128), lambda i: (i, 0, 0, 0)),
        ],
        out_specs=part,
        scratch_shapes=[pltpu.VMEM((BLOCK, 1024), BF16), pltpu.VMEM((1024, 256), BF16)],
        compiler_params=pltpu.CompilerParams(vmem_limit_bytes=40 * 2**20),
    )(row_perms, col_places, front, children)
    return out.reshape(root_front.shape)


def solution(mesh):
    return jax.shard_map(
        body,
        mesh=mesh,
        in_specs=(
            P(None, "wide", None, None, "narrow", None),
            P("wide", None, None, None, None, "narrow", None),
            P(),
        ),
        out_specs=P(None, "wide", None, None, "narrow", None),
        check_vma=False,
    )
```

```python
import functools

import jax
import jax.numpy as jnp
from jax import lax
from jax.experimental import pallas as pl
from jax.experimental.pallas import tpu as pltpu
from jax.sharding import PartitionSpec as P

BLOCK = 128
HALF = 64
ROW_BLOCKS = 6
COL_BLOCKS = 12
CHILDREN = 8
N_WIDE = 16
N_NARROW = 8
SPAN = 512
CHUNK = HALF * COL_BLOCKS
MESH = pl.DeviceIdType.MESH
F32 = jnp.float32
BF16 = jnp.bfloat16


def mod(value, n):
    return lax.rem(value, n)


def shift_of(p, q):
    return p // 8 + (mod(p, 8) > q).astype(jnp.int32)


def halves(value):
    high = value.astype(BF16)
    low = (value - high.astype(F32)).astype(BF16)
    return high, low


def dot_full(a, b, dims):
    return lax.dot_general(
        a, b, (dims, ((), ())), precision=lax.Precision.HIGHEST, preferred_element_type=F32
    )


def thirds(value):
    high = value.astype(BF16).astype(F32)
    rest = value - high
    mid = rest.astype(BF16).astype(F32)
    low = rest - mid
    return high, mid, low


def factor_128(pair, beside):
    lane = lax.broadcasted_iota(jnp.int32, (8, 128), 1)
    sub = lax.broadcasted_iota(jnp.int32, (8, 128), 0)

    def step(b, carry):
        beside.begin(b)
        beside.work(b)
        first = pl.multiple_of(b * 8, 8)
        rows = pair[pl.ds(first, 8), :]
        rows_a = rows[:, :128]
        rows_b = rows[:, 128:]
        turned = pltpu.roll(rows_a, mod(128 - first, 128), 1)
        cols = [jnp.broadcast_to(turned[:, j : j + 1], (8, 128)) for j in range(8)]
        e = {}
        for a in range(8):
            for j in range(a + 1):
                e[a, j] = jnp.broadcast_to(cols[j][a : a + 1, :], (8, 128))
        inv = []
        low = {}
        for j in range(8):
            d = e[j, j]
            r = lax.rsqrt(d)
            r = r * (1.5 - 0.5 * d * r * r)
            inv.append(r)
            for a in range(j + 1, 8):
                low[a, j] = e[a, j] * r
            for a in range(j + 1, 8):
                for c in range(j + 1, a + 1):
                    e[a, c] = e[a, c] - low[a, j] * low[c, j]
        ups_a = []
        ups_b = []
        out_a = jnp.zeros((8, 128), F32)
        out_b = jnp.zeros((8, 128), F32)
        for a in range(8):
            row_a = jnp.broadcast_to(rows_a[a : a + 1, :], (8, 128))
            row_b = jnp.broadcast_to(rows_b[a : a + 1, :], (8, 128))
            for j in range(a):
                row_a = row_a - low[a, j] * ups_a[j]
                row_b = row_b - low[a, j] * ups_b[j]
            row_a = row_a * inv[a]
            row_b = row_b * inv[a]
            ups_a.append(row_a)
            ups_b.append(row_b)
            out_a = jnp.where(sub == a, row_a, out_a)
            out_b = jnp.where(sub == a, row_b, out_b)
        done = jnp.concatenate([out_a, out_b], axis=1)
        pair[pl.ds(first, 8), :] = done
        mult = jnp.where(lane >= first + 8, out_a, 0.0)
        mh, mm, ml = thirds(mult)
        uh, um, ul = thirds(done)
        left = jnp.concatenate([mh, mh, mm, mh, ml, mm], axis=0).astype(BF16)
        right = jnp.concatenate([uh, um, uh, ul, uh, um], axis=0).astype(BF16)
        gone = lax.dot_general(
            left, right, (((0,), (0,)), ((), ())), preferred_element_type=F32
        )
        pair[...] = pair[...] - gone
        beside.end(b)
        return carry

    lax.fori_loop(0, 16, step, 0)


def factor_block(jb, work, pair, beside):
    at = jb * 128
    eye = (
        lax.broadcasted_iota(jnp.int32, (128, 128), 0)
        == lax.broadcasted_iota(jnp.int32, (128, 128), 1)
    ).astype(F32)
    pair[:, 0:128] = work[at : at + 128, at : at + 128]
    pair[:, 128:256] = eye
    factor_128(pair, beside)
    inverse = pair[:, 128:256]
    if jb:
        work[at : at + 128, SPAN : SPAN + at] = dot_full(
            inverse, work[at : at + 128, SPAN : SPAN + at], ((1,), (0,))
        )
    work[at : at + 128, SPAN + at : SPAN + at + 128] = inverse
    if jb < 3:
        rest = at + 128
        above = dot_full(inverse, work[at : at + 128, rest:SPAN], ((1,), (0,)))
        work[rest:SPAN, rest:SPAN] -= dot_full(above, above, ((0,), (0,)))
        work[rest:SPAN, SPAN : SPAN + rest] -= dot_full(
            above, work[at : at + 128, SPAN : SPAN + rest], ((0,), (0,))
        )


def kernel(
    child_map, child, root, out, bulk_in, row_out, col_out,
    marks, row_perms, col_places, chunk_buf, front, bulk_out, unit_in, front_out, front_in, cols, diag, rows, work,
    pair, rows_f, rows_h, rows_l, prod, inv_h, inv_l,
    keep_s, tab_s, s_marks, s_chunk, s_front, s_out, bulk_s, bulk_r, unit_s, unit_r, front_s, front_r,
    cols_s, cols_r, hand_s, dz_s, dz_r, dy_s, dy_r, r1_s, r1_r, rz_s, rz_r, ry_s, ry_r,
):
    p = lax.axis_index("wide")
    q = lax.axis_index("narrow")
    core = mod(p, 2)
    chip = p // 2
    ph = p // 8
    pl8 = mod(p, 8)
    zl = q // 4
    y = mod(q, 4)
    own = pl8 == q
    shift = shift_of(p, q)
    q_other = mod(q + 4, 8)

    def remote(src, dst, ssem, rsem, wide, narrow):
        return pltpu.make_async_remote_copy(
            src_ref=src, dst_ref=dst, send_sem=ssem, recv_sem=rsem,
            device_id=(wide, narrow), device_id_type=MESH,
        )

    def local(src, dst, sem):
        return pltpu.make_async_copy(src, dst, sem)

    def chunk_of(n):
        k = n // 16
        late = jnp.where(n < 4, n, 4 + mod(p + n, 12))
        dest = jnp.where(n < 16, late, mod(p + n, 16))
        return k, dest

    def chunk_copy(n):
        k, dest = chunk_of(n)
        at = pl.multiple_of((k * 16 + dest) * CHUNK, CHUNK)
        slot = mod(n, 4)
        to = pl.multiple_of(slot * CHUNK, CHUNK)
        return local(child.at[pl.ds(at, CHUNK)], chunk_buf.at[pl.ds(to, CHUNK)], s_chunk.at[slot])

    for n in range(4):
        chunk_copy(jnp.int32(n)).start()
    marks_load = local(child_map, marks, s_marks.at[0])
    marks_load.start()
    front_load = local(root, front, s_front.at[0])
    front_load.start()

    barrier = pltpu.get_barrier_semaphore()

    def greet(wide, narrow):
        pl.semaphore_signal(barrier, inc=1, device_id=(wide, narrow), device_id_type=MESH)

    def greet_wide(i, carry):
        greet(mod(p + i, 16), q)
        return carry

    lax.fori_loop(1, 16, greet_wide, 0)
    for i in range(1, 4):
        greet(p, zl * 4 + mod(y + i, 4))

    greet(p, q_other)
    pl.semaphore_wait(barrier, 19)

    def packed(n, la, lb):
        base = mod(n, 4) * CHUNK
        xa = chunk_buf[pl.ds(base + la, HALF, stride=COL_BLOCKS), :]
        xb = chunk_buf[pl.ds(base + lb, HALF, stride=COL_BLOCKS), :]
        return jnp.concatenate([xa, xb], axis=1)

    def next_chunk(n):
        @pl.when(n + 4 < 48)
        def _():
            chunk_copy(n + 4).start()

    def unit_copy(u):
        slot = u // 8
        owner = mod(u, 8) * 2 + (slot > 0).astype(jnp.int32)
        return owner, remote(
            bulk_out.at[mod(u, 4) * 3, u // 4], unit_in.at[slot * 8 + chip], unit_s.at[u], unit_r.at[slot * 8 + chip],
            owner, q,
        )

    def front_copy(m):
        u = m * 4 + p
        slot = u // 8
        owner = mod(u, 8) * 2 + (slot > 0).astype(jnp.int32)
        return owner, slot, remote(
            front_out.at[m], front_in.at[slot], front_s.at[m], front_r.at[slot], owner, q
        )

    def bulk_copy(k, dest):
        kk = 2 * k + core
        return remote(
            bulk_out.at[dest * 3 + k], bulk_in.at[kk * 8 + chip],
            bulk_s.at[dest * 3 + k], bulk_r.at[kk * 8 + chip], dest, q,
        )

    def keep_copy(k):
        return local(bulk_out.at[p * 3 + k], bulk_in.at[(2 * k + core) * 8 + chip], keep_s.at[k])

    def panel_row(kk, dest):
        return jnp.logical_and(kk == 0, dest < 4)

    def pack(n, carry):
        chunk_copy(n).wait()
        k, dest = chunk_of(n)

        def one(m, c):
            bulk_out[dest * 3 + k, m] = packed(n, 2 * m, 2 * m + 1)
            return c

        lax.fori_loop(0, 6, one, 0)

        @pl.when(panel_row(2 * k + core, dest))
        def _():
            def unit(m, c):
                u = m * 4 + dest
                owner, copy = unit_copy(u)

                @pl.when(owner != p)
                def _():
                    copy.start()

                @pl.when(owner == p)
                def _():
                    unit_in[(u // 8) * 8 + chip] = bulk_out[dest * 3, m]
                return c

            lax.fori_loop(0, 6, unit, 0)
        next_chunk(n)
        return carry

    def fire(n, carry):
        k, dest = chunk_of(n)

        @pl.when(jnp.logical_not(panel_row(2 * k + core, dest)))
        def _():
            @pl.when(dest != p)
            def _():
                bulk_copy(k, dest).start()

            @pl.when(dest == p)
            def _():
                keep_copy(k).start()
        return carry

    class Beside:
        def __init__(self, first, fired):
            self.first, self.fired = first, fired

        def begin(self, b):
            @pl.when(mod(b, 2) == 0)
            def _():
                chunk_copy(self.first + b // 2).wait()

        def work(self, b):
            n = self.first + b // 2
            k, dest = chunk_of(n)
            for i in range(3):
                m = mod(b, 2) * 3 + i
                bulk_out[dest * 3 + k, m] = packed(n, 2 * m, 2 * m + 1)

        def end(self, b):
            n = self.first + b // 2

            @pl.when(mod(b, 2) == 1)
            def _():
                next_chunk(n)

                @pl.when(n < self.fired)
                def _():
                    fire(n, 0)

    lax.fori_loop(0, 4, pack, 0)
    front_load.wait()

    @pl.when(p < 4)
    def _():
        def one(m, c):
            for h in range(2):
                front_out[m, :, h * 128 : h * 128 + 128] = front[
                    pl.ds(2 * m + h, BLOCK, stride=COL_BLOCKS), :
                ]
            owner, slot, copy = front_copy(m)

            @pl.when(owner != p)
            def _():
                copy.start()

            @pl.when(owner == p)
            def _():
                front_in[slot] = front_out[m]
            return c

        lax.fori_loop(0, 6, one, 0)

    def assemble(source, m, row):
        sides = []
        for h in range(2):
            total = jnp.zeros((BLOCK, BLOCK), F32)
            for pair_id in range(CHILDREN // 2):
                parts = []
                for g in (2 * pair_id, 2 * pair_id + 1):
                    place = jnp.broadcast_to(col_places[2 * m + h, g : g + 1, :], (HALF, 128))
                    taken = jnp.take_along_axis(
                        source(g), jnp.maximum(place, 0), axis=1, mode="promise_in_bounds"
                    )
                    parts.append(jnp.where(place >= 0, taken, 0.0))
                turned = jnp.concatenate(parts, axis=0).T
                order = jnp.broadcast_to(row_perms[row, pair_id : pair_id + 1, :], (BLOCK, BLOCK))
                total += jnp.take_along_axis(turned, order, axis=1, mode="promise_in_bounds")
            sides.append(total.T)
        return sides

    def cols_at(u):
        return cols.at[u // 4, pl.ds(pl.multiple_of(mod(u, 4) * 128, 128), 128), :]

    def cols_copy(u, dc):
        return remote(
            cols_at(u), cols_at(u), cols_s.at[(u // 8) * 8 + dc], cols_r.at[u],
            mod(chip + dc, 8) * 2 + core, q,
        )

    def hand_copy(u):
        return remote(cols_at(u), cols_at(u), hand_s.at[u], cols_r.at[u], chip * 2 + 1 - core, q)

    def own_unit(slot, carry):
        u = slot * 8 + chip
        block = mod(u, 4)

        def landed(g, c):
            @pl.when(jnp.logical_or(core == 1, g != chip))
            def _():
                remote(
                    bulk_out.at[0, 0], unit_in.at[slot * 8 + g], unit_s.at[0],
                    unit_r.at[slot * 8 + g], g * 2, q,
                ).wait_recv()
            return c

        lax.fori_loop(0, 8, landed, 0)

        @pl.when(block != p)
        def _():
            remote(
                front_out.at[0], front_in.at[slot], front_s.at[0], front_r.at[slot], block, q
            ).wait_recv()

        sides = assemble(lambda g: unit_in[slot * 8 + g], u // 4, 6)
        cols[u // 4, pl.ds(pl.multiple_of(block * 128, 128), 128), :] = (
            jnp.concatenate(sides, axis=1) + front_in[slot]
        )

        def send(dc, c):
            cols_copy(u, dc).start()
            return c

        lax.fori_loop(1, 8, send, 0)
        hand_copy(u).start()
        return carry

    def hand_on(u, carry):
        @pl.when(mod(u, 8) != chip)
        def _():
            cols_copy(u, 1).wait_recv()
            hand_copy(u).start()
        return carry

    def taken(u, carry):
        hand_copy(u).wait_recv()
        return carry

    first_slot = core
    last_slot = 1 + 2 * core

    marks_load.wait()
    ranks = lax.broadcasted_iota(jnp.int32, (HALF, 128), 0)
    spots = lax.broadcasted_iota(jnp.int32, (HALF, 128), 1)

    def places(block):
        at = pl.multiple_of((block // 2) * 128, 128)
        part = marks[:, pl.ds(at, 128)]
        mine = jnp.where(mod(block, 2) == 0, part, pltpu.roll(part, 64, 1)) - block * BLOCK
        tall = mine.T
        found = []
        for g in range(CHILDREN):
            hit = jnp.broadcast_to(tall[0:HALF, g : g + 1], (HALF, 128)) == spots
            found.append(jnp.max(jnp.where(hit, ranks, -1), axis=0, keepdims=True))
        return found

    def row_table(i, carry, block=None):
        found = places(i * 16 + p if block is None else block)
        for j in range(4):
            first, second = found[2 * j], found[2 * j + 1]
            row_perms[i, j : j + 1, :] = jnp.where(first >= 0, first, second + HALF)
        return carry


    def col_table(l, carry):
        found = places(l * 8 + q)
        for g in range(CHILDREN):
            col_places[l, g : g + 1, :] = jnp.where(
                found[g] >= 0, found[g] + mod(l, 2) * HALF, -1
            )
        return carry

    row_table(6, 0, mod(chip, 4))

    def unit_table(slot, carry):
        m = slot * 2 + chip // 4
        return col_table(2 * m + 1, col_table(2 * m, carry))

    lax.fori_loop(core, 1 + 2 * core, unit_table, 0)
    lax.fori_loop(first_slot, last_slot, own_unit, 0)
    lax.fori_loop(4, 10, pack, 0)

    @pl.when(core == 0)
    def _():
        lax.fori_loop(0, 4, hand_on, 0)

    @pl.when(core == 1)
    def _():
        lax.fori_loop(0, 4, taken, 0)

    dz = remote(diag.at[y], diag.at[y], dz_s.at[0], dz_r.at[0], p, q_other)

    @pl.when(zl == 0)
    def _():
        diag[y] = cols[0, :, 0:128]
        dz.start()

    @pl.when(zl == 1)
    def _():
        dz.wait_recv()

    def dy(i):
        return remote(diag.at[y], diag.at[y], dy_s.at[i], dy_r.at[y], p, zl * 4 + mod(y + i, 4))

    for i in range(1, 4):
        dy(i).start()

    lax.fori_loop(0, 8, fire, 0)

    @pl.when(core == 0)
    def _():
        lax.fori_loop(4, 8, hand_on, 0)
        lax.fori_loop(8, 24, taken, 0)

    @pl.when(core == 1)
    def _():
        lax.fori_loop(8, 24, hand_on, 0)
        lax.fori_loop(4, 8, taken, 0)

    def r1(c):
        return remote(
            cols.at[:, pl.ds(c * 128, 128), pl.ds(pl.multiple_of(ph * 128, 128), 128)],
            rows.at[c], r1_s.at[c], r1_r.at[0], p, zl * 4 + c,
        )

    rz = remote(rows.at[y], rows.at[y], rz_s.at[0], rz_r.at[0], p, q_other)

    def ry(i):
        return remote(rows.at[y], rows.at[y], ry_s.at[i], ry_r.at[y], p, zl * 4 + mod(y + i, 4))

    @pl.when(own)
    def _():
        for c in range(4):
            @pl.when(y != c)
            def _():
                r1(c).start()

            @pl.when(y == c)
            def _():
                rows[c] = cols[:, c * 128 : c * 128 + 128, pl.ds(pl.multiple_of(ph * 128, 128), 128)]


    lax.fori_loop(10, 16, pack, 0)
    lax.fori_loop(8, 10, fire, 0)
    lax.fori_loop(0, 6, row_table, 0)
    lax.fori_loop(0, 12, col_table, 0)

    for i in range(1, 4):
        src = mod(y + i, 4)
        remote(diag.at[src], diag.at[src], dy_s.at[i], dy_r.at[src], p, q_other).wait_recv()

    for c in range(4):
        work[:, c * 128 : c * 128 + 128] = diag[c]
    full = work[:, 0:SPAN]
    work[:, 0:SPAN] = 0.5 * (full + full.T)
    work[:, SPAN:] = jnp.zeros((SPAN, SPAN), F32)

    holder = zl == pl8 // 4

    @pl.when(holder)
    def _():
        @pl.when(jnp.logical_not(own))
        def _():
            remote(
                rows.at[y], rows.at[y], r1_s.at[0], r1_r.at[0], p, q_other
            ).wait_recv()
        rz.start()

    factor_block(0, work, pair, Beside(16, 18))

    @pl.when(jnp.logical_not(holder))
    def _():
        rz.wait_recv()

    for i in range(1, 4):
        ry(i).start()

    lax.fori_loop(10, 16, fire, 0)
    lax.fori_loop(18, 24, fire, 0)
    factor_block(1, work, pair, Beside(24, 48))
    factor_block(2, work, pair, Beside(32, 48))
    factor_block(3, work, pair, Beside(40, 48))

    def sent_unit(slot, carry):
        u = slot * 8 + chip

        def one(dc, c):
            cols_copy(u, dc).wait_send()
            return c

        lax.fori_loop(1, 8, one, 0)
        hand_copy(u).wait_send()
        return carry

    lax.fori_loop(first_slot, last_slot, sent_unit, 0)

    def handed(u, carry):
        @pl.when(mod(u, 8) != chip)
        def _():
            hand_copy(u).wait_send()
        return carry

    @pl.when(core == 0)
    def _():
        lax.fori_loop(0, 8, handed, 0)

    @pl.when(core == 1)
    def _():
        lax.fori_loop(8, 24, handed, 0)

    @pl.when(zl == 0)
    def _():
        dz.wait_send()

    for i in range(1, 4):
        dy(i).wait_send()

    @pl.when(own)
    def _():
        for c in range(4):
            @pl.when(y != c)
            def _():
                r1(c).wait_send()

    @pl.when(holder)
    def _():
        rz.wait_send()

    for i in range(1, 4):
        ry(i).wait_send()

    for i in range(1, 4):
        src = mod(y + i, 4)
        remote(rows.at[src], rows.at[src], ry_s.at[i], ry_r.at[src], p, q_other).wait_recv()

    inverse_h, inverse_l = halves(work[:, SPAN:])
    inv_h[...] = inverse_h
    inv_l[...] = inverse_l

    def solve(block):
        high, low = halves(block)
        total = jnp.dot(inv_h[...], high, preferred_element_type=F32)
        total += jnp.dot(inv_h[...], low, preferred_element_type=F32)
        total += jnp.dot(inv_l[...], high, preferred_element_type=F32)
        return total

    def solve_rows(kk, carry):
        block = jnp.concatenate([rows[c, kk] for c in range(4)], axis=0)
        turned = solve(block).T
        at = pl.multiple_of(kk * 128, 128)
        high, low = halves(turned)
        rows_h[pl.ds(at, 128), :] = high
        rows_l[pl.ds(at, 128), :] = low
        for c in range(4):
            rows_f[c, pl.ds(at, 128), :] = turned[:, c * 128 : c * 128 + 128]
        return carry

    lax.fori_loop(0, 6, solve_rows, 0)

    def solve_cols(m, carry):
        solved = solve(cols[m])
        high, low = halves(solved)
        cols[m] = solved
        total = jnp.dot(rows_h[...], high, preferred_element_type=F32)
        total += jnp.dot(rows_h[...], low, preferred_element_type=F32)
        total += jnp.dot(rows_l[...], high, preferred_element_type=F32)
        prod[...] = total

        def less(kk, c):
            at = pl.multiple_of(kk * 128, 128)
            for h in range(2):
                where = pl.ds(kk * (128 * COL_BLOCKS) + 2 * m + h, BLOCK, stride=COL_BLOCKS)
                front[where, :] = (
                    front[where, :] - prod[pl.ds(at, 128), h * 128 : h * 128 + 128]
                )
            return c

        lax.fori_loop(0, 6, less, 0)
        return carry

    lax.fori_loop(0, 6, solve_cols, 0)

    def store(kk):
        at = pl.multiple_of(kk * (128 * COL_BLOCKS), 128 * COL_BLOCKS)
        span = pl.ds(at, 128 * COL_BLOCKS)
        return local(front.at[span], out.at[span], s_out.at[kk])

    @pl.when(p < 4)
    def _():
        for l in range(COL_BLOCKS):
            @pl.when(l * 8 + q > p)
            def _():
                front[pl.ds(l, BLOCK, stride=COL_BLOCKS), :] = cols[
                    l // 2, pl.ds(pl.multiple_of(p * 128, 128), 128),
                    (l % 2) * 128 : (l % 2) * 128 + 128,
                ]

    @pl.when(q < 4)
    def _():
        for kk in range(ROW_BLOCKS):
            @pl.when(kk * 16 + p > q)
            def _():
                front[pl.ds(kk * (128 * COL_BLOCKS), BLOCK, stride=COL_BLOCKS), :] = rows_f[
                    q, kk * 128 : kk * 128 + 128, :
                ]

        @pl.when(p == q)
        def _():
            tile = rows_f[q, 0:128, :]
            lower = lax.broadcasted_iota(jnp.int32, (128, 128), 0) >= lax.broadcasted_iota(
                jnp.int32, (128, 128), 1
            )
            front[pl.ds(0, BLOCK, stride=COL_BLOCKS), :] = jnp.where(lower, tile, tile.T)

    lax.fori_loop(0, 6, lambda kk, c: (store(kk).start(), c)[1], 0)

    def landed(i, carry):
        kk, g = i // 8, mod(i, 8)
        mine = jnp.logical_and(g == chip, mod(kk, 2) == core)

        @pl.when(jnp.logical_not(jnp.logical_or(mine, panel_row(kk, p))))
        def _():
            remote(
                bulk_out.at[0], bulk_in.at[i], bulk_s.at[0], bulk_r.at[i], g * 2 + mod(kk, 2), q
            ).wait_recv()
        return carry

    lax.fori_loop(0, 48, landed, 0)

    def kept(k, carry):
        @pl.when(jnp.logical_not(panel_row(2 * k + core, p)))
        def _():
            keep_copy(k).wait()
        return carry

    lax.fori_loop(0, 3, kept, 0)
    tables = [
        local(row_perms, row_out, tab_s.at[0]), local(col_places, col_out, tab_s.at[1])
    ]
    for copy in tables:
        copy.start()
    for copy in tables:
        copy.wait()

    def sent_bulk(n, carry):
        k, dest = chunk_of(n)

        @pl.when(jnp.logical_not(jnp.logical_or(dest == p, panel_row(2 * k + core, dest))))
        def _():
            bulk_copy(k, dest).wait_send()
        return carry

    lax.fori_loop(0, 48, sent_bulk, 0)

    @pl.when(core == 0)
    def _():
        def one(u, c):
            owner, copy = unit_copy(u)

            @pl.when(owner != p)
            def _():
                copy.wait_send()
            return c

        lax.fori_loop(0, 24, one, 0)

    @pl.when(p < 4)
    def _():
        def one(m, c):
            owner, slot, copy = front_copy(m)

            @pl.when(owner != p)
            def _():
                copy.wait_send()
            return c

        lax.fori_loop(0, 6, one, 0)

    def stored(kk, carry):
        store(kk).wait()
        return carry

    lax.fori_loop(0, 6, stored, 0)


def add_children(row_perms, col_places, front, children, out, pick, wide_buf):
    kk = pl.program_id(0)
    p = lax.axis_index("wide")
    q = lax.axis_index("narrow")
    panel = jnp.logical_and(kk == 0, p < 4)

    @pl.when(panel)
    def _():
        out[...] = front[...]

    @pl.when(jnp.logical_not(panel))
    def _():
        level = lax.broadcasted_iota(jnp.int32, (128, 128), 1)
        for j in range(4):
            order = jnp.broadcast_to(row_perms[kk, j : j + 1, :], (128, 128)).T
            table = jnp.where(order == level, 1.0, 0.0).astype(BF16)
            pick[:, j * 128 : j * 128 + 128] = table
            pick[:, 512 + j * 128 : 640 + j * 128] = table

        def one(m, carry):
            for g in range(CHILDREN):
                for h in range(2):
                    place = jnp.broadcast_to(col_places[2 * m + h, g : g + 1, :], (HALF, 128))
                    taken = jnp.take_along_axis(
                        children[g, m], jnp.maximum(place, 0), axis=1, mode="promise_in_bounds"
                    )
                    high, low = halves(jnp.where(place >= 0, taken, 0.0))
                    wide_buf[g * 64 : g * 64 + 64, h * 128 : h * 128 + 128] = high
                    wide_buf[512 + g * 64 : 576 + g * 64, h * 128 : h * 128 + 128] = low
            total = jnp.dot(pick[...], wide_buf[...], preferred_element_type=F32)
            for h in range(2):
                where = pl.ds(2 * m + h, BLOCK, stride=COL_BLOCKS)
                side = total[:, h * 128 : h * 128 + 128]
                if h == 0:
                    side = jnp.where(jnp.logical_and(m == 0, q < 4), 0.0, side)
                out[where, :] = front[where, :] + side
            return carry

        lax.fori_loop(0, 6, one, 0)


def body(root_front, child_update, child_map):
    child = child_update.reshape(3 * 16 * CHUNK, HALF)
    root = root_front.reshape(ROW_BLOCKS * BLOCK * COL_BLOCKS, BLOCK)
    vmem = lambda *shape: pltpu.VMEM(shape, F32)
    sems = lambda n: pltpu.SemaphoreType.DMA((n,))
    front, children, row_perms, col_places = pl.pallas_call(
        kernel,
        out_shape=[
            jax.ShapeDtypeStruct(root.shape, F32),
            jax.ShapeDtypeStruct((48, 6, HALF, 128), F32),
            jax.ShapeDtypeStruct((8, 4, 128), jnp.int32),
            jax.ShapeDtypeStruct((COL_BLOCKS, CHILDREN, 128), jnp.int32),
        ],
        in_specs=[pl.BlockSpec(memory_space=pl.ANY)] * 3,
        out_specs=[pl.BlockSpec(memory_space=pl.ANY)] * 4,
        scratch_shapes=[
            pltpu.VMEM((CHILDREN, 6144), jnp.int32),
            pltpu.VMEM((8, 4, 128), jnp.int32),
            pltpu.VMEM((COL_BLOCKS, CHILDREN, 128), jnp.int32),
            vmem(4 * CHUNK, HALF),
            vmem(ROW_BLOCKS * BLOCK * COL_BLOCKS, BLOCK),
            vmem(48, 6, HALF, 128),
            vmem(24, HALF, 128),
            vmem(6, BLOCK, 256),
            vmem(3, BLOCK, 256),
            vmem(6, SPAN, 256),
            vmem(4, SPAN, 128),
            vmem(4, 6, BLOCK, BLOCK),
            vmem(SPAN, 2 * SPAN),
            vmem(BLOCK, 2 * BLOCK),
            vmem(4, 768, BLOCK),
            pltpu.VMEM((768, SPAN), BF16),
            pltpu.VMEM((768, SPAN), BF16),
            vmem(768, 256),
            pltpu.VMEM((SPAN, SPAN), BF16),
            pltpu.VMEM((SPAN, SPAN), BF16),
            sems(3), sems(2), sems(1), sems(4), sems(1), sems(6), sems(48), sems(48), sems(24), sems(24),
            sems(6), sems(3), sems(24), sems(24), sems(24), sems(1), sems(1), sems(4), sems(4),
            sems(4), sems(1), sems(1), sems(1), sems(4), sems(4),
        ],
        compiler_params=pltpu.CompilerParams(
            collective_id=0, has_side_effects=True, vmem_limit_bytes=60 * 2**20
        ),
    )(child_map, child, root)
    part = pl.BlockSpec((BLOCK * COL_BLOCKS, BLOCK), lambda i: (i, 0))
    out = pl.pallas_call(
        add_children,
        grid=(ROW_BLOCKS,),
        out_shape=jax.ShapeDtypeStruct(root.shape, F32),
        in_specs=[
            pl.BlockSpec((8, 4, 128), lambda i: (0, 0, 0)),
            pl.BlockSpec((COL_BLOCKS, CHILDREN, 128), lambda i: (0, 0, 0)),
            part,
            pl.BlockSpec((CHILDREN, 6, HALF, 128), lambda i: (i, 0, 0, 0)),
        ],
        out_specs=part,
        scratch_shapes=[pltpu.VMEM((BLOCK, 1024), BF16), pltpu.VMEM((1024, 256), BF16)],
        compiler_params=pltpu.CompilerParams(vmem_limit_bytes=60 * 2**20),
    )(row_perms, col_places, front, children)
    return out.reshape(root_front.shape)


def solution(mesh):
    return jax.shard_map(
        body,
        mesh=mesh,
        in_specs=(
            P(None, "wide", None, None, "narrow", None),
            P("wide", None, None, None, None, "narrow", None),
            P(),
        ),
        out_specs=P(None, "wide", None, None, "narrow", None),
        check_vma=False,
    )
```

```python
import functools

import jax
import jax.numpy as jnp
from jax import lax
from jax.experimental import pallas as pl
from jax.experimental.pallas import tpu as pltpu
from jax.sharding import PartitionSpec as P

BLOCK = 128
HALF = 64
ROW_BLOCKS = 6
COL_BLOCKS = 12
CHILDREN = 8
N_WIDE = 16
N_NARROW = 8
SPAN = 512
CHUNK = HALF * COL_BLOCKS
MESH = pl.DeviceIdType.MESH
F32 = jnp.float32
BF16 = jnp.bfloat16


def mod(value, n):
    return lax.rem(value, n)


def shift_of(p, q):
    return p // 8 + (mod(p, 8) > q).astype(jnp.int32)


def halves(value):
    high = value.astype(BF16)
    low = (value - high.astype(F32)).astype(BF16)
    return high, low


def dot_full(a, b, dims):
    return lax.dot_general(
        a, b, (dims, ((), ())), precision=lax.Precision.HIGHEST, preferred_element_type=F32
    )


def thirds(value):
    high = value.astype(BF16).astype(F32)
    rest = value - high
    mid = rest.astype(BF16).astype(F32)
    low = rest - mid
    return high, mid, low


def factor_128(pair, beside):
    lane = lax.broadcasted_iota(jnp.int32, (8, 128), 1)
    sub = lax.broadcasted_iota(jnp.int32, (8, 128), 0)

    def step(b, carry):
        if beside is not None:
            beside.begin(b)
            beside.work(b)
        first = pl.multiple_of(b * 8, 8)
        rows = pair[pl.ds(first, 8), :]
        rows_a = rows[:, :128]
        rows_b = rows[:, 128:]
        turned = pltpu.roll(rows_a, mod(128 - first, 128), 1)
        cols = [jnp.broadcast_to(turned[:, j : j + 1], (8, 128)) for j in range(8)]
        e = {}
        for a in range(8):
            for j in range(a + 1):
                e[a, j] = jnp.broadcast_to(cols[j][a : a + 1, :], (8, 128))
        inv = []
        low = {}
        for j in range(8):
            d = e[j, j]
            r = lax.rsqrt(d)
            r = r * (1.5 - 0.5 * d * r * r)
            inv.append(r)
            for a in range(j + 1, 8):
                low[a, j] = e[a, j] * r
            for a in range(j + 1, 8):
                for c in range(j + 1, a + 1):
                    e[a, c] = e[a, c] - low[a, j] * low[c, j]
        ups_a = []
        ups_b = []
        out_a = jnp.zeros((8, 128), F32)
        out_b = jnp.zeros((8, 128), F32)
        for a in range(8):
            row_a = jnp.broadcast_to(rows_a[a : a + 1, :], (8, 128))
            row_b = jnp.broadcast_to(rows_b[a : a + 1, :], (8, 128))
            for j in range(a):
                row_a = row_a - low[a, j] * ups_a[j]
                row_b = row_b - low[a, j] * ups_b[j]
            row_a = row_a * inv[a]
            row_b = row_b * inv[a]
            ups_a.append(row_a)
            ups_b.append(row_b)
            out_a = jnp.where(sub == a, row_a, out_a)
            out_b = jnp.where(sub == a, row_b, out_b)
        done = jnp.concatenate([out_a, out_b], axis=1)
        pair[pl.ds(first, 8), :] = done
        mult = jnp.where(lane >= first + 8, out_a, 0.0)
        mh, mm, ml = thirds(mult)
        uh, um, ul = thirds(done)
        left = jnp.concatenate([mh, mh, mm, mh, ml, mm], axis=0).astype(BF16)
        right = jnp.concatenate([uh, um, uh, ul, uh, um], axis=0).astype(BF16)
        gone = lax.dot_general(
            left, right, (((0,), (0,)), ((), ())), preferred_element_type=F32
        )
        pair[...] = pair[...] - gone
        if beside is not None:
            beside.end(b)
        return carry

    lax.fori_loop(0, 16, step, 0)


def factor_block(jb, work, pair, beside):
    at = jb * 128
    eye = (
        lax.broadcasted_iota(jnp.int32, (128, 128), 0)
        == lax.broadcasted_iota(jnp.int32, (128, 128), 1)
    ).astype(F32)
    pair[:, 0:128] = work[at : at + 128, at : at + 128]
    pair[:, 128:256] = eye
    factor_128(pair, beside)
    inverse = pair[:, 128:256]
    if jb:
        work[at : at + 128, SPAN : SPAN + at] = dot_full(
            inverse, work[at : at + 128, SPAN : SPAN + at], ((1,), (0,))
        )
    work[at : at + 128, SPAN + at : SPAN + at + 128] = inverse
    if jb < 3:
        rest = at + 128
        above = dot_full(inverse, work[at : at + 128, rest:SPAN], ((1,), (0,)))
        work[rest:SPAN, rest:SPAN] -= dot_full(above, above, ((0,), (0,)))
        work[rest:SPAN, SPAN : SPAN + rest] -= dot_full(
            above, work[at : at + 128, SPAN : SPAN + rest], ((0,), (0,))
        )


def kernel(
    child_map, child, root, out, bulk_in, row_out, col_out,
    marks, row_perms, col_places, chunk_buf, front, bulk_out, unit_in, front_out, front_in, cols, diag, rows, work,
    pair, rows_f, rows_h, rows_l, prod, inv_h, inv_l, relay,
    keep_s, tab_s, s_marks, s_chunk, s_front, s_out, relay_s, relay_r, bulk_s, bulk_r, unit_s, unit_r, front_s, front_r,
    cols_s, cols_r, hand_s, dz_s, dz_r, dy_s, dy_r, r1_s, r1_r, rz_s, rz_r, ry_s, ry_r,
):
    p = lax.axis_index("wide")
    q = lax.axis_index("narrow")
    core = mod(p, 2)
    chip = p // 2
    ph = p // 8
    pl8 = mod(p, 8)
    zl = q // 4
    y = mod(q, 4)
    own = pl8 == q
    shift = shift_of(p, q)
    q_other = mod(q + 4, 8)

    def remote(src, dst, ssem, rsem, wide, narrow):
        return pltpu.make_async_remote_copy(
            src_ref=src, dst_ref=dst, send_sem=ssem, recv_sem=rsem,
            device_id=(wide, narrow), device_id_type=MESH,
        )

    def local(src, dst, sem):
        return pltpu.make_async_copy(src, dst, sem)

    def chunk_of(n):
        first = jnp.where(
            ph == 0,
            jnp.where(n < 12, 8 + mod(p + n, 8), 4 + mod(n, 4)),
            jnp.where(n < 8, 4 + mod(p + n, 4), 8 + mod(p + n, 8)),
        )
        first = jnp.where(n < 4, n, first)
        late = n - 16
        k = jnp.where(n < 16, 0, 1 + mod(late // 8, 2))
        side = jnp.where(n < 32, 1 - ph, ph)
        dest = jnp.where(n < 16, first, side * 8 + mod(p + n, 8))
        return k, dest

    def chunk_copy(n):
        k, dest = chunk_of(n)
        at = pl.multiple_of((k * 16 + dest) * CHUNK, CHUNK)
        slot = mod(n, 4)
        to = pl.multiple_of(slot * CHUNK, CHUNK)
        return local(child.at[pl.ds(at, CHUNK)], chunk_buf.at[pl.ds(to, CHUNK)], s_chunk.at[slot])

    for n in range(4):
        chunk_copy(jnp.int32(n)).start()
    marks_load = local(child_map, marks, s_marks.at[0])
    marks_load.start()
    front_load = local(root, front, s_front.at[0])
    front_load.start()

    barrier = pltpu.get_barrier_semaphore()

    def greet(wide, narrow):
        pl.semaphore_signal(barrier, inc=1, device_id=(wide, narrow), device_id_type=MESH)

    def greet_wide(i, carry):
        greet(mod(p + i, 16), q)
        return carry

    lax.fori_loop(1, 16, greet_wide, 0)
    for i in range(1, 4):
        greet(p, zl * 4 + mod(y + i, 4))


    def greet_plane(i, carry):
        greet(i, q_other)
        return carry

    lax.fori_loop(0, 16, greet_plane, 0)
    pl.semaphore_wait(barrier, 34)

    def packed(n, la, lb):
        base = mod(n, 4) * CHUNK
        xa = chunk_buf[pl.ds(base + la, HALF, stride=COL_BLOCKS), :]
        xb = chunk_buf[pl.ds(base + lb, HALF, stride=COL_BLOCKS), :]
        return jnp.concatenate([xa, xb], axis=1)

    def next_chunk(n):
        @pl.when(n + 4 < 48)
        def _():
            chunk_copy(n + 4).start()

    def unit_copy(u):
        slot = u // 8
        owner = mod(u, 8) * 2 + (slot > 0).astype(jnp.int32)
        return owner, remote(
            bulk_out.at[mod(u, 4) * 3, u // 4], unit_in.at[slot * 8 + chip], unit_s.at[u], unit_r.at[slot * 8 + chip],
            owner, q,
        )

    def front_copy(m):
        u = m * 4 + p
        slot = u // 8
        owner = mod(u, 8) * 2 + (slot > 0).astype(jnp.int32)
        return owner, slot, remote(
            front_out.at[m], front_in.at[slot], front_s.at[m], front_r.at[slot], owner, q
        )

    zh = ph
    xs = mod(chip, 4)

    def bulk_copy(k, dest):
        kk = 2 * k + core
        return remote(
            bulk_out.at[dest * 3 + k], bulk_in.at[kk * 8 + chip],
            bulk_s.at[dest * 3 + k], bulk_r.at[kk * 8 + chip], dest, q,
        )

    def keep_copy(k):
        return local(bulk_out.at[p * 3 + k], bulk_in.at[(2 * k + core) * 8 + chip], keep_s.at[k])

    def first_copy(k, dest):
        xd = mod(dest // 2, 4)
        far = mod(xd - xs + 6, 4) == 0
        xi = jnp.where(far, mod(xd + 1, 4), xd)
        gap = mod(xs - xi + 4, 4)
        way = jnp.where(far, 3, jnp.where(gap == 3, 2, gap))
        zi = jnp.where(mod(core + xs + k, 2) == 0, zh, 1 - zh)
        slot = k * 8 + way * 2 + core
        return remote(
            bulk_out.at[dest * 3 + k], relay.at[slot], bulk_s.at[dest * 3 + k],
            relay_r.at[slot], (zi * 4 + xi) * 2 + mod(dest, 2), q_other,
        )

    def second_copy(k, way, cs):
        slot = k * 8 + way * 2 + cs
        side = jnp.where(jnp.logical_or(way == 1, way == 3), 1, jnp.where(way == 2, 3, 0))
        source_x = mod(xs + side, 4)
        dest_x = jnp.where(way == 3, mod(xs + 3, 4), xs)
        source_z = jnp.where(mod(cs + source_x + k, 2) == 0, zh, 1 - zh)
        dest = ((1 - source_z) * 4 + dest_x) * 2 + core
        place = (2 * k + cs) * 8 + source_z * 4 + source_x
        return dest, remote(
            relay.at[slot], bulk_in.at[place], relay_s.at[slot], bulk_r.at[place], dest, q_other
        )

    def relay_one(i, carry):
        k, way, cs = i // 8, mod(i, 8) // 2, mod(i, 2)
        dest, copy = second_copy(k, way, cs)

        @pl.when(jnp.logical_not(panel_row(2 * k + cs, dest)))
        def _():
            remote(
                bulk_out.at[0], relay.at[i], bulk_s.at[0], relay_r.at[i], p, q_other
            ).wait_recv()
            copy.start()
        return carry

    def panel_row(kk, dest):
        return jnp.logical_and(kk == 0, dest < 4)

    def pack(n, carry):
        chunk_copy(n).wait()
        k, dest = chunk_of(n)

        def one(m, c):
            bulk_out[dest * 3 + k, m] = packed(n, 2 * m, 2 * m + 1)
            return c

        lax.fori_loop(0, 6, one, 0)

        @pl.when(panel_row(2 * k + core, dest))
        def _():
            def unit(m, c):
                u = m * 4 + dest
                owner, copy = unit_copy(u)

                @pl.when(owner != p)
                def _():
                    copy.start()

                @pl.when(owner == p)
                def _():
                    unit_in[(u // 8) * 8 + chip] = bulk_out[dest * 3, m]
                return c

            lax.fori_loop(0, 6, unit, 0)
        next_chunk(n)
        return carry

    def fire(n, carry):
        k, dest = chunk_of(n)

        @pl.when(jnp.logical_not(panel_row(2 * k + core, dest)))
        def _():
            crossing = dest // 8 != ph

            @pl.when(crossing)
            def _():
                first_copy(k, dest).start()

            @pl.when(jnp.logical_not(jnp.logical_or(crossing, dest == p)))
            def _():
                bulk_copy(k, dest).start()

            @pl.when(dest == p)
            def _():
                keep_copy(k).start()
        return carry

    def pack_fire(n, carry):
        return fire(n, pack(n, carry))

    class Beside:
        def __init__(self, first, fired):
            self.first, self.fired = first, fired

        def begin(self, b):
            @pl.when(mod(b, 2) == 0)
            def _():
                chunk_copy(self.first + b // 2).wait()

        def work(self, b):
            n = self.first + b // 2
            k, dest = chunk_of(n)
            for i in range(3):
                m = mod(b, 2) * 3 + i
                bulk_out[dest * 3 + k, m] = packed(n, 2 * m, 2 * m + 1)

        def end(self, b):
            n = self.first + b // 2

            @pl.when(mod(b, 2) == 1)
            def _():
                next_chunk(n)

                @pl.when(n < self.fired)
                def _():
                    fire(n, 0)

    lax.fori_loop(0, 4, pack, 0)
    front_load.wait()

    @pl.when(p < 4)
    def _():
        def one(m, c):
            for h in range(2):
                front_out[m, :, h * 128 : h * 128 + 128] = front[
                    pl.ds(2 * m + h, BLOCK, stride=COL_BLOCKS), :
                ]
            owner, slot, copy = front_copy(m)

            @pl.when(owner != p)
            def _():
                copy.start()

            @pl.when(owner == p)
            def _():
                front_in[slot] = front_out[m]
            return c

        lax.fori_loop(0, 6, one, 0)

    def assemble(source, m, row):
        sides = []
        for h in range(2):
            total = jnp.zeros((BLOCK, BLOCK), F32)
            for pair_id in range(CHILDREN // 2):
                parts = []
                for g in (2 * pair_id, 2 * pair_id + 1):
                    place = jnp.broadcast_to(col_places[2 * m + h, g : g + 1, :], (HALF, 128))
                    taken = jnp.take_along_axis(
                        source(g), jnp.maximum(place, 0), axis=1, mode="promise_in_bounds"
                    )
                    parts.append(jnp.where(place >= 0, taken, 0.0))
                turned = jnp.concatenate(parts, axis=0).T
                order = jnp.broadcast_to(row_perms[row, pair_id : pair_id + 1, :], (BLOCK, BLOCK))
                total += jnp.take_along_axis(turned, order, axis=1, mode="promise_in_bounds")
            sides.append(total.T)
        return sides

    def cols_at(u):
        return cols.at[u // 4, pl.ds(pl.multiple_of(mod(u, 4) * 128, 128), 128), :]

    def cols_copy(u, dc):
        return remote(
            cols_at(u), cols_at(u), cols_s.at[(u // 8) * 8 + dc], cols_r.at[u],
            mod(chip + dc, 8) * 2 + core, q,
        )

    def hand_copy(u):
        return remote(cols_at(u), cols_at(u), hand_s.at[u], cols_r.at[u], chip * 2 + 1 - core, q)

    def own_unit(slot, carry):
        u = slot * 8 + chip
        block = mod(u, 4)

        def landed(g, c):
            @pl.when(jnp.logical_or(core == 1, g != chip))
            def _():
                remote(
                    bulk_out.at[0, 0], unit_in.at[slot * 8 + g], unit_s.at[0],
                    unit_r.at[slot * 8 + g], g * 2, q,
                ).wait_recv()
            return c

        lax.fori_loop(0, 8, landed, 0)

        @pl.when(block != p)
        def _():
            remote(
                front_out.at[0], front_in.at[slot], front_s.at[0], front_r.at[slot], block, q
            ).wait_recv()

        sides = assemble(lambda g: unit_in[slot * 8 + g], u // 4, 6)
        cols[u // 4, pl.ds(pl.multiple_of(block * 128, 128), 128), :] = (
            jnp.concatenate(sides, axis=1) + front_in[slot]
        )

        def send(dc, c):
            cols_copy(u, dc).start()
            return c

        lax.fori_loop(1, 8, send, 0)
        hand_copy(u).start()
        return carry

    def hand_on(u, carry):
        @pl.when(mod(u, 8) != chip)
        def _():
            cols_copy(u, 1).wait_recv()
            hand_copy(u).start()
        return carry

    def taken(u, carry):
        hand_copy(u).wait_recv()
        return carry

    first_slot = core
    last_slot = 1 + 2 * core

    marks_load.wait()
    ranks = lax.broadcasted_iota(jnp.int32, (HALF, 128), 0)
    spots = lax.broadcasted_iota(jnp.int32, (HALF, 128), 1)

    def places(block):
        at = pl.multiple_of((block // 2) * 128, 128)
        part = marks[:, pl.ds(at, 128)]
        mine = jnp.where(mod(block, 2) == 0, part, pltpu.roll(part, 64, 1)) - block * BLOCK
        tall = mine.T
        found = []
        for g in range(CHILDREN):
            hit = jnp.broadcast_to(tall[0:HALF, g : g + 1], (HALF, 128)) == spots
            found.append(jnp.max(jnp.where(hit, ranks, -1), axis=0, keepdims=True))
        return found

    def row_table(i, carry, block=None):
        found = places(i * 16 + p if block is None else block)
        for j in range(4):
            first, second = found[2 * j], found[2 * j + 1]
            row_perms[i, j : j + 1, :] = jnp.where(first >= 0, first, second + HALF)
        return carry


    def col_table(l, carry):
        found = places(l * 8 + q)
        for g in range(CHILDREN):
            col_places[l, g : g + 1, :] = jnp.where(
                found[g] >= 0, found[g] + mod(l, 2) * HALF, -1
            )
        return carry

    row_table(6, 0, mod(chip, 4))

    def unit_table(slot, carry):
        m = slot * 2 + chip // 4
        return col_table(2 * m + 1, col_table(2 * m, carry))

    lax.fori_loop(core, 1 + 2 * core, unit_table, 0)
    lax.fori_loop(first_slot, last_slot, own_unit, 0)
    lax.fori_loop(0, 4, fire, 0)
    lax.fori_loop(4, 10, pack_fire, 0)

    @pl.when(core == 0)
    def _():
        lax.fori_loop(0, 4, hand_on, 0)

    @pl.when(core == 1)
    def _():
        lax.fori_loop(0, 4, taken, 0)

    dz = remote(diag.at[y], diag.at[y], dz_s.at[0], dz_r.at[0], p, q_other)

    @pl.when(zl == 0)
    def _():
        diag[y] = cols[0, :, 0:128]
        dz.start()

    @pl.when(zl == 1)
    def _():
        dz.wait_recv()

    def dy(i):
        return remote(diag.at[y], diag.at[y], dy_s.at[i], dy_r.at[y], p, zl * 4 + mod(y + i, 4))

    for i in range(1, 4):
        dy(i).start()


    @pl.when(core == 0)
    def _():
        lax.fori_loop(4, 8, hand_on, 0)
        lax.fori_loop(8, 24, taken, 0)

    @pl.when(core == 1)
    def _():
        lax.fori_loop(8, 24, hand_on, 0)
        lax.fori_loop(4, 8, taken, 0)

    def r1(c):
        return remote(
            cols.at[:, pl.ds(c * 128, 128), pl.ds(pl.multiple_of(ph * 128, 128), 128)],
            rows.at[c], r1_s.at[c], r1_r.at[0], p, zl * 4 + c,
        )

    rz = remote(rows.at[y], rows.at[y], rz_s.at[0], rz_r.at[0], p, q_other)

    def ry(i):
        return remote(rows.at[y], rows.at[y], ry_s.at[i], ry_r.at[y], p, zl * 4 + mod(y + i, 4))

    @pl.when(own)
    def _():
        for c in range(4):
            @pl.when(y != c)
            def _():
                r1(c).start()

            @pl.when(y == c)
            def _():
                rows[c] = cols[:, c * 128 : c * 128 + 128, pl.ds(pl.multiple_of(ph * 128, 128), 128)]


    lax.fori_loop(10, 20, pack_fire, 0)

    holder = zl == pl8 // 4

    @pl.when(holder)
    def _():
        @pl.when(jnp.logical_not(own))
        def _():
            remote(
                rows.at[y], rows.at[y], r1_s.at[0], r1_r.at[0], p, q_other
            ).wait_recv()
        rz.start()

    lax.fori_loop(20, 32, pack_fire, 0)

    for i in range(1, 4):
        src = mod(y + i, 4)
        remote(diag.at[src], diag.at[src], dy_s.at[i], dy_r.at[src], p, q_other).wait_recv()

    for c in range(4):
        work[:, c * 128 : c * 128 + 128] = diag[c]
    full = work[:, 0:SPAN]
    work[:, 0:SPAN] = 0.5 * (full + full.T)
    work[:, SPAN:] = jnp.zeros((SPAN, SPAN), F32)

    lax.fori_loop(0, 8, relay_one, 0)
    factor_block(0, work, pair, Beside(32, 48))

    @pl.when(jnp.logical_not(holder))
    def _():
        rz.wait_recv()

    for i in range(1, 4):
        ry(i).start()

    lax.fori_loop(8, 16, relay_one, 0)
    factor_block(1, work, pair, Beside(40, 48))
    lax.fori_loop(16, 24, relay_one, 0)
    factor_block(2, work, pair, None)
    factor_block(3, work, pair, None)
    lax.fori_loop(0, 6, row_table, 0)
    lax.fori_loop(0, 12, col_table, 0)

    def sent_unit(slot, carry):
        u = slot * 8 + chip

        def one(dc, c):
            cols_copy(u, dc).wait_send()
            return c

        lax.fori_loop(1, 8, one, 0)
        hand_copy(u).wait_send()
        return carry

    lax.fori_loop(first_slot, last_slot, sent_unit, 0)

    def handed(u, carry):
        @pl.when(mod(u, 8) != chip)
        def _():
            hand_copy(u).wait_send()
        return carry

    @pl.when(core == 0)
    def _():
        lax.fori_loop(0, 8, handed, 0)

    @pl.when(core == 1)
    def _():
        lax.fori_loop(8, 24, handed, 0)

    @pl.when(zl == 0)
    def _():
        dz.wait_send()

    for i in range(1, 4):
        dy(i).wait_send()

    @pl.when(own)
    def _():
        for c in range(4):
            @pl.when(y != c)
            def _():
                r1(c).wait_send()

    @pl.when(holder)
    def _():
        rz.wait_send()

    for i in range(1, 4):
        ry(i).wait_send()

    for i in range(1, 4):
        src = mod(y + i, 4)
        remote(rows.at[src], rows.at[src], ry_s.at[i], ry_r.at[src], p, q_other).wait_recv()

    inverse_h, inverse_l = halves(work[:, SPAN:])
    inv_h[...] = inverse_h
    inv_l[...] = inverse_l

    def solve(block):
        high, low = halves(block)
        total = jnp.dot(inv_h[...], high, preferred_element_type=F32)
        total += jnp.dot(inv_h[...], low, preferred_element_type=F32)
        total += jnp.dot(inv_l[...], high, preferred_element_type=F32)
        return total

    def solve_rows(kk, carry):
        block = jnp.concatenate([rows[c, kk] for c in range(4)], axis=0)
        turned = solve(block).T
        at = pl.multiple_of(kk * 128, 128)
        high, low = halves(turned)
        rows_h[pl.ds(at, 128), :] = high
        rows_l[pl.ds(at, 128), :] = low
        for c in range(4):
            rows_f[c, pl.ds(at, 128), :] = turned[:, c * 128 : c * 128 + 128]
        return carry

    lax.fori_loop(0, 6, solve_rows, 0)

    def solve_cols(m, carry):
        solved = solve(cols[m])
        high, low = halves(solved)
        cols[m] = solved
        total = jnp.dot(rows_h[...], high, preferred_element_type=F32)
        total += jnp.dot(rows_h[...], low, preferred_element_type=F32)
        total += jnp.dot(rows_l[...], high, preferred_element_type=F32)
        prod[...] = total

        def less(kk, c):
            at = pl.multiple_of(kk * 128, 128)
            for h in range(2):
                where = pl.ds(kk * (128 * COL_BLOCKS) + 2 * m + h, BLOCK, stride=COL_BLOCKS)
                front[where, :] = (
                    front[where, :] - prod[pl.ds(at, 128), h * 128 : h * 128 + 128]
                )
            return c

        lax.fori_loop(0, 6, less, 0)
        return carry

    lax.fori_loop(0, 6, solve_cols, 0)

    def store(kk):
        at = pl.multiple_of(kk * (128 * COL_BLOCKS), 128 * COL_BLOCKS)
        span = pl.ds(at, 128 * COL_BLOCKS)
        return local(front.at[span], out.at[span], s_out.at[kk])

    @pl.when(p < 4)
    def _():
        for l in range(COL_BLOCKS):
            @pl.when(l * 8 + q > p)
            def _():
                front[pl.ds(l, BLOCK, stride=COL_BLOCKS), :] = cols[
                    l // 2, pl.ds(pl.multiple_of(p * 128, 128), 128),
                    (l % 2) * 128 : (l % 2) * 128 + 128,
                ]

    @pl.when(q < 4)
    def _():
        for kk in range(ROW_BLOCKS):
            @pl.when(kk * 16 + p > q)
            def _():
                front[pl.ds(kk * (128 * COL_BLOCKS), BLOCK, stride=COL_BLOCKS), :] = rows_f[
                    q, kk * 128 : kk * 128 + 128, :
                ]

        @pl.when(p == q)
        def _():
            tile = rows_f[q, 0:128, :]
            lower = lax.broadcasted_iota(jnp.int32, (128, 128), 0) >= lax.broadcasted_iota(
                jnp.int32, (128, 128), 1
            )
            front[pl.ds(0, BLOCK, stride=COL_BLOCKS), :] = jnp.where(lower, tile, tile.T)

    lax.fori_loop(0, 6, lambda kk, c: (store(kk).start(), c)[1], 0)

    def landed(i, carry):
        kk, g = i // 8, mod(i, 8)
        mine = jnp.logical_and(g == chip, mod(kk, 2) == core)

        @pl.when(jnp.logical_not(jnp.logical_or(mine, panel_row(kk, p))))
        def _():
            remote(
                bulk_out.at[0], bulk_in.at[i], bulk_s.at[0], bulk_r.at[i], g * 2 + mod(kk, 2), q
            ).wait_recv()
        return carry

    lax.fori_loop(0, 48, landed, 0)

    def kept(k, carry):
        @pl.when(jnp.logical_not(panel_row(2 * k + core, p)))
        def _():
            keep_copy(k).wait()
        return carry

    lax.fori_loop(0, 3, kept, 0)
    tables = [
        local(row_perms, row_out, tab_s.at[0]), local(col_places, col_out, tab_s.at[1])
    ]
    for copy in tables:
        copy.start()
    for copy in tables:
        copy.wait()

    def sent_bulk(n, carry):
        k, dest = chunk_of(n)

        @pl.when(jnp.logical_not(jnp.logical_or(dest == p, panel_row(2 * k + core, dest))))
        def _():
            bulk_copy(k, dest).wait_send()
        return carry

    lax.fori_loop(0, 48, sent_bulk, 0)

    @pl.when(core == 0)
    def _():
        def one(u, c):
            owner, copy = unit_copy(u)

            @pl.when(owner != p)
            def _():
                copy.wait_send()
            return c

        lax.fori_loop(0, 24, one, 0)

    @pl.when(p < 4)
    def _():
        def one(m, c):
            owner, slot, copy = front_copy(m)

            @pl.when(owner != p)
            def _():
                copy.wait_send()
            return c

        lax.fori_loop(0, 6, one, 0)

    def relayed(i, carry):
        k, way, cs = i // 8, mod(i, 8) // 2, mod(i, 2)
        dest, copy = second_copy(k, way, cs)

        @pl.when(jnp.logical_not(panel_row(2 * k + cs, dest)))
        def _():
            copy.wait_send()
        return carry

    lax.fori_loop(0, 24, relayed, 0)

    def stored(kk, carry):
        store(kk).wait()
        return carry

    lax.fori_loop(0, 6, stored, 0)


def add_children(row_perms, col_places, front, children, out, pick, wide_buf):
    kk = pl.program_id(0)
    p = lax.axis_index("wide")
    q = lax.axis_index("narrow")
    panel = jnp.logical_and(kk == 0, p < 4)

    @pl.when(panel)
    def _():
        out[...] = front[...]

    @pl.when(jnp.logical_not(panel))
    def _():
        level = lax.broadcasted_iota(jnp.int32, (128, 128), 1)
        for j in range(4):
            order = jnp.broadcast_to(row_perms[kk, j : j + 1, :], (128, 128)).T
            table = jnp.where(order == level, 1.0, 0.0).astype(BF16)
            pick[:, j * 128 : j * 128 + 128] = table
            pick[:, 512 + j * 128 : 640 + j * 128] = table

        def one(m, carry):
            for g in range(CHILDREN):
                for h in range(2):
                    place = jnp.broadcast_to(col_places[2 * m + h, g : g + 1, :], (HALF, 128))
                    taken = jnp.take_along_axis(
                        children[g, m], jnp.maximum(place, 0), axis=1, mode="promise_in_bounds"
                    )
                    high, low = halves(jnp.where(place >= 0, taken, 0.0))
                    wide_buf[g * 64 : g * 64 + 64, h * 128 : h * 128 + 128] = high
                    wide_buf[512 + g * 64 : 576 + g * 64, h * 128 : h * 128 + 128] = low
            total = jnp.dot(pick[...], wide_buf[...], preferred_element_type=F32)
            for h in range(2):
                where = pl.ds(2 * m + h, BLOCK, stride=COL_BLOCKS)
                side = total[:, h * 128 : h * 128 + 128]
                if h == 0:
                    side = jnp.where(jnp.logical_and(m == 0, q < 4), 0.0, side)
                out[where, :] = front[where, :] + side
            return carry

        lax.fori_loop(0, 6, one, 0)


def body(root_front, child_update, child_map):
    child = child_update.reshape(3 * 16 * CHUNK, HALF)
    root = root_front.reshape(ROW_BLOCKS * BLOCK * COL_BLOCKS, BLOCK)
    vmem = lambda *shape: pltpu.VMEM(shape, F32)
    sems = lambda n: pltpu.SemaphoreType.DMA((n,))
    front, children, row_perms, col_places = pl.pallas_call(
        kernel,
        out_shape=[
            jax.ShapeDtypeStruct(root.shape, F32),
            jax.ShapeDtypeStruct((48, 6, HALF, 128), F32),
            jax.ShapeDtypeStruct((8, 4, 128), jnp.int32),
            jax.ShapeDtypeStruct((COL_BLOCKS, CHILDREN, 128), jnp.int32),
        ],
        in_specs=[pl.BlockSpec(memory_space=pl.ANY)] * 3,
        out_specs=[pl.BlockSpec(memory_space=pl.ANY)] * 4,
        scratch_shapes=[
            pltpu.VMEM((CHILDREN, 6144), jnp.int32),
            pltpu.VMEM((8, 4, 128), jnp.int32),
            pltpu.VMEM((COL_BLOCKS, CHILDREN, 128), jnp.int32),
            vmem(4 * CHUNK, HALF),
            vmem(ROW_BLOCKS * BLOCK * COL_BLOCKS, BLOCK),
            vmem(48, 6, HALF, 128),
            vmem(24, HALF, 128),
            vmem(6, BLOCK, 256),
            vmem(3, BLOCK, 256),
            vmem(6, SPAN, 256),
            vmem(4, SPAN, 128),
            vmem(4, 6, BLOCK, BLOCK),
            vmem(SPAN, 2 * SPAN),
            vmem(BLOCK, 2 * BLOCK),
            vmem(4, 768, BLOCK),
            pltpu.VMEM((768, SPAN), BF16),
            pltpu.VMEM((768, SPAN), BF16),
            vmem(768, 256),
            pltpu.VMEM((SPAN, SPAN), BF16),
            pltpu.VMEM((SPAN, SPAN), BF16),
            vmem(24, 6, HALF, 128),
            sems(3), sems(2), sems(1), sems(4), sems(1), sems(6), sems(24), sems(24), sems(48), sems(48), sems(24), sems(24),
            sems(6), sems(3), sems(24), sems(24), sems(24), sems(1), sems(1), sems(4), sems(4),
            sems(4), sems(1), sems(1), sems(1), sems(4), sems(4),
        ],
        compiler_params=pltpu.CompilerParams(
            collective_id=0, has_side_effects=True, vmem_limit_bytes=60 * 2**20
        ),
    )(child_map, child, root)
    part = pl.BlockSpec((BLOCK * COL_BLOCKS, BLOCK), lambda i: (i, 0))
    out = pl.pallas_call(
        add_children,
        grid=(ROW_BLOCKS,),
        out_shape=jax.ShapeDtypeStruct(root.shape, F32),
        in_specs=[
            pl.BlockSpec((8, 4, 128), lambda i: (0, 0, 0)),
            pl.BlockSpec((COL_BLOCKS, CHILDREN, 128), lambda i: (0, 0, 0)),
            part,
            pl.BlockSpec((CHILDREN, 6, HALF, 128), lambda i: (i, 0, 0, 0)),
        ],
        out_specs=part,
        scratch_shapes=[pltpu.VMEM((BLOCK, 1024), BF16), pltpu.VMEM((1024, 256), BF16)],
        compiler_params=pltpu.CompilerParams(vmem_limit_bytes=60 * 2**20),
    )(row_perms, col_places, front, children)
    return out.reshape(root_front.shape)


def solution(mesh):
    return jax.shard_map(
        body,
        mesh=mesh,
        in_specs=(
            P(None, "wide", None, None, "narrow", None),
            P("wide", None, None, None, None, "narrow", None),
            P(),
        ),
        out_specs=P(None, "wide", None, None, "narrow", None),
        check_vma=False,
    )
```

```python
import functools

import jax
import jax.numpy as jnp
from jax import lax
from jax.experimental import pallas as pl
from jax.experimental.pallas import tpu as pltpu
from jax.sharding import PartitionSpec as P

BLOCK = 128
HALF = 64
ROW_BLOCKS = 6
COL_BLOCKS = 12
CHILDREN = 8
N_WIDE = 16
N_NARROW = 8
SPAN = 512
CHUNK = HALF * COL_BLOCKS
MESH = pl.DeviceIdType.MESH
F32 = jnp.float32
BF16 = jnp.bfloat16


def mod(value, n):
    return lax.rem(value, n)


def shift_of(p, q):
    return p // 8 + (mod(p, 8) > q).astype(jnp.int32)


def halves(value):
    high = value.astype(BF16)
    low = (value - high.astype(F32)).astype(BF16)
    return high, low


def dot_full(a, b, dims):
    return lax.dot_general(
        a, b, (dims, ((), ())), precision=lax.Precision.HIGHEST, preferred_element_type=F32
    )


def thirds(value):
    high = value.astype(BF16).astype(F32)
    rest = value - high
    mid = rest.astype(BF16).astype(F32)
    low = rest - mid
    return high, mid, low


def factor_128(pair, beside):
    lane = lax.broadcasted_iota(jnp.int32, (8, 128), 1)
    sub = lax.broadcasted_iota(jnp.int32, (8, 128), 0)

    def step(b, carry):
        if beside is not None:
            beside.begin(b)
            beside.work(b)
        first = pl.multiple_of(b * 8, 8)
        rows = pair[pl.ds(first, 8), :]
        rows_a = rows[:, :128]
        rows_b = rows[:, 128:]
        turned = pltpu.roll(rows_a, mod(128 - first, 128), 1)
        cols = [jnp.broadcast_to(turned[:, j : j + 1], (8, 128)) for j in range(8)]
        e = {}
        for a in range(8):
            for j in range(a + 1):
                e[a, j] = jnp.broadcast_to(cols[j][a : a + 1, :], (8, 128))
        inv = []
        low = {}
        for j in range(8):
            d = e[j, j]
            r = lax.rsqrt(d)
            r = r * (1.5 - 0.5 * d * r * r)
            inv.append(r)
            for a in range(j + 1, 8):
                low[a, j] = e[a, j] * r
            for a in range(j + 1, 8):
                for c in range(j + 1, a + 1):
                    e[a, c] = e[a, c] - low[a, j] * low[c, j]
        ups_a = []
        ups_b = []
        out_a = jnp.zeros((8, 128), F32)
        out_b = jnp.zeros((8, 128), F32)
        for a in range(8):
            row_a = jnp.broadcast_to(rows_a[a : a + 1, :], (8, 128))
            row_b = jnp.broadcast_to(rows_b[a : a + 1, :], (8, 128))
            for j in range(a):
                row_a = row_a - low[a, j] * ups_a[j]
                row_b = row_b - low[a, j] * ups_b[j]
            row_a = row_a * inv[a]
            row_b = row_b * inv[a]
            ups_a.append(row_a)
            ups_b.append(row_b)
            out_a = jnp.where(sub == a, row_a, out_a)
            out_b = jnp.where(sub == a, row_b, out_b)
        done = jnp.concatenate([out_a, out_b], axis=1)
        pair[pl.ds(first, 8), :] = done
        mult = jnp.where(lane >= first + 8, out_a, 0.0)
        mh, mm, ml = thirds(mult)
        uh, um, ul = thirds(done)
        left = jnp.concatenate([mh, mh, mm, mh, ml, mm], axis=0).astype(BF16)
        right = jnp.concatenate([uh, um, uh, ul, uh, um], axis=0).astype(BF16)
        gone = lax.dot_general(
            left, right, (((0,), (0,)), ((), ())), preferred_element_type=F32
        )
        pair[...] = pair[...] - gone
        if beside is not None:
            beside.end(b)
        return carry

    lax.fori_loop(0, 16, step, 0)


def factor_block(jb, work, pair, beside):
    at = jb * 128
    eye = (
        lax.broadcasted_iota(jnp.int32, (128, 128), 0)
        == lax.broadcasted_iota(jnp.int32, (128, 128), 1)
    ).astype(F32)
    pair[:, 0:128] = work[at : at + 128, at : at + 128]
    pair[:, 128:256] = eye
    factor_128(pair, beside)
    inverse = pair[:, 128:256]
    if jb:
        work[at : at + 128, SPAN : SPAN + at] = dot_full(
            inverse, work[at : at + 128, SPAN : SPAN + at], ((1,), (0,))
        )
    work[at : at + 128, SPAN + at : SPAN + at + 128] = inverse
    if jb < 3:
        rest = at + 128
        above = dot_full(inverse, work[at : at + 128, rest:SPAN], ((1,), (0,)))
        work[rest:SPAN, rest:SPAN] -= dot_full(above, above, ((0,), (0,)))
        work[rest:SPAN, SPAN : SPAN + rest] -= dot_full(
            above, work[at : at + 128, SPAN : SPAN + rest], ((0,), (0,))
        )


def kernel(
    child_map, child, root, out, bulk_in, row_out, col_out,
    marks, row_perms, col_places, chunk_buf, front, bulk_out, unit_in, front_out, front_in, cols, diag, rows, work,
    pair, rows_f, rows_h, rows_l, prod, inv_h, inv_l, relay, kids, pick, wide_buf,
    kids_s, keep_s, tab_s, s_marks, s_chunk, s_front, s_out, relay_s, relay_r, bulk_s, bulk_r, unit_s, unit_r, front_s, front_r,
    cols_s, cols_r, hand_s, dz_s, dz_r, dy_s, dy_r, r1_s, r1_r, rz_s, rz_r, ry_s, ry_r,
):
    p = lax.axis_index("wide")
    q = lax.axis_index("narrow")
    core = mod(p, 2)
    chip = p // 2
    ph = p // 8
    pl8 = mod(p, 8)
    zl = q // 4
    y = mod(q, 4)
    own = pl8 == q
    shift = shift_of(p, q)
    q_other = mod(q + 4, 8)

    def remote(src, dst, ssem, rsem, wide, narrow):
        return pltpu.make_async_remote_copy(
            src_ref=src, dst_ref=dst, send_sem=ssem, recv_sem=rsem,
            device_id=(wide, narrow), device_id_type=MESH,
        )

    def local(src, dst, sem):
        return pltpu.make_async_copy(src, dst, sem)

    def chunk_of(n):
        first = jnp.where(
            ph == 0,
            jnp.where(n < 12, 8 + mod(p + n, 8), 4 + mod(n, 4)),
            jnp.where(n < 8, 4 + mod(p + n, 4), 8 + mod(p + n, 8)),
        )
        first = jnp.where(n < 4, n, first)
        late = n - 16
        k = jnp.where(n < 16, 0, 1 + mod(late // 8, 2))
        side = jnp.where(n < 32, 1 - ph, ph)
        dest = jnp.where(n < 16, first, side * 8 + mod(p + n, 8))
        return k, dest

    def chunk_copy(n):
        k, dest = chunk_of(n)
        at = pl.multiple_of((k * 16 + dest) * CHUNK, CHUNK)
        slot = mod(n, 4)
        to = pl.multiple_of(slot * CHUNK, CHUNK)
        return local(child.at[pl.ds(at, CHUNK)], chunk_buf.at[pl.ds(to, CHUNK)], s_chunk.at[slot])

    for n in range(4):
        chunk_copy(jnp.int32(n)).start()
    marks_load = local(child_map, marks, s_marks.at[0])
    marks_load.start()
    front_load = local(root, front, s_front.at[0])
    front_load.start()

    barrier = pltpu.get_barrier_semaphore()

    def greet(wide, narrow):
        pl.semaphore_signal(barrier, inc=1, device_id=(wide, narrow), device_id_type=MESH)

    def greet_wide(i, carry):
        greet(mod(p + i, 16), q)
        return carry

    lax.fori_loop(1, 16, greet_wide, 0)
    for i in range(1, 4):
        greet(p, zl * 4 + mod(y + i, 4))


    def greet_plane(i, carry):
        greet(i, q_other)
        return carry

    lax.fori_loop(0, 16, greet_plane, 0)
    pl.semaphore_wait(barrier, 34)

    def packed(n, la, lb):
        base = mod(n, 4) * CHUNK
        xa = chunk_buf[pl.ds(base + la, HALF, stride=COL_BLOCKS), :]
        xb = chunk_buf[pl.ds(base + lb, HALF, stride=COL_BLOCKS), :]
        return jnp.concatenate([xa, xb], axis=1)

    def next_chunk(n):
        @pl.when(n + 4 < 48)
        def _():
            chunk_copy(n + 4).start()

    def unit_copy(u):
        slot = u // 8
        owner = mod(u, 8) * 2 + (slot > 0).astype(jnp.int32)
        return owner, remote(
            bulk_out.at[mod(u, 4) * 3, u // 4], unit_in.at[slot * 8 + chip], unit_s.at[u], unit_r.at[slot * 8 + chip],
            owner, q,
        )

    def front_copy(m):
        u = m * 4 + p
        slot = u // 8
        owner = mod(u, 8) * 2 + (slot > 0).astype(jnp.int32)
        return owner, slot, remote(
            front_out.at[m], front_in.at[slot], front_s.at[m], front_r.at[slot], owner, q
        )

    zh = ph
    xs = mod(chip, 4)

    def bulk_copy(k, dest):
        kk = 2 * k + core
        return remote(
            bulk_out.at[dest * 3 + k], bulk_in.at[kk * 8 + chip],
            bulk_s.at[dest * 3 + k], bulk_r.at[kk * 8 + chip], dest, q,
        )

    def keep_copy(k):
        return local(bulk_out.at[p * 3 + k], bulk_in.at[(2 * k + core) * 8 + chip], keep_s.at[k])

    def first_copy(k, dest):
        xd = mod(dest // 2, 4)
        far = mod(xd - xs + 6, 4) == 0
        xi = jnp.where(far, mod(xd + 1, 4), xd)
        gap = mod(xs - xi + 4, 4)
        way = jnp.where(far, 3, jnp.where(gap == 3, 2, gap))
        zi = jnp.where(mod(core + xs + k, 2) == 0, zh, 1 - zh)
        slot = k * 8 + way * 2 + core
        return remote(
            bulk_out.at[dest * 3 + k], relay.at[slot], bulk_s.at[dest * 3 + k],
            relay_r.at[slot], (zi * 4 + xi) * 2 + mod(dest, 2), q_other,
        )

    def second_copy(k, way, cs):
        slot = k * 8 + way * 2 + cs
        side = jnp.where(jnp.logical_or(way == 1, way == 3), 1, jnp.where(way == 2, 3, 0))
        source_x = mod(xs + side, 4)
        dest_x = jnp.where(way == 3, mod(xs + 3, 4), xs)
        source_z = jnp.where(mod(cs + source_x + k, 2) == 0, zh, 1 - zh)
        dest = ((1 - source_z) * 4 + dest_x) * 2 + core
        place = (2 * k + cs) * 8 + source_z * 4 + source_x
        return dest, remote(
            relay.at[slot], bulk_in.at[place], relay_s.at[slot], bulk_r.at[place], dest, q_other
        )

    def relay_one(i, carry):
        k, way, cs = i // 8, mod(i, 8) // 2, mod(i, 2)
        dest, copy = second_copy(k, way, cs)

        @pl.when(jnp.logical_not(panel_row(2 * k + cs, dest)))
        def _():
            remote(
                bulk_out.at[0], relay.at[i], bulk_s.at[0], relay_r.at[i], p, q_other
            ).wait_recv()
            copy.start()
        return carry

    def panel_row(kk, dest):
        return jnp.logical_and(kk == 0, dest < 4)

    def pack(n, carry):
        chunk_copy(n).wait()
        k, dest = chunk_of(n)

        def one(m, c):
            bulk_out[dest * 3 + k, m] = packed(n, 2 * m, 2 * m + 1)
            return c

        lax.fori_loop(0, 6, one, 0)

        @pl.when(panel_row(2 * k + core, dest))
        def _():
            def unit(m, c):
                u = m * 4 + dest
                owner, copy = unit_copy(u)

                @pl.when(owner != p)
                def _():
                    copy.start()

                @pl.when(owner == p)
                def _():
                    unit_in[(u // 8) * 8 + chip] = bulk_out[dest * 3, m]
                return c

            lax.fori_loop(0, 6, unit, 0)
        next_chunk(n)
        return carry

    def fire(n, carry):
        k, dest = chunk_of(n)

        @pl.when(jnp.logical_not(panel_row(2 * k + core, dest)))
        def _():
            crossing = dest // 8 != ph

            @pl.when(crossing)
            def _():
                first_copy(k, dest).start()

            @pl.when(jnp.logical_not(jnp.logical_or(crossing, dest == p)))
            def _():
                bulk_copy(k, dest).start()

            @pl.when(dest == p)
            def _():
                keep_copy(k).start()
        return carry

    def pack_fire(n, carry):
        return fire(n, pack(n, carry))

    class Beside:
        def __init__(self, first, fired):
            self.first, self.fired = first, fired

        def begin(self, b):
            @pl.when(mod(b, 2) == 0)
            def _():
                chunk_copy(self.first + b // 2).wait()

        def work(self, b):
            n = self.first + b // 2
            k, dest = chunk_of(n)
            for i in range(3):
                m = mod(b, 2) * 3 + i
                bulk_out[dest * 3 + k, m] = packed(n, 2 * m, 2 * m + 1)

        def end(self, b):
            n = self.first + b // 2

            @pl.when(mod(b, 2) == 1)
            def _():
                next_chunk(n)

                @pl.when(n < self.fired)
                def _():
                    fire(n, 0)

    lax.fori_loop(0, 4, pack, 0)
    front_load.wait()

    @pl.when(p < 4)
    def _():
        def one(m, c):
            for h in range(2):
                front_out[m, :, h * 128 : h * 128 + 128] = front[
                    pl.ds(2 * m + h, BLOCK, stride=COL_BLOCKS), :
                ]
            owner, slot, copy = front_copy(m)

            @pl.when(owner != p)
            def _():
                copy.start()

            @pl.when(owner == p)
            def _():
                front_in[slot] = front_out[m]
            return c

        lax.fori_loop(0, 6, one, 0)

    def assemble(source, m, row):
        sides = []
        for h in range(2):
            total = jnp.zeros((BLOCK, BLOCK), F32)
            for pair_id in range(CHILDREN // 2):
                parts = []
                for g in (2 * pair_id, 2 * pair_id + 1):
                    place = jnp.broadcast_to(col_places[2 * m + h, g : g + 1, :], (HALF, 128))
                    taken = jnp.take_along_axis(
                        source(g), jnp.maximum(place, 0), axis=1, mode="promise_in_bounds"
                    )
                    parts.append(jnp.where(place >= 0, taken, 0.0))
                turned = jnp.concatenate(parts, axis=0).T
                order = jnp.broadcast_to(row_perms[row, pair_id : pair_id + 1, :], (BLOCK, BLOCK))
                total += jnp.take_along_axis(turned, order, axis=1, mode="promise_in_bounds")
            sides.append(total.T)
        return sides

    def cols_at(u):
        return cols.at[u // 4, pl.ds(pl.multiple_of(mod(u, 4) * 128, 128), 128), :]

    def cross_copy(u):
        return remote(
            cols_at(u), cols_at(u), cols_s.at[(u // 8) * 8], cols_r.at[u],
            mod(chip + 4, 8) * 2 + core, q,
        )

    def along_copy(u, dx):
        far = jnp.where(mod(u, 8) == chip, 0, 3)
        return remote(
            cols_at(u), cols_at(u), cols_s.at[(u // 8) * 8 + far + dx], cols_r.at[u],
            (ph * 4 + mod(chip + dx, 4)) * 2 + core, q,
        )

    def along(u):
        def send(dx, c):
            along_copy(u, dx).start()
            return c

        lax.fori_loop(1, 4, send, 0)

    def hand_copy(u):
        return remote(cols_at(u), cols_at(u), hand_s.at[u], cols_r.at[u], chip * 2 + 1 - core, q)

    def own_unit(slot, carry):
        u = slot * 8 + chip
        block = mod(u, 4)

        def landed(g, c):
            @pl.when(jnp.logical_or(core == 1, g != chip))
            def _():
                remote(
                    bulk_out.at[0, 0], unit_in.at[slot * 8 + g], unit_s.at[0],
                    unit_r.at[slot * 8 + g], g * 2, q,
                ).wait_recv()
            return c

        lax.fori_loop(0, 8, landed, 0)

        @pl.when(block != p)
        def _():
            remote(
                front_out.at[0], front_in.at[slot], front_s.at[0], front_r.at[slot], block, q
            ).wait_recv()

        sides = assemble(lambda g: unit_in[slot * 8 + g], u // 4, 6)
        cols[u // 4, pl.ds(pl.multiple_of(block * 128, 128), 128), :] = (
            jnp.concatenate(sides, axis=1) + front_in[slot]
        )

        cross_copy(u).start()
        along(u)
        hand_copy(u).start()
        return carry

    def spread_on(slot, carry):
        u = slot * 8 + mod(chip + 4, 8)
        cross_copy(u).wait_recv()
        along(u)
        hand_copy(u).start()
        return carry

    def hand_on(u, carry):
        @pl.when(mod(u - chip + 32, 4) != 0)
        def _():
            cross_copy(u).wait_recv()
            hand_copy(u).start()
        return carry

    def taken(u, carry):
        hand_copy(u).wait_recv()
        return carry

    first_slot = core
    last_slot = 1 + 2 * core

    marks_load.wait()
    ranks = lax.broadcasted_iota(jnp.int32, (HALF, 128), 0)
    spots = lax.broadcasted_iota(jnp.int32, (HALF, 128), 1)

    def places(block):
        at = pl.multiple_of((block // 2) * 128, 128)
        part = marks[:, pl.ds(at, 128)]
        mine = jnp.where(mod(block, 2) == 0, part, pltpu.roll(part, 64, 1)) - block * BLOCK
        tall = mine.T
        found = []
        for g in range(CHILDREN):
            hit = jnp.broadcast_to(tall[0:HALF, g : g + 1], (HALF, 128)) == spots
            found.append(jnp.max(jnp.where(hit, ranks, -1), axis=0, keepdims=True))
        return found

    def row_table(i, carry, block=None):
        found = places(i * 16 + p if block is None else block)
        for j in range(4):
            first, second = found[2 * j], found[2 * j + 1]
            row_perms[i, j : j + 1, :] = jnp.where(first >= 0, first, second + HALF)
        return carry


    def col_table(l, carry):
        found = places(l * 8 + q)
        for g in range(CHILDREN):
            col_places[l, g : g + 1, :] = jnp.where(
                found[g] >= 0, found[g] + mod(l, 2) * HALF, -1
            )
        return carry

    row_table(6, 0, mod(chip, 4))

    def unit_table(slot, carry):
        m = slot * 2 + chip // 4
        return col_table(2 * m + 1, col_table(2 * m, carry))

    lax.fori_loop(core, 1 + 2 * core, unit_table, 0)
    lax.fori_loop(first_slot, last_slot, own_unit, 0)
    lax.fori_loop(0, 4, fire, 0)
    lax.fori_loop(4, 8, pack_fire, 0)
    lax.fori_loop(first_slot, last_slot, spread_on, 0)
    lax.fori_loop(8, 10, pack_fire, 0)

    @pl.when(core == 0)
    def _():
        lax.fori_loop(0, 4, hand_on, 0)

    @pl.when(core == 1)
    def _():
        lax.fori_loop(0, 4, taken, 0)

    dz = remote(diag.at[y], diag.at[y], dz_s.at[0], dz_r.at[0], p, q_other)

    @pl.when(zl == 0)
    def _():
        diag[y] = cols[0, :, 0:128]
        dz.start()

    @pl.when(zl == 1)
    def _():
        dz.wait_recv()

    def dy(i):
        return remote(diag.at[y], diag.at[y], dy_s.at[i], dy_r.at[y], p, zl * 4 + mod(y + i, 4))

    for i in range(1, 4):
        dy(i).start()


    @pl.when(core == 0)
    def _():
        lax.fori_loop(4, 8, hand_on, 0)
        lax.fori_loop(8, 24, taken, 0)

    @pl.when(core == 1)
    def _():
        lax.fori_loop(8, 24, hand_on, 0)
        lax.fori_loop(4, 8, taken, 0)

    def r1(c):
        return remote(
            cols.at[:, pl.ds(c * 128, 128), pl.ds(pl.multiple_of(ph * 128, 128), 128)],
            rows.at[c], r1_s.at[c], r1_r.at[0], p, zl * 4 + c,
        )

    rz = remote(rows.at[y], rows.at[y], rz_s.at[0], rz_r.at[0], p, q_other)

    def ry(i):
        return remote(rows.at[y], rows.at[y], ry_s.at[i], ry_r.at[y], p, zl * 4 + mod(y + i, 4))

    @pl.when(own)
    def _():
        for c in range(4):
            @pl.when(y != c)
            def _():
                r1(c).start()

            @pl.when(y == c)
            def _():
                rows[c] = cols[:, c * 128 : c * 128 + 128, pl.ds(pl.multiple_of(ph * 128, 128), 128)]


    lax.fori_loop(10, 20, pack_fire, 0)

    holder = zl == pl8 // 4

    @pl.when(holder)
    def _():
        @pl.when(jnp.logical_not(own))
        def _():
            remote(
                rows.at[y], rows.at[y], r1_s.at[0], r1_r.at[0], p, q_other
            ).wait_recv()
        rz.start()

    lax.fori_loop(20, 32, pack_fire, 0)

    for i in range(1, 4):
        src = mod(y + i, 4)
        remote(diag.at[src], diag.at[src], dy_s.at[i], dy_r.at[src], p, q_other).wait_recv()

    for c in range(4):
        work[:, c * 128 : c * 128 + 128] = diag[c]
    full = work[:, 0:SPAN]
    work[:, 0:SPAN] = 0.5 * (full + full.T)
    work[:, SPAN:] = jnp.zeros((SPAN, SPAN), F32)

    lax.fori_loop(0, 8, relay_one, 0)
    factor_block(0, work, pair, Beside(32, 48))

    @pl.when(jnp.logical_not(holder))
    def _():
        rz.wait_recv()

    for i in range(1, 4):
        ry(i).start()

    lax.fori_loop(8, 16, relay_one, 0)
    factor_block(1, work, pair, Beside(40, 48))
    lax.fori_loop(16, 24, relay_one, 0)
    factor_block(2, work, pair, None)
    factor_block(3, work, pair, None)
    lax.fori_loop(0, 6, row_table, 0)
    lax.fori_loop(0, 12, col_table, 0)

    def sent_unit(slot, carry):
        u = slot * 8 + chip

        cross_copy(u).wait_send()

        def one(dx, c):
            along_copy(u, dx).wait_send()
            along_copy(slot * 8 + mod(chip + 4, 8), dx).wait_send()
            return c

        lax.fori_loop(1, 4, one, 0)
        hand_copy(u).wait_send()
        return carry

    lax.fori_loop(first_slot, last_slot, sent_unit, 0)

    def handed(u, carry):
        @pl.when(mod(u, 8) != chip)
        def _():
            hand_copy(u).wait_send()
        return carry

    @pl.when(core == 0)
    def _():
        lax.fori_loop(0, 8, handed, 0)

    @pl.when(core == 1)
    def _():
        lax.fori_loop(8, 24, handed, 0)

    @pl.when(zl == 0)
    def _():
        dz.wait_send()

    for i in range(1, 4):
        dy(i).wait_send()

    @pl.when(own)
    def _():
        for c in range(4):
            @pl.when(y != c)
            def _():
                r1(c).wait_send()

    @pl.when(holder)
    def _():
        rz.wait_send()

    for i in range(1, 4):
        ry(i).wait_send()

    for i in range(1, 4):
        src = mod(y + i, 4)
        remote(rows.at[src], rows.at[src], ry_s.at[i], ry_r.at[src], p, q_other).wait_recv()

    inverse_h, inverse_l = halves(work[:, SPAN:])
    inv_h[...] = inverse_h
    inv_l[...] = inverse_l

    def solve(block):
        high, low = halves(block)
        total = jnp.dot(inv_h[...], high, preferred_element_type=F32)
        total += jnp.dot(inv_h[...], low, preferred_element_type=F32)
        total += jnp.dot(inv_l[...], high, preferred_element_type=F32)
        return total

    def solve_rows(kk, carry):
        block = jnp.concatenate([rows[c, kk] for c in range(4)], axis=0)
        turned = solve(block).T
        at = pl.multiple_of(kk * 128, 128)
        high, low = halves(turned)
        rows_h[pl.ds(at, 128), :] = high
        rows_l[pl.ds(at, 128), :] = low
        for c in range(4):
            rows_f[c, pl.ds(at, 128), :] = turned[:, c * 128 : c * 128 + 128]
        return carry

    lax.fori_loop(0, 6, solve_rows, 0)

    def solve_cols(m, carry):
        solved = solve(cols[m])
        high, low = halves(solved)
        cols[m] = solved
        total = jnp.dot(rows_h[...], high, preferred_element_type=F32)
        total += jnp.dot(rows_h[...], low, preferred_element_type=F32)
        total += jnp.dot(rows_l[...], high, preferred_element_type=F32)
        prod[...] = total

        def less(kk, c):
            at = pl.multiple_of(kk * 128, 128)
            for h in range(2):
                where = pl.ds(kk * (128 * COL_BLOCKS) + 2 * m + h, BLOCK, stride=COL_BLOCKS)
                front[where, :] = (
                    front[where, :] - prod[pl.ds(at, 128), h * 128 : h * 128 + 128]
                )
            return c

        lax.fori_loop(0, 6, less, 0)
        return carry

    lax.fori_loop(0, 6, solve_cols, 0)

    def store(kk):
        at = pl.multiple_of(kk * (128 * COL_BLOCKS), 128 * COL_BLOCKS)
        span = pl.ds(at, 128 * COL_BLOCKS)
        return local(front.at[span], out.at[span], s_out.at[kk])

    @pl.when(p < 4)
    def _():
        for l in range(COL_BLOCKS):
            @pl.when(l * 8 + q > p)
            def _():
                front[pl.ds(l, BLOCK, stride=COL_BLOCKS), :] = cols[
                    l // 2, pl.ds(pl.multiple_of(p * 128, 128), 128),
                    (l % 2) * 128 : (l % 2) * 128 + 128,
                ]

    @pl.when(q < 4)
    def _():
        for kk in range(ROW_BLOCKS):
            @pl.when(kk * 16 + p > q)
            def _():
                front[pl.ds(kk * (128 * COL_BLOCKS), BLOCK, stride=COL_BLOCKS), :] = rows_f[
                    q, kk * 128 : kk * 128 + 128, :
                ]

        @pl.when(p == q)
        def _():
            tile = rows_f[q, 0:128, :]
            lower = lax.broadcasted_iota(jnp.int32, (128, 128), 0) >= lax.broadcasted_iota(
                jnp.int32, (128, 128), 1
            )
            front[pl.ds(0, BLOCK, stride=COL_BLOCKS), :] = jnp.where(lower, tile, tile.T)

    def arrived(kk):
        def landed(g, c):
            mine = jnp.logical_and(g == chip, mod(kk, 2) == core)

            @pl.when(jnp.logical_not(mine))
            def _():
                remote(
                    bulk_out.at[0], bulk_in.at[kk * 8 + g], bulk_s.at[0], bulk_r.at[kk * 8 + g],
                    g * 2 + mod(kk, 2), q,
                ).wait_recv()

            @pl.when(mine)
            def _():
                keep_copy(kk // 2).wait()
            return c

        lax.fori_loop(0, 8, landed, 0)

    def early(kk, carry):
        @pl.when(jnp.logical_not(panel_row(kk, p)))
        def _():
            arrived(kk)
            at = pl.multiple_of(kk * 8, 8)
            load = local(bulk_in.at[pl.ds(at, 8)], kids, kids_s.at[0])
            load.start()
            set_pick(pick, row_perms, kk)
            load.wait()

            def one(m, c):
                total = add_pair(m, col_places, lambda g: kids[g, m], pick, wide_buf)
                for h in range(2):
                    where = pl.ds(kk * (128 * COL_BLOCKS) + 2 * m + h, BLOCK, stride=COL_BLOCKS)
                    side = total[:, h * 128 : h * 128 + 128]
                    if h == 0:
                        side = jnp.where(jnp.logical_and(m == 0, q < 4), 0.0, side)
                    front[where, :] = front[where, :] + side
                return c

            lax.fori_loop(0, 6, one, 0)
        store(kk).start()
        return carry

    lax.fori_loop(EARLY, 6, lambda kk, c: (store(kk).start(), c)[1], 0)
    lax.fori_loop(0, EARLY, early, 0)
    lax.fori_loop(EARLY, 6, lambda kk, c: (arrived(kk), c)[1], 0)
    tables = [
        local(row_perms, row_out, tab_s.at[0]), local(col_places, col_out, tab_s.at[1])
    ]
    for copy in tables:
        copy.start()
    for copy in tables:
        copy.wait()

    def sent_bulk(n, carry):
        k, dest = chunk_of(n)

        @pl.when(jnp.logical_not(jnp.logical_or(dest == p, panel_row(2 * k + core, dest))))
        def _():
            bulk_copy(k, dest).wait_send()
        return carry

    lax.fori_loop(0, 48, sent_bulk, 0)

    @pl.when(core == 0)
    def _():
        def one(u, c):
            owner, copy = unit_copy(u)

            @pl.when(owner != p)
            def _():
                copy.wait_send()
            return c

        lax.fori_loop(0, 24, one, 0)

    @pl.when(p < 4)
    def _():
        def one(m, c):
            owner, slot, copy = front_copy(m)

            @pl.when(owner != p)
            def _():
                copy.wait_send()
            return c

        lax.fori_loop(0, 6, one, 0)

    def relayed(i, carry):
        k, way, cs = i // 8, mod(i, 8) // 2, mod(i, 2)
        dest, copy = second_copy(k, way, cs)

        @pl.when(jnp.logical_not(panel_row(2 * k + cs, dest)))
        def _():
            copy.wait_send()
        return carry

    lax.fori_loop(0, 24, relayed, 0)

    def stored(kk, carry):
        store(kk).wait()
        return carry

    lax.fori_loop(0, 6, stored, 0)


def set_pick(pick, row_perms, kk):
    level = lax.broadcasted_iota(jnp.int32, (128, 128), 1)
    for j in range(4):
        order = jnp.broadcast_to(row_perms[kk, j : j + 1, :], (128, 128)).T
        table = jnp.where(order == level, 1.0, 0.0).astype(BF16)
        pick[:, j * 128 : j * 128 + 128] = table
        pick[:, 512 + j * 128 : 640 + j * 128] = table


def add_pair(m, col_places, child_of, pick, wide_buf):
    for g in range(CHILDREN):
        for h in range(2):
            place = jnp.broadcast_to(col_places[2 * m + h, g : g + 1, :], (HALF, 128))
            taken = jnp.take_along_axis(
                child_of(g), jnp.maximum(place, 0), axis=1, mode="promise_in_bounds"
            )
            high, low = halves(jnp.where(place >= 0, taken, 0.0))
            wide_buf[g * 64 : g * 64 + 64, h * 128 : h * 128 + 128] = high
            wide_buf[512 + g * 64 : 576 + g * 64, h * 128 : h * 128 + 128] = low
    return jnp.dot(pick[...], wide_buf[...], preferred_element_type=F32)


EARLY = 4


def add_children(row_perms, col_places, front, children, out, pick, wide_buf):
    kk = mod(pl.program_id(0) + EARLY, ROW_BLOCKS)
    q = lax.axis_index("narrow")

    @pl.when(kk < EARLY)
    def _():
        out[...] = front[...]

    @pl.when(kk >= EARLY)
    def _():
        set_pick(pick, row_perms, kk)

        def one(m, carry):
            total = add_pair(m, col_places, lambda g: children[g, m], pick, wide_buf)
            for h in range(2):
                where = pl.ds(2 * m + h, BLOCK, stride=COL_BLOCKS)
                side = total[:, h * 128 : h * 128 + 128]
                if h == 0:
                    side = jnp.where(jnp.logical_and(m == 0, q < 4), 0.0, side)
                out[where, :] = front[where, :] + side
            return carry

        lax.fori_loop(0, 6, one, 0)


def body(root_front, child_update, child_map):
    child = child_update.reshape(3 * 16 * CHUNK, HALF)
    root = root_front.reshape(ROW_BLOCKS * BLOCK * COL_BLOCKS, BLOCK)
    vmem = lambda *shape: pltpu.VMEM(shape, F32)
    sems = lambda n: pltpu.SemaphoreType.DMA((n,))
    front, children, row_perms, col_places = pl.pallas_call(
        kernel,
        out_shape=[
            jax.ShapeDtypeStruct(root.shape, F32),
            jax.ShapeDtypeStruct((48, 6, HALF, 128), F32),
            jax.ShapeDtypeStruct((8, 4, 128), jnp.int32),
            jax.ShapeDtypeStruct((COL_BLOCKS, CHILDREN, 128), jnp.int32),
        ],
        in_specs=[pl.BlockSpec(memory_space=pl.ANY)] * 3,
        out_specs=[pl.BlockSpec(memory_space=pl.ANY)] * 4,
        scratch_shapes=[
            pltpu.VMEM((CHILDREN, 6144), jnp.int32),
            pltpu.VMEM((8, 4, 128), jnp.int32),
            pltpu.VMEM((COL_BLOCKS, CHILDREN, 128), jnp.int32),
            vmem(4 * CHUNK, HALF),
            vmem(ROW_BLOCKS * BLOCK * COL_BLOCKS, BLOCK),
            vmem(48, 6, HALF, 128),
            vmem(24, HALF, 128),
            vmem(6, BLOCK, 256),
            vmem(3, BLOCK, 256),
            vmem(6, SPAN, 256),
            vmem(4, SPAN, 128),
            vmem(4, 6, BLOCK, BLOCK),
            vmem(SPAN, 2 * SPAN),
            vmem(BLOCK, 2 * BLOCK),
            vmem(4, 768, BLOCK),
            pltpu.VMEM((768, SPAN), BF16),
            pltpu.VMEM((768, SPAN), BF16),
            vmem(768, 256),
            pltpu.VMEM((SPAN, SPAN), BF16),
            pltpu.VMEM((SPAN, SPAN), BF16),
            vmem(24, 6, HALF, 128),
            vmem(CHILDREN, 6, HALF, 128),
            pltpu.VMEM((BLOCK, 1024), BF16),
            pltpu.VMEM((1024, 256), BF16),
            sems(1), sems(3), sems(2), sems(1), sems(4), sems(1), sems(6), sems(24), sems(24), sems(48), sems(48), sems(24), sems(24),
            sems(6), sems(3), sems(24), sems(24), sems(24), sems(1), sems(1), sems(4), sems(4),
            sems(4), sems(1), sems(1), sems(1), sems(4), sems(4),
        ],
        compiler_params=pltpu.CompilerParams(
            collective_id=0, has_side_effects=True, vmem_limit_bytes=60 * 2**20
        ),
    )(child_map, child, root)
    part = pl.BlockSpec((BLOCK * COL_BLOCKS, BLOCK), lambda i: (mod(i + EARLY, ROW_BLOCKS), 0))
    out = pl.pallas_call(
        add_children,
        grid=(ROW_BLOCKS,),
        out_shape=jax.ShapeDtypeStruct(root.shape, F32),
        in_specs=[
            pl.BlockSpec((8, 4, 128), lambda i: (0, 0, 0)),
            pl.BlockSpec((COL_BLOCKS, CHILDREN, 128), lambda i: (0, 0, 0)),
            part,
            pl.BlockSpec(
                (CHILDREN, 6, HALF, 128),
                lambda i: (jnp.minimum(i + EARLY, ROW_BLOCKS - 1), 0, 0, 0),
            ),
        ],
        out_specs=part,
        scratch_shapes=[pltpu.VMEM((BLOCK, 1024), BF16), pltpu.VMEM((1024, 256), BF16)],
        compiler_params=pltpu.CompilerParams(vmem_limit_bytes=60 * 2**20),
    )(row_perms, col_places, front, children)
    return out.reshape(root_front.shape)


def solution(mesh):
    return jax.shard_map(
        body,
        mesh=mesh,
        in_specs=(
            P(None, "wide", None, None, "narrow", None),
            P("wide", None, None, None, None, "narrow", None),
            P(),
        ),
        out_specs=P(None, "wide", None, None, "narrow", None),
        check_vma=False,
    )
```

```python
import functools

import jax
import jax.numpy as jnp
from jax import lax
from jax.experimental import pallas as pl
from jax.experimental.pallas import tpu as pltpu
from jax.sharding import PartitionSpec as P

BLOCK = 128
HALF = 64
ROW_BLOCKS = 6
COL_BLOCKS = 12
CHILDREN = 8
N_WIDE = 16
N_NARROW = 8
SPAN = 512
CHUNK = HALF * COL_BLOCKS
MESH = pl.DeviceIdType.MESH
F32 = jnp.float32
BF16 = jnp.bfloat16


def mod(value, n):
    return lax.rem(value, n)


def shift_of(p, q):
    return p // 8 + (mod(p, 8) > q).astype(jnp.int32)


def halves(value):
    high = value.astype(BF16)
    low = (value - high.astype(F32)).astype(BF16)
    return high, low


def dot_full(a, b, dims):
    return lax.dot_general(
        a, b, (dims, ((), ())), precision=lax.Precision.HIGHEST, preferred_element_type=F32
    )


def thirds(value):
    high = value.astype(BF16).astype(F32)
    rest = value - high
    mid = rest.astype(BF16).astype(F32)
    low = rest - mid
    return high, mid, low


def factor_128(pair, beside):
    lane = lax.broadcasted_iota(jnp.int32, (8, 128), 1)
    sub = lax.broadcasted_iota(jnp.int32, (8, 128), 0)

    def step(b, carry):
        if beside is not None:
            beside.begin(b)
            beside.work(b)
        first = pl.multiple_of(b * 8, 8)
        rows = pair[pl.ds(first, 8), :]
        rows_a = rows[:, :128]
        rows_b = rows[:, 128:]
        turned = pltpu.roll(rows_a, mod(128 - first, 128), 1)
        cols = [jnp.broadcast_to(turned[:, j : j + 1], (8, 128)) for j in range(8)]
        e = {}
        for a in range(8):
            for j in range(a + 1):
                e[a, j] = jnp.broadcast_to(cols[j][a : a + 1, :], (8, 128))
        inv = []
        low = {}
        for j in range(8):
            d = e[j, j]
            r = lax.rsqrt(d)
            r = r * (1.5 - 0.5 * d * r * r)
            inv.append(r)
            for a in range(j + 1, 8):
                low[a, j] = e[a, j] * r
            for a in range(j + 1, 8):
                for c in range(j + 1, a + 1):
                    e[a, c] = e[a, c] - low[a, j] * low[c, j]
        ups_a = []
        ups_b = []
        out_a = jnp.zeros((8, 128), F32)
        out_b = jnp.zeros((8, 128), F32)
        for a in range(8):
            row_a = jnp.broadcast_to(rows_a[a : a + 1, :], (8, 128))
            row_b = jnp.broadcast_to(rows_b[a : a + 1, :], (8, 128))
            for j in range(a):
                row_a = row_a - low[a, j] * ups_a[j]
                row_b = row_b - low[a, j] * ups_b[j]
            row_a = row_a * inv[a]
            row_b = row_b * inv[a]
            ups_a.append(row_a)
            ups_b.append(row_b)
            out_a = jnp.where(sub == a, row_a, out_a)
            out_b = jnp.where(sub == a, row_b, out_b)
        done = jnp.concatenate([out_a, out_b], axis=1)
        pair[pl.ds(first, 8), :] = done
        mult = jnp.where(lane >= first + 8, out_a, 0.0)
        mh, mm, ml = thirds(mult)
        uh, um, ul = thirds(done)
        left = jnp.concatenate([mh, mh, mm, mh, ml, mm], axis=0).astype(BF16)
        right = jnp.concatenate([uh, um, uh, ul, uh, um], axis=0).astype(BF16)
        gone = lax.dot_general(
            left, right, (((0,), (0,)), ((), ())), preferred_element_type=F32
        )
        pair[...] = pair[...] - gone
        if beside is not None:
            beside.end(b)
        return carry

    lax.fori_loop(0, 16, step, 0)


def factor_block(jb, work, pair, beside):
    at = jb * 128
    eye = (
        lax.broadcasted_iota(jnp.int32, (128, 128), 0)
        == lax.broadcasted_iota(jnp.int32, (128, 128), 1)
    ).astype(F32)
    pair[:, 0:128] = work[at : at + 128, at : at + 128]
    pair[:, 128:256] = eye
    factor_128(pair, beside)
    inverse = pair[:, 128:256]
    if jb:
        work[at : at + 128, SPAN : SPAN + at] = dot_full(
            inverse, work[at : at + 128, SPAN : SPAN + at], ((1,), (0,))
        )
    work[at : at + 128, SPAN + at : SPAN + at + 128] = inverse
    if jb < 3:
        rest = at + 128
        above = dot_full(inverse, work[at : at + 128, rest:SPAN], ((1,), (0,)))
        work[rest:SPAN, rest:SPAN] -= dot_full(above, above, ((0,), (0,)))
        work[rest:SPAN, SPAN : SPAN + rest] -= dot_full(
            above, work[at : at + 128, SPAN : SPAN + rest], ((0,), (0,))
        )


def kernel(
    child_map, child, root, out, bulk_in, row_out, col_out,
    marks, row_perms, col_places, chunk_buf, front, bulk_out, unit_in, front_out, front_in, cols, diag, rows, work,
    pair, rows_f, rows_h, rows_l, prod, inv_h, inv_l, relay, kids, pick, wide_buf,
    kids_s, keep_s, tab_s, s_marks, s_chunk, s_front, s_out, relay_s, relay_r, bulk_s, bulk_r, unit_s, unit_r, front_s, front_r,
    cols_s, cols_r, hand_s, dz_s, dz_r, dy_s, dy_r, r1_s, r1_r, rz_s, rz_r, ry_s, ry_r,
):
    p = lax.axis_index("wide")
    q = lax.axis_index("narrow")
    core = mod(p, 2)
    chip = p // 2
    ph = p // 8
    pl8 = mod(p, 8)
    zl = q // 4
    y = mod(q, 4)
    own = pl8 == q
    shift = shift_of(p, q)
    q_other = mod(q + 4, 8)

    def remote(src, dst, ssem, rsem, wide, narrow):
        return pltpu.make_async_remote_copy(
            src_ref=src, dst_ref=dst, send_sem=ssem, recv_sem=rsem,
            device_id=(wide, narrow), device_id_type=MESH,
        )

    def local(src, dst, sem):
        return pltpu.make_async_copy(src, dst, sem)

    def chunk_of(n):
        first = jnp.where(
            ph == 0,
            jnp.where(n < 12, 8 + mod(p + n, 8), 4 + mod(n, 4)),
            jnp.where(n < 8, 4 + mod(p + n, 4), 8 + mod(p + n, 8)),
        )
        first = jnp.where(n < 4, n, first)
        late = n - 16
        k = jnp.where(n < 16, 0, 1 + mod(late // 8, 2))
        side = jnp.where(n < 32, 1 - ph, ph)
        dest = jnp.where(n < 16, first, side * 8 + mod(p + n, 8))
        return k, dest

    def chunk_copy(n):
        k, dest = chunk_of(n)
        at = pl.multiple_of((k * 16 + dest) * CHUNK, CHUNK)
        slot = mod(n, 4)
        to = pl.multiple_of(slot * CHUNK, CHUNK)
        return local(child.at[pl.ds(at, CHUNK)], chunk_buf.at[pl.ds(to, CHUNK)], s_chunk.at[slot])

    for n in range(4):
        chunk_copy(jnp.int32(n)).start()
    marks_load = local(child_map, marks, s_marks.at[0])
    marks_load.start()
    front_load = local(root, front, s_front.at[0])
    front_load.start()

    barrier = pltpu.get_barrier_semaphore()

    def greet(wide, narrow):
        pl.semaphore_signal(barrier, inc=1, device_id=(wide, narrow), device_id_type=MESH)

    def greet_wide(i, carry):
        greet(mod(p + i, 16), q)
        return carry

    lax.fori_loop(1, 16, greet_wide, 0)
    for i in range(1, 4):
        greet(p, zl * 4 + mod(y + i, 4))


    def greet_plane(i, carry):
        greet(i, q_other)
        return carry

    lax.fori_loop(0, 16, greet_plane, 0)
    pl.semaphore_wait(barrier, 34)

    def packed(n, la, lb):
        base = mod(n, 4) * CHUNK
        xa = chunk_buf[pl.ds(base + la, HALF, stride=COL_BLOCKS), :]
        xb = chunk_buf[pl.ds(base + lb, HALF, stride=COL_BLOCKS), :]
        return jnp.concatenate([xa, xb], axis=1)

    def next_chunk(n):
        @pl.when(n + 4 < 48)
        def _():
            chunk_copy(n + 4).start()

    def unit_copy(u):
        slot = u // 8
        owner = mod(u, 8) * 2 + (slot > 0).astype(jnp.int32)
        return owner, remote(
            bulk_out.at[mod(u, 4) * 3, u // 4], unit_in.at[slot * 8 + chip], unit_s.at[u], unit_r.at[slot * 8 + chip],
            owner, q,
        )

    def front_copy(m):
        u = m * 4 + p
        slot = u // 8
        owner = mod(u, 8) * 2 + (slot > 0).astype(jnp.int32)
        return owner, slot, remote(
            front_out.at[m], front_in.at[slot], front_s.at[m], front_r.at[slot], owner, q
        )

    zh = ph
    xs = mod(chip, 4)

    def bulk_copy(k, dest):
        kk = 2 * k + core
        return remote(
            bulk_out.at[dest * 3 + k], bulk_in.at[kk * 8 + chip],
            bulk_s.at[dest * 3 + k], bulk_r.at[kk * 8 + chip], dest, q,
        )

    def keep_copy(k):
        return local(bulk_out.at[p * 3 + k], bulk_in.at[(2 * k + core) * 8 + chip], keep_s.at[k])

    def first_copy(k, dest):
        xd = mod(dest // 2, 4)
        far = mod(xd - xs + 6, 4) == 0
        xi = jnp.where(far, mod(xd + 1, 4), xd)
        gap = mod(xs - xi + 4, 4)
        way = jnp.where(far, 3, jnp.where(gap == 3, 2, gap))
        zi = jnp.where(mod(core + xs + k, 2) == 0, zh, 1 - zh)
        slot = k * 8 + way * 2 + core
        return remote(
            bulk_out.at[dest * 3 + k], relay.at[slot], bulk_s.at[dest * 3 + k],
            relay_r.at[slot], (zi * 4 + xi) * 2 + mod(dest, 2), q_other,
        )

    def second_copy(k, way, cs):
        slot = k * 8 + way * 2 + cs
        side = jnp.where(jnp.logical_or(way == 1, way == 3), 1, jnp.where(way == 2, 3, 0))
        source_x = mod(xs + side, 4)
        dest_x = jnp.where(way == 3, mod(xs + 3, 4), xs)
        source_z = jnp.where(mod(cs + source_x + k, 2) == 0, zh, 1 - zh)
        dest = ((1 - source_z) * 4 + dest_x) * 2 + core
        place = (2 * k + cs) * 8 + source_z * 4 + source_x
        return dest, remote(
            relay.at[slot], bulk_in.at[place], relay_s.at[slot], bulk_r.at[place], dest, q_other
        )

    def relay_one(i, carry):
        k, way, cs = i // 8, mod(i, 8) // 2, mod(i, 2)
        dest, copy = second_copy(k, way, cs)

        @pl.when(jnp.logical_not(panel_row(2 * k + cs, dest)))
        def _():
            remote(
                bulk_out.at[0], relay.at[i], bulk_s.at[0], relay_r.at[i], p, q_other
            ).wait_recv()
            copy.start()
        return carry

    def panel_row(kk, dest):
        return jnp.logical_and(kk == 0, dest < 4)

    def pack(n, carry):
        chunk_copy(n).wait()
        k, dest = chunk_of(n)

        def one(m, c):
            bulk_out[dest * 3 + k, m] = packed(n, 2 * m, 2 * m + 1)
            return c

        lax.fori_loop(0, 6, one, 0)

        @pl.when(panel_row(2 * k + core, dest))
        def _():
            def unit(m, c):
                u = m * 4 + dest
                owner, copy = unit_copy(u)

                @pl.when(owner != p)
                def _():
                    copy.start()

                @pl.when(owner == p)
                def _():
                    unit_in[(u // 8) * 8 + chip] = bulk_out[dest * 3, m]
                return c

            lax.fori_loop(0, 6, unit, 0)
        next_chunk(n)
        return carry

    def fire(n, carry):
        k, dest = chunk_of(n)

        @pl.when(jnp.logical_not(panel_row(2 * k + core, dest)))
        def _():
            crossing = dest // 8 != ph

            @pl.when(crossing)
            def _():
                first_copy(k, dest).start()

            @pl.when(jnp.logical_not(jnp.logical_or(crossing, dest == p)))
            def _():
                bulk_copy(k, dest).start()

            @pl.when(dest == p)
            def _():
                keep_copy(k).start()
        return carry

    def pack_fire(n, carry):
        return fire(n, pack(n, carry))

    class Beside:
        def __init__(self, first, fired):
            self.first, self.fired = first, fired

        def begin(self, b):
            @pl.when(mod(b, 2) == 0)
            def _():
                chunk_copy(self.first + b // 2).wait()

        def work(self, b):
            n = self.first + b // 2
            k, dest = chunk_of(n)
            for i in range(3):
                m = mod(b, 2) * 3 + i
                bulk_out[dest * 3 + k, m] = packed(n, 2 * m, 2 * m + 1)

        def end(self, b):
            n = self.first + b // 2

            @pl.when(mod(b, 2) == 1)
            def _():
                next_chunk(n)

                @pl.when(n < self.fired)
                def _():
                    fire(n, 0)

    lax.fori_loop(0, 4, pack, 0)
    front_load.wait()

    @pl.when(p < 4)
    def _():
        def one(m, c):
            for h in range(2):
                front_out[m, :, h * 128 : h * 128 + 128] = front[
                    pl.ds(2 * m + h, BLOCK, stride=COL_BLOCKS), :
                ]
            owner, slot, copy = front_copy(m)

            @pl.when(owner != p)
            def _():
                copy.start()

            @pl.when(owner == p)
            def _():
                front_in[slot] = front_out[m]
            return c

        lax.fori_loop(0, 6, one, 0)

    def assemble(source, m, row):
        sides = []
        for h in range(2):
            total = jnp.zeros((BLOCK, BLOCK), F32)
            for pair_id in range(CHILDREN // 2):
                parts = []
                for g in (2 * pair_id, 2 * pair_id + 1):
                    place = jnp.broadcast_to(col_places[2 * m + h, g : g + 1, :], (HALF, 128))
                    taken = jnp.take_along_axis(
                        source(g), jnp.maximum(place, 0), axis=1, mode="promise_in_bounds"
                    )
                    parts.append(jnp.where(place >= 0, taken, 0.0))
                turned = jnp.concatenate(parts, axis=0).T
                order = jnp.broadcast_to(row_perms[row, pair_id : pair_id + 1, :], (BLOCK, BLOCK))
                total += jnp.take_along_axis(turned, order, axis=1, mode="promise_in_bounds")
            sides.append(total.T)
        return sides

    def cols_at(u):
        return cols.at[u // 4, pl.ds(pl.multiple_of(mod(u, 4) * 128, 128), 128), :]

    def cross_copy(u):
        return remote(
            cols_at(u), cols_at(u), cols_s.at[(u // 8) * 8], cols_r.at[u],
            mod(chip + 4, 8) * 2 + core, q,
        )

    def along_copy(u, dx):
        far = jnp.where(mod(u, 8) == chip, 0, 3)
        return remote(
            cols_at(u), cols_at(u), cols_s.at[(u // 8) * 8 + far + dx], cols_r.at[u],
            (ph * 4 + mod(chip + dx, 4)) * 2 + core, q,
        )

    def along(u):
        def send(dx, c):
            along_copy(u, dx).start()
            return c

        lax.fori_loop(1, 4, send, 0)

    def hand_copy(u):
        return remote(cols_at(u), cols_at(u), hand_s.at[u], cols_r.at[u], chip * 2 + 1 - core, q)

    def own_unit(slot, carry):
        u = slot * 8 + chip
        block = mod(u, 4)

        def landed(g, c):
            @pl.when(jnp.logical_or(core == 1, g != chip))
            def _():
                remote(
                    bulk_out.at[0, 0], unit_in.at[slot * 8 + g], unit_s.at[0],
                    unit_r.at[slot * 8 + g], g * 2, q,
                ).wait_recv()
            return c

        lax.fori_loop(0, 8, landed, 0)

        @pl.when(block != p)
        def _():
            remote(
                front_out.at[0], front_in.at[slot], front_s.at[0], front_r.at[slot], block, q
            ).wait_recv()

        sides = assemble(lambda g: unit_in[slot * 8 + g], u // 4, 6)
        cols[u // 4, pl.ds(pl.multiple_of(block * 128, 128), 128), :] = (
            jnp.concatenate(sides, axis=1) + front_in[slot]
        )

        cross_copy(u).start()
        along(u)
        hand_copy(u).start()
        return carry

    def spread_on(slot, carry):
        u = slot * 8 + mod(chip + 4, 8)
        cross_copy(u).wait_recv()
        along(u)
        hand_copy(u).start()
        return carry

    def hand_on(u, carry):
        @pl.when(mod(u - chip + 32, 4) != 0)
        def _():
            cross_copy(u).wait_recv()
            hand_copy(u).start()
        return carry

    def taken(u, carry):
        hand_copy(u).wait_recv()
        return carry

    first_slot = core
    last_slot = 1 + 2 * core

    marks_load.wait()
    ranks = lax.broadcasted_iota(jnp.int32, (HALF, 128), 0)
    spots = lax.broadcasted_iota(jnp.int32, (HALF, 128), 1)

    def places(block):
        at = pl.multiple_of((block // 2) * 128, 128)
        part = marks[:, pl.ds(at, 128)]
        mine = jnp.where(mod(block, 2) == 0, part, pltpu.roll(part, 64, 1)) - block * BLOCK
        tall = mine.T
        found = []
        for g in range(CHILDREN):
            hit = jnp.broadcast_to(tall[0:HALF, g : g + 1], (HALF, 128)) == spots
            found.append(jnp.max(jnp.where(hit, ranks, -1), axis=0, keepdims=True))
        return found

    def row_table(i, carry, block=None):
        found = places(i * 16 + p if block is None else block)
        for j in range(4):
            first, second = found[2 * j], found[2 * j + 1]
            row_perms[i, j : j + 1, :] = jnp.where(first >= 0, first, second + HALF)
        return carry


    def col_table(l, carry):
        found = places(l * 8 + q)
        for g in range(CHILDREN):
            col_places[l, g : g + 1, :] = jnp.where(
                found[g] >= 0, found[g] + mod(l, 2) * HALF, -1
            )
        return carry

    row_table(6, 0, mod(chip, 4))

    class Tables:
        def begin(self, b):
            pass

        def work(self, b):
            col_table(jnp.minimum(b, 11), 0)
            row_table(jnp.minimum(b, 5), 0)

        def end(self, b):
            pass

    def unit_table(slot, carry):
        m = slot * 2 + chip // 4
        return col_table(2 * m + 1, col_table(2 * m, carry))

    lax.fori_loop(core, 1 + 2 * core, unit_table, 0)
    lax.fori_loop(first_slot, last_slot, own_unit, 0)
    lax.fori_loop(0, 4, fire, 0)
    lax.fori_loop(4, 8, pack_fire, 0)
    lax.fori_loop(first_slot, last_slot, spread_on, 0)
    lax.fori_loop(8, 10, pack_fire, 0)

    @pl.when(core == 0)
    def _():
        lax.fori_loop(0, 4, hand_on, 0)

    @pl.when(core == 1)
    def _():
        lax.fori_loop(0, 4, taken, 0)

    dz = remote(diag.at[y], diag.at[y], dz_s.at[0], dz_r.at[0], p, q_other)

    @pl.when(zl == 0)
    def _():
        diag[y] = cols[0, :, 0:128]
        dz.start()

    @pl.when(zl == 1)
    def _():
        dz.wait_recv()

    def dy(i):
        return remote(diag.at[y], diag.at[y], dy_s.at[i], dy_r.at[y], p, zl * 4 + mod(y + i, 4))

    for i in range(1, 4):
        dy(i).start()


    @pl.when(core == 0)
    def _():
        lax.fori_loop(4, 8, hand_on, 0)
        lax.fori_loop(8, 24, taken, 0)

    @pl.when(core == 1)
    def _():
        lax.fori_loop(8, 24, hand_on, 0)
        lax.fori_loop(4, 8, taken, 0)

    def r1(c):
        return remote(
            cols.at[:, pl.ds(c * 128, 128), pl.ds(pl.multiple_of(ph * 128, 128), 128)],
            rows.at[c], r1_s.at[c], r1_r.at[0], p, zl * 4 + c,
        )

    rz = remote(rows.at[y], rows.at[y], rz_s.at[0], rz_r.at[0], p, q_other)

    def ry(i):
        return remote(rows.at[y], rows.at[y], ry_s.at[i], ry_r.at[y], p, zl * 4 + mod(y + i, 4))

    @pl.when(own)
    def _():
        for c in range(4):
            @pl.when(y != c)
            def _():
                r1(c).start()

            @pl.when(y == c)
            def _():
                rows[c] = cols[:, c * 128 : c * 128 + 128, pl.ds(pl.multiple_of(ph * 128, 128), 128)]


    lax.fori_loop(10, 20, pack_fire, 0)

    holder = zl == pl8 // 4

    @pl.when(holder)
    def _():
        @pl.when(jnp.logical_not(own))
        def _():
            remote(
                rows.at[y], rows.at[y], r1_s.at[0], r1_r.at[0], p, q_other
            ).wait_recv()
        rz.start()

    lax.fori_loop(20, 24, pack_fire, 0)

    for i in range(1, 4):
        src = mod(y + i, 4)
        remote(diag.at[src], diag.at[src], dy_s.at[i], dy_r.at[src], p, q_other).wait_recv()

    for c in range(4):
        work[:, c * 128 : c * 128 + 128] = diag[c]
    full = work[:, 0:SPAN]
    work[:, 0:SPAN] = 0.5 * (full + full.T)
    work[:, SPAN:] = jnp.zeros((SPAN, SPAN), F32)

    lax.fori_loop(0, 8, relay_one, 0)
    factor_block(0, work, pair, Beside(24, 48))

    @pl.when(jnp.logical_not(holder))
    def _():
        rz.wait_recv()

    for i in range(1, 4):
        ry(i).start()

    lax.fori_loop(8, 16, relay_one, 0)
    factor_block(1, work, pair, Beside(32, 48))
    lax.fori_loop(16, 24, relay_one, 0)
    factor_block(2, work, pair, Beside(40, 48))
    factor_block(3, work, pair, Tables())

    def sent_unit(slot, carry):
        u = slot * 8 + chip

        cross_copy(u).wait_send()

        def one(dx, c):
            along_copy(u, dx).wait_send()
            along_copy(slot * 8 + mod(chip + 4, 8), dx).wait_send()
            return c

        lax.fori_loop(1, 4, one, 0)
        hand_copy(u).wait_send()
        return carry

    lax.fori_loop(first_slot, last_slot, sent_unit, 0)

    def handed(u, carry):
        @pl.when(mod(u, 8) != chip)
        def _():
            hand_copy(u).wait_send()
        return carry

    @pl.when(core == 0)
    def _():
        lax.fori_loop(0, 8, handed, 0)

    @pl.when(core == 1)
    def _():
        lax.fori_loop(8, 24, handed, 0)

    @pl.when(zl == 0)
    def _():
        dz.wait_send()

    for i in range(1, 4):
        dy(i).wait_send()

    @pl.when(own)
    def _():
        for c in range(4):
            @pl.when(y != c)
            def _():
                r1(c).wait_send()

    @pl.when(holder)
    def _():
        rz.wait_send()

    for i in range(1, 4):
        ry(i).wait_send()

    for i in range(1, 4):
        src = mod(y + i, 4)
        remote(rows.at[src], rows.at[src], ry_s.at[i], ry_r.at[src], p, q_other).wait_recv()

    inverse_h, inverse_l = halves(work[:, SPAN:])
    inv_h[...] = inverse_h
    inv_l[...] = inverse_l

    def solve(block):
        high, low = halves(block)
        total = jnp.dot(inv_h[...], high, preferred_element_type=F32)
        total += jnp.dot(inv_h[...], low, preferred_element_type=F32)
        total += jnp.dot(inv_l[...], high, preferred_element_type=F32)
        return total

    def solve_rows(i, carry):
        parts = [
            jnp.concatenate([rows[c, 2 * i + h] for c in range(4)], axis=0) for h in range(2)
        ]
        turned = solve(jnp.concatenate(parts, axis=1)).T
        at = pl.multiple_of(i * 256, 256)
        high, low = halves(turned)
        rows_h[pl.ds(at, 256), :] = high
        rows_l[pl.ds(at, 256), :] = low
        for c in range(4):
            rows_f[c, pl.ds(at, 256), :] = turned[:, c * 128 : c * 128 + 128]
        return carry

    lax.fori_loop(0, 3, solve_rows, 0)

    def solve_cols(m, carry):
        solved = solve(cols[m])
        high, low = halves(solved)
        cols[m] = solved
        total = jnp.dot(rows_h[...], high, preferred_element_type=F32)
        total += jnp.dot(rows_h[...], low, preferred_element_type=F32)
        total += jnp.dot(rows_l[...], high, preferred_element_type=F32)
        prod[...] = total

        def less(kk, c):
            at = pl.multiple_of(kk * 128, 128)
            for h in range(2):
                where = pl.ds(kk * (128 * COL_BLOCKS) + 2 * m + h, BLOCK, stride=COL_BLOCKS)
                front[where, :] = (
                    front[where, :] - prod[pl.ds(at, 128), h * 128 : h * 128 + 128]
                )
            return c

        lax.fori_loop(0, 6, less, 0)
        return carry

    lax.fori_loop(0, 6, solve_cols, 0)

    def store(kk):
        at = pl.multiple_of(kk * (128 * COL_BLOCKS), 128 * COL_BLOCKS)
        span = pl.ds(at, 128 * COL_BLOCKS)
        return local(front.at[span], out.at[span], s_out.at[kk])

    @pl.when(p < 4)
    def _():
        for l in range(COL_BLOCKS):
            @pl.when(l * 8 + q > p)
            def _():
                front[pl.ds(l, BLOCK, stride=COL_BLOCKS), :] = cols[
                    l // 2, pl.ds(pl.multiple_of(p * 128, 128), 128),
                    (l % 2) * 128 : (l % 2) * 128 + 128,
                ]

    @pl.when(q < 4)
    def _():
        for kk in range(ROW_BLOCKS):
            @pl.when(kk * 16 + p > q)
            def _():
                front[pl.ds(kk * (128 * COL_BLOCKS), BLOCK, stride=COL_BLOCKS), :] = rows_f[
                    q, kk * 128 : kk * 128 + 128, :
                ]

        @pl.when(p == q)
        def _():
            tile = rows_f[q, 0:128, :]
            lower = lax.broadcasted_iota(jnp.int32, (128, 128), 0) >= lax.broadcasted_iota(
                jnp.int32, (128, 128), 1
            )
            front[pl.ds(0, BLOCK, stride=COL_BLOCKS), :] = jnp.where(lower, tile, tile.T)

    def arrived(kk):
        def landed(g, c):
            mine = jnp.logical_and(g == chip, mod(kk, 2) == core)

            @pl.when(jnp.logical_not(mine))
            def _():
                remote(
                    bulk_out.at[0], bulk_in.at[kk * 8 + g], bulk_s.at[0], bulk_r.at[kk * 8 + g],
                    g * 2 + mod(kk, 2), q,
                ).wait_recv()

            @pl.when(mine)
            def _():
                keep_copy(kk // 2).wait()
            return c

        lax.fori_loop(0, 8, landed, 0)

    def early(kk, carry):
        @pl.when(jnp.logical_not(panel_row(kk, p)))
        def _():
            arrived(kk)
            at = pl.multiple_of(kk * 8, 8)
            load = local(bulk_in.at[pl.ds(at, 8)], kids, kids_s.at[0])
            load.start()
            set_pick(pick, row_perms, kk)
            load.wait()

            def one(m, c):
                total = add_pair(m, col_places, lambda g: kids[g, m], pick, wide_buf)
                for h in range(2):
                    where = pl.ds(kk * (128 * COL_BLOCKS) + 2 * m + h, BLOCK, stride=COL_BLOCKS)
                    side = total[:, h * 128 : h * 128 + 128]
                    if h == 0:
                        side = jnp.where(jnp.logical_and(m == 0, q < 4), 0.0, side)
                    front[where, :] = front[where, :] + side
                return c

            lax.fori_loop(0, 6, one, 0)
        store(kk).start()
        return carry

    lax.fori_loop(EARLY, 6, lambda kk, c: (store(kk).start(), c)[1], 0)
    lax.fori_loop(0, EARLY, early, 0)
    lax.fori_loop(EARLY, 6, lambda kk, c: (arrived(kk), c)[1], 0)
    tables = [
        local(row_perms, row_out, tab_s.at[0]), local(col_places, col_out, tab_s.at[1])
    ]
    for copy in tables:
        copy.start()
    for copy in tables:
        copy.wait()

    def sent_bulk(n, carry):
        k, dest = chunk_of(n)

        @pl.when(jnp.logical_not(jnp.logical_or(dest == p, panel_row(2 * k + core, dest))))
        def _():
            bulk_copy(k, dest).wait_send()
        return carry

    lax.fori_loop(0, 48, sent_bulk, 0)

    @pl.when(core == 0)
    def _():
        def one(u, c):
            owner, copy = unit_copy(u)

            @pl.when(owner != p)
            def _():
                copy.wait_send()
            return c

        lax.fori_loop(0, 24, one, 0)

    @pl.when(p < 4)
    def _():
        def one(m, c):
            owner, slot, copy = front_copy(m)

            @pl.when(owner != p)
            def _():
                copy.wait_send()
            return c

        lax.fori_loop(0, 6, one, 0)

    def relayed(i, carry):
        k, way, cs = i // 8, mod(i, 8) // 2, mod(i, 2)
        dest, copy = second_copy(k, way, cs)

        @pl.when(jnp.logical_not(panel_row(2 * k + cs, dest)))
        def _():
            copy.wait_send()
        return carry

    lax.fori_loop(0, 24, relayed, 0)

    def stored(kk, carry):
        store(kk).wait()
        return carry

    lax.fori_loop(0, 6, stored, 0)


def set_pick(pick, row_perms, kk):
    level = lax.broadcasted_iota(jnp.int32, (128, 128), 1)
    for j in range(4):
        order = jnp.broadcast_to(row_perms[kk, j : j + 1, :], (128, 128)).T
        table = jnp.where(order == level, 1.0, 0.0).astype(BF16)
        pick[:, j * 128 : j * 128 + 128] = table
        pick[:, 512 + j * 128 : 640 + j * 128] = table


def add_pair(m, col_places, child_of, pick, wide_buf):
    for g in range(CHILDREN):
        for h in range(2):
            place = jnp.broadcast_to(col_places[2 * m + h, g : g + 1, :], (HALF, 128))
            taken = jnp.take_along_axis(
                child_of(g), jnp.maximum(place, 0), axis=1, mode="promise_in_bounds"
            )
            high, low = halves(jnp.where(place >= 0, taken, 0.0))
            wide_buf[g * 64 : g * 64 + 64, h * 128 : h * 128 + 128] = high
            wide_buf[512 + g * 64 : 576 + g * 64, h * 128 : h * 128 + 128] = low
    return jnp.dot(pick[...], wide_buf[...], preferred_element_type=F32)


EARLY = 4


def add_children(row_perms, col_places, front, children, out, pick, wide_buf):
    kk = mod(pl.program_id(0) + EARLY, ROW_BLOCKS)
    q = lax.axis_index("narrow")

    @pl.when(kk < EARLY)
    def _():
        out[...] = front[...]

    @pl.when(kk >= EARLY)
    def _():
        set_pick(pick, row_perms, kk)

        def one(m, carry):
            total = add_pair(m, col_places, lambda g: children[g, m], pick, wide_buf)
            for h in range(2):
                where = pl.ds(2 * m + h, BLOCK, stride=COL_BLOCKS)
                side = total[:, h * 128 : h * 128 + 128]
                if h == 0:
                    side = jnp.where(jnp.logical_and(m == 0, q < 4), 0.0, side)
                out[where, :] = front[where, :] + side
            return carry

        lax.fori_loop(0, 6, one, 0)


def body(root_front, child_update, child_map):
    child = child_update.reshape(3 * 16 * CHUNK, HALF)
    root = root_front.reshape(ROW_BLOCKS * BLOCK * COL_BLOCKS, BLOCK)
    vmem = lambda *shape: pltpu.VMEM(shape, F32)
    sems = lambda n: pltpu.SemaphoreType.DMA((n,))
    front, children, row_perms, col_places = pl.pallas_call(
        kernel,
        out_shape=[
            jax.ShapeDtypeStruct(root.shape, F32),
            jax.ShapeDtypeStruct((48, 6, HALF, 128), F32),
            jax.ShapeDtypeStruct((8, 4, 128), jnp.int32),
            jax.ShapeDtypeStruct((COL_BLOCKS, CHILDREN, 128), jnp.int32),
        ],
        in_specs=[pl.BlockSpec(memory_space=pl.ANY)] * 3,
        out_specs=[pl.BlockSpec(memory_space=pl.ANY)] * 4,
        scratch_shapes=[
            pltpu.VMEM((CHILDREN, 6144), jnp.int32),
            pltpu.VMEM((8, 4, 128), jnp.int32),
            pltpu.VMEM((COL_BLOCKS, CHILDREN, 128), jnp.int32),
            vmem(4 * CHUNK, HALF),
            vmem(ROW_BLOCKS * BLOCK * COL_BLOCKS, BLOCK),
            vmem(48, 6, HALF, 128),
            vmem(24, HALF, 128),
            vmem(6, BLOCK, 256),
            vmem(3, BLOCK, 256),
            vmem(6, SPAN, 256),
            vmem(4, SPAN, 128),
            vmem(4, 6, BLOCK, BLOCK),
            vmem(SPAN, 2 * SPAN),
            vmem(BLOCK, 2 * BLOCK),
            vmem(4, 768, BLOCK),
            pltpu.VMEM((768, SPAN), BF16),
            pltpu.VMEM((768, SPAN), BF16),
            vmem(768, 256),
            pltpu.VMEM((SPAN, SPAN), BF16),
            pltpu.VMEM((SPAN, SPAN), BF16),
            vmem(24, 6, HALF, 128),
            vmem(CHILDREN, 6, HALF, 128),
            pltpu.VMEM((BLOCK, 1024), BF16),
            pltpu.VMEM((1024, 256), BF16),
            sems(1), sems(3), sems(2), sems(1), sems(4), sems(1), sems(6), sems(24), sems(24), sems(48), sems(48), sems(24), sems(24),
            sems(6), sems(3), sems(24), sems(24), sems(24), sems(1), sems(1), sems(4), sems(4),
            sems(4), sems(1), sems(1), sems(1), sems(4), sems(4),
        ],
        compiler_params=pltpu.CompilerParams(
            collective_id=0, has_side_effects=True, vmem_limit_bytes=60 * 2**20
        ),
    )(child_map, child, root)
    part = pl.BlockSpec((BLOCK * COL_BLOCKS, BLOCK), lambda i: (mod(i + EARLY, ROW_BLOCKS), 0))
    out = pl.pallas_call(
        add_children,
        grid=(ROW_BLOCKS,),
        out_shape=jax.ShapeDtypeStruct(root.shape, F32),
        in_specs=[
            pl.BlockSpec((8, 4, 128), lambda i: (0, 0, 0)),
            pl.BlockSpec((COL_BLOCKS, CHILDREN, 128), lambda i: (0, 0, 0)),
            part,
            pl.BlockSpec(
                (CHILDREN, 6, HALF, 128),
                lambda i: (jnp.minimum(i + EARLY, ROW_BLOCKS - 1), 0, 0, 0),
            ),
        ],
        out_specs=part,
        scratch_shapes=[pltpu.VMEM((BLOCK, 1024), BF16), pltpu.VMEM((1024, 256), BF16)],
        compiler_params=pltpu.CompilerParams(vmem_limit_bytes=60 * 2**20),
    )(row_perms, col_places, front, children)
    return out.reshape(root_front.shape)


def solution(mesh):
    return jax.shard_map(
        body,
        mesh=mesh,
        in_specs=(
            P(None, "wide", None, None, "narrow", None),
            P("wide", None, None, None, None, "narrow", None),
            P(),
        ),
        out_specs=P(None, "wide", None, None, "narrow", None),
        check_vma=False,
    )
```

```python
import functools

import jax
import jax.numpy as jnp
from jax import lax
from jax.experimental import pallas as pl
from jax.experimental.pallas import tpu as pltpu
from jax.sharding import PartitionSpec as P

BLOCK = 128
HALF = 64
ROW_BLOCKS = 6
COL_BLOCKS = 12
CHILDREN = 8
N_WIDE = 16
N_NARROW = 8
SPAN = 512
CHUNK = HALF * COL_BLOCKS
MESH = pl.DeviceIdType.MESH
F32 = jnp.float32
BF16 = jnp.bfloat16


def mod(value, n):
    return lax.rem(value, n)


def shift_of(p, q):
    return p // 8 + (mod(p, 8) > q).astype(jnp.int32)


def halves(value):
    high = value.astype(BF16)
    low = (value - high.astype(F32)).astype(BF16)
    return high, low


def dot_full(a, b, dims):
    return lax.dot_general(
        a, b, (dims, ((), ())), precision=lax.Precision.HIGHEST, preferred_element_type=F32
    )


def thirds(value):
    high = value.astype(BF16).astype(F32)
    rest = value - high
    mid = rest.astype(BF16).astype(F32)
    low = rest - mid
    return high, mid, low


def factor_eight(cols):
    e = {}
    for a in range(8):
        for j in range(a + 1):
            e[a, j] = jnp.broadcast_to(cols[j][a : a + 1, :], (8, 128))
    inv = []
    low = {}
    for j in range(8):
        d = e[j, j]
        r = lax.rsqrt(d)
        r = r * (1.5 - 0.5 * d * r * r)
        inv.append(r)
        for a in range(j + 1, 8):
            low[a, j] = e[a, j] * r
        for a in range(j + 1, 8):
            for c in range(j + 1, a + 1):
                e[a, c] = e[a, c] - low[a, j] * low[c, j]
    return low, inv


def solve_eight(rows, low, inv):
    found = []
    for a in range(8):
        row = jnp.broadcast_to(rows[a : a + 1, :], (8, 128))
        for j in range(a):
            row = row - low[a, j] * found[j]
        found.append(row * inv[a])
    return found


def factor_128(pair, beside):
    lane = lax.broadcasted_iota(jnp.int32, (16, 128), 1)
    sub = lax.broadcasted_iota(jnp.int32, (8, 128), 0)

    def spread(value, j):
        return jnp.broadcast_to(value[:, j : j + 1], (8, 128))

    def gather_rows(found):
        total = found[0]
        for a in range(1, 8):
            total = jnp.where(sub == a, found[a], total)
        return total

    def step(b, carry):
        if beside is not None:
            beside.begin(b)
            beside.work(b)
        first = pl.multiple_of(b * 16, 16)
        rows = pair[pl.ds(first, 16), :]
        back = mod(128 - first, 128)
        top_a, top_b = rows[0:8, :128], rows[0:8, 128:]
        end_a, end_b = rows[8:16, :128], rows[8:16, 128:]
        top_t = pltpu.roll(top_a, back, 1)
        end_t = pltpu.roll(end_a, back, 1)
        low, inv = factor_eight([spread(top_t, j) for j in range(8)])
        ups_t = solve_eight(top_t, low, inv)
        ups_a = solve_eight(top_a, low, inv)
        ups_b = solve_eight(top_b, low, inv)
        link = []
        for a in range(8):
            value = spread(end_t, a)
            for j in range(a):
                value = value - link[j] * low[a, j]
            link.append(value * inv[a])
        for a in range(8):
            end_t = end_t - link[a] * ups_t[a]
            end_a = end_a - link[a] * ups_a[a]
            end_b = end_b - link[a] * ups_b[a]
        low, inv = factor_eight([spread(end_t, 8 + j) for j in range(8)])
        more_a = solve_eight(end_a, low, inv)
        more_b = solve_eight(end_b, low, inv)
        done_a = jnp.concatenate([gather_rows(ups_a), gather_rows(more_a)], axis=0)
        done_b = jnp.concatenate([gather_rows(ups_b), gather_rows(more_b)], axis=0)
        done = jnp.concatenate([done_a, done_b], axis=1)
        pair[pl.ds(first, 16), :] = done
        mult = jnp.where(lane >= first + 16, done_a, 0.0)
        mh, mm, ml = thirds(mult)
        uh, um, ul = thirds(done)
        left = jnp.concatenate([mh, mh, mm, mh, ml, mm], axis=0).astype(BF16)
        right = jnp.concatenate([uh, um, uh, ul, uh, um], axis=0).astype(BF16)
        gone = lax.dot_general(
            left, right, (((0,), (0,)), ((), ())), preferred_element_type=F32
        )
        pair[...] = pair[...] - gone
        if beside is not None:
            beside.end(b)
        return carry

    lax.fori_loop(0, 8, step, 0)


def factor_block(jb, work, pair, beside):
    at = jb * 128
    eye = (
        lax.broadcasted_iota(jnp.int32, (128, 128), 0)
        == lax.broadcasted_iota(jnp.int32, (128, 128), 1)
    ).astype(F32)
    pair[:, 0:128] = work[at : at + 128, at : at + 128]
    pair[:, 128:256] = eye
    factor_128(pair, beside)
    inverse = pair[:, 128:256]
    if jb:
        work[at : at + 128, SPAN : SPAN + at] = dot_full(
            inverse, work[at : at + 128, SPAN : SPAN + at], ((1,), (0,))
        )
    work[at : at + 128, SPAN + at : SPAN + at + 128] = inverse
    if jb < 3:
        rest = at + 128
        above = dot_full(inverse, work[at : at + 128, rest:SPAN], ((1,), (0,)))
        work[rest:SPAN, rest:SPAN] -= dot_full(above, above, ((0,), (0,)))
        work[rest:SPAN, SPAN : SPAN + rest] -= dot_full(
            above, work[at : at + 128, SPAN : SPAN + rest], ((0,), (0,))
        )


def kernel(
    child_map, child, root, out, bulk_in, row_out, col_out,
    marks, row_perms, col_places, chunk_buf, front, bulk_out, unit_in, front_out, front_in, cols, diag, rows, work,
    pair, rows_f, rows_h, rows_l, prod, inv_h, inv_l, relay, kids, pick, wide_buf,
    kids_s, keep_s, tab_s, s_marks, s_chunk, s_front, s_out, relay_s, relay_r, bulk_s, bulk_r, unit_s, unit_r, front_s, front_r,
    cols_s, cols_r, hand_s, dz_s, dz_r, dy_s, dy_r, r1_s, r1_r, rz_s, rz_r, ry_s, ry_r,
):
    p = lax.axis_index("wide")
    q = lax.axis_index("narrow")
    core = mod(p, 2)
    chip = p // 2
    ph = p // 8
    pl8 = mod(p, 8)
    zl = q // 4
    y = mod(q, 4)
    own = pl8 == q
    shift = shift_of(p, q)
    q_other = mod(q + 4, 8)

    def remote(src, dst, ssem, rsem, wide, narrow):
        return pltpu.make_async_remote_copy(
            src_ref=src, dst_ref=dst, send_sem=ssem, recv_sem=rsem,
            device_id=(wide, narrow), device_id_type=MESH,
        )

    def local(src, dst, sem):
        return pltpu.make_async_copy(src, dst, sem)

    def chunk_of(n):
        first = jnp.where(
            ph == 0,
            jnp.where(n < 12, 8 + mod(p + n, 8), 4 + mod(n, 4)),
            jnp.where(n < 8, 4 + mod(p + n, 4), 8 + mod(p + n, 8)),
        )
        first = jnp.where(n < 4, n, first)
        late = n - 16
        k = jnp.where(n < 16, 0, 1 + mod(late // 8, 2))
        side = jnp.where(n < 32, 1 - ph, ph)
        dest = jnp.where(n < 16, first, side * 8 + mod(p + n, 8))
        return k, dest

    def chunk_copy(n):
        k, dest = chunk_of(n)
        at = pl.multiple_of((k * 16 + dest) * CHUNK, CHUNK)
        slot = mod(n, 4)
        to = pl.multiple_of(slot * CHUNK, CHUNK)
        return local(child.at[pl.ds(at, CHUNK)], chunk_buf.at[pl.ds(to, CHUNK)], s_chunk.at[slot])

    for n in range(4):
        chunk_copy(jnp.int32(n)).start()
    marks_load = local(child_map, marks, s_marks.at[0])
    marks_load.start()
    front_load = local(root, front, s_front.at[0])
    front_load.start()

    barrier = pltpu.get_barrier_semaphore()

    def greet(wide, narrow):
        pl.semaphore_signal(barrier, inc=1, device_id=(wide, narrow), device_id_type=MESH)

    def greet_wide(i, carry):
        greet(mod(p + i, 16), q)
        return carry

    lax.fori_loop(1, 16, greet_wide, 0)
    for i in range(1, 4):
        greet(p, zl * 4 + mod(y + i, 4))


    def greet_plane(i, carry):
        greet(i, q_other)
        return carry

    lax.fori_loop(0, 16, greet_plane, 0)
    pl.semaphore_wait(barrier, 34)

    def packed(n, la, lb):
        base = mod(n, 4) * CHUNK
        xa = chunk_buf[pl.ds(base + la, HALF, stride=COL_BLOCKS), :]
        xb = chunk_buf[pl.ds(base + lb, HALF, stride=COL_BLOCKS), :]
        return jnp.concatenate([xa, xb], axis=1)

    def next_chunk(n):
        @pl.when(n + 4 < 48)
        def _():
            chunk_copy(n + 4).start()

    def unit_copy(u):
        slot = u // 8
        owner = mod(u, 8) * 2 + (slot > 0).astype(jnp.int32)
        return owner, remote(
            bulk_out.at[mod(u, 4) * 3, u // 4], unit_in.at[slot * 8 + chip], unit_s.at[u], unit_r.at[slot * 8 + chip],
            owner, q,
        )

    def front_copy(m):
        u = m * 4 + p
        slot = u // 8
        owner = mod(u, 8) * 2 + (slot > 0).astype(jnp.int32)
        return owner, slot, remote(
            front_out.at[m], front_in.at[slot], front_s.at[m], front_r.at[slot], owner, q
        )

    zh = ph
    xs = mod(chip, 4)

    def bulk_copy(k, dest):
        kk = 2 * k + core
        return remote(
            bulk_out.at[dest * 3 + k], bulk_in.at[kk * 8 + chip],
            bulk_s.at[dest * 3 + k], bulk_r.at[kk * 8 + chip], dest, q,
        )

    def keep_copy(k):
        return local(bulk_out.at[p * 3 + k], bulk_in.at[(2 * k + core) * 8 + chip], keep_s.at[k])

    def first_copy(k, dest):
        xd = mod(dest // 2, 4)
        far = mod(xd - xs + 6, 4) == 0
        xi = jnp.where(far, mod(xd + 1, 4), xd)
        gap = mod(xs - xi + 4, 4)
        way = jnp.where(far, 3, jnp.where(gap == 3, 2, gap))
        zi = jnp.where(mod(core + xs + k, 2) == 0, zh, 1 - zh)
        slot = k * 8 + way * 2 + core
        return remote(
            bulk_out.at[dest * 3 + k], relay.at[slot], bulk_s.at[dest * 3 + k],
            relay_r.at[slot], (zi * 4 + xi) * 2 + mod(dest, 2), q_other,
        )

    def second_copy(k, way, cs):
        slot = k * 8 + way * 2 + cs
        side = jnp.where(jnp.logical_or(way == 1, way == 3), 1, jnp.where(way == 2, 3, 0))
        source_x = mod(xs + side, 4)
        dest_x = jnp.where(way == 3, mod(xs + 3, 4), xs)
        source_z = jnp.where(mod(cs + source_x + k, 2) == 0, zh, 1 - zh)
        dest = ((1 - source_z) * 4 + dest_x) * 2 + core
        place = (2 * k + cs) * 8 + source_z * 4 + source_x
        return dest, remote(
            relay.at[slot], bulk_in.at[place], relay_s.at[slot], bulk_r.at[place], dest, q_other
        )

    def relay_one(i, carry):
        k, way, cs = i // 8, mod(i, 8) // 2, mod(i, 2)
        dest, copy = second_copy(k, way, cs)

        @pl.when(jnp.logical_not(panel_row(2 * k + cs, dest)))
        def _():
            remote(
                bulk_out.at[0], relay.at[i], bulk_s.at[0], relay_r.at[i], p, q_other
            ).wait_recv()
            copy.start()
        return carry

    def panel_row(kk, dest):
        return jnp.logical_and(kk == 0, dest < 4)

    def pack(n, carry):
        chunk_copy(n).wait()
        k, dest = chunk_of(n)

        def one(m, c):
            bulk_out[dest * 3 + k, m] = packed(n, 2 * m, 2 * m + 1)
            return c

        lax.fori_loop(0, 6, one, 0)

        @pl.when(panel_row(2 * k + core, dest))
        def _():
            def unit(m, c):
                u = m * 4 + dest
                owner, copy = unit_copy(u)

                @pl.when(owner != p)
                def _():
                    copy.start()

                @pl.when(owner == p)
                def _():
                    unit_in[(u // 8) * 8 + chip] = bulk_out[dest * 3, m]
                return c

            lax.fori_loop(0, 6, unit, 0)
        next_chunk(n)
        return carry

    def fire(n, carry):
        k, dest = chunk_of(n)

        @pl.when(jnp.logical_not(panel_row(2 * k + core, dest)))
        def _():
            crossing = dest // 8 != ph

            @pl.when(crossing)
            def _():
                first_copy(k, dest).start()

            @pl.when(jnp.logical_not(jnp.logical_or(crossing, dest == p)))
            def _():
                bulk_copy(k, dest).start()

            @pl.when(dest == p)
            def _():
                keep_copy(k).start()
        return carry

    def pack_fire(n, carry):
        return fire(n, pack(n, carry))

    class Beside:
        def __init__(self, first):
            self.first = first

        def begin(self, b):
            chunk_copy(self.first + b).wait()

        def work(self, b):
            n = self.first + b
            k, dest = chunk_of(n)
            for m in range(6):
                bulk_out[dest * 3 + k, m] = packed(n, 2 * m, 2 * m + 1)

        def end(self, b):
            next_chunk(self.first + b)
            fire(self.first + b, 0)

    lax.fori_loop(0, 4, pack, 0)
    front_load.wait()

    @pl.when(p < 4)
    def _():
        def one(m, c):
            for h in range(2):
                front_out[m, :, h * 128 : h * 128 + 128] = front[
                    pl.ds(2 * m + h, BLOCK, stride=COL_BLOCKS), :
                ]
            owner, slot, copy = front_copy(m)

            @pl.when(owner != p)
            def _():
                copy.start()

            @pl.when(owner == p)
            def _():
                front_in[slot] = front_out[m]
            return c

        lax.fori_loop(0, 6, one, 0)

    def assemble(source, m, row):
        sides = []
        for h in range(2):
            total = jnp.zeros((BLOCK, BLOCK), F32)
            for pair_id in range(CHILDREN // 2):
                parts = []
                for g in (2 * pair_id, 2 * pair_id + 1):
                    place = jnp.broadcast_to(col_places[2 * m + h, g : g + 1, :], (HALF, 128))
                    taken = jnp.take_along_axis(
                        source(g), jnp.maximum(place, 0), axis=1, mode="promise_in_bounds"
                    )
                    parts.append(jnp.where(place >= 0, taken, 0.0))
                turned = jnp.concatenate(parts, axis=0).T
                order = jnp.broadcast_to(row_perms[row, pair_id : pair_id + 1, :], (BLOCK, BLOCK))
                total += jnp.take_along_axis(turned, order, axis=1, mode="promise_in_bounds")
            sides.append(total.T)
        return sides

    def cols_at(u):
        return cols.at[u // 4, pl.ds(pl.multiple_of(mod(u, 4) * 128, 128), 128), :]

    def cross_copy(u):
        return remote(
            cols_at(u), cols_at(u), cols_s.at[(u // 8) * 8], cols_r.at[u],
            mod(chip + 4, 8) * 2 + core, q,
        )

    def along_copy(u, dx):
        far = jnp.where(mod(u, 8) == chip, 0, 3)
        return remote(
            cols_at(u), cols_at(u), cols_s.at[(u // 8) * 8 + far + dx], cols_r.at[u],
            (ph * 4 + mod(chip + dx, 4)) * 2 + core, q,
        )

    def along(u):
        def send(dx, c):
            along_copy(u, dx).start()
            return c

        lax.fori_loop(1, 4, send, 0)

    def hand_copy(u):
        return remote(cols_at(u), cols_at(u), hand_s.at[u], cols_r.at[u], chip * 2 + 1 - core, q)

    def own_unit(slot, carry):
        u = slot * 8 + chip
        block = mod(u, 4)

        def landed(g, c):
            @pl.when(jnp.logical_or(core == 1, g != chip))
            def _():
                remote(
                    bulk_out.at[0, 0], unit_in.at[slot * 8 + g], unit_s.at[0],
                    unit_r.at[slot * 8 + g], g * 2, q,
                ).wait_recv()
            return c

        lax.fori_loop(0, 8, landed, 0)

        @pl.when(block != p)
        def _():
            remote(
                front_out.at[0], front_in.at[slot], front_s.at[0], front_r.at[slot], block, q
            ).wait_recv()

        sides = assemble(lambda g: unit_in[slot * 8 + g], u // 4, 6)
        cols[u // 4, pl.ds(pl.multiple_of(block * 128, 128), 128), :] = (
            jnp.concatenate(sides, axis=1) + front_in[slot]
        )

        cross_copy(u).start()
        along(u)
        hand_copy(u).start()
        return carry

    def spread_on(slot, carry):
        u = slot * 8 + mod(chip + 4, 8)
        cross_copy(u).wait_recv()
        along(u)
        hand_copy(u).start()
        return carry

    def hand_on(u, carry):
        @pl.when(mod(u - chip + 32, 4) != 0)
        def _():
            cross_copy(u).wait_recv()
            hand_copy(u).start()
        return carry

    def taken(u, carry):
        hand_copy(u).wait_recv()
        return carry

    first_slot = core
    last_slot = 1 + 2 * core

    marks_load.wait()
    ranks = lax.broadcasted_iota(jnp.int32, (HALF, 128), 0)
    spots = lax.broadcasted_iota(jnp.int32, (HALF, 128), 1)

    def places(block):
        at = pl.multiple_of((block // 2) * 128, 128)
        part = marks[:, pl.ds(at, 128)]
        mine = jnp.where(mod(block, 2) == 0, part, pltpu.roll(part, 64, 1)) - block * BLOCK
        tall = mine.T
        found = []
        for g in range(CHILDREN):
            hit = jnp.broadcast_to(tall[0:HALF, g : g + 1], (HALF, 128)) == spots
            found.append(jnp.max(jnp.where(hit, ranks, -1), axis=0, keepdims=True))
        return found

    def row_table(i, carry, block=None):
        found = places(i * 16 + p if block is None else block)
        for j in range(4):
            first, second = found[2 * j], found[2 * j + 1]
            row_perms[i, j : j + 1, :] = jnp.where(first >= 0, first, second + HALF)
        return carry


    def col_table(l, carry):
        found = places(l * 8 + q)
        for g in range(CHILDREN):
            col_places[l, g : g + 1, :] = jnp.where(
                found[g] >= 0, found[g] + mod(l, 2) * HALF, -1
            )
        return carry

    row_table(6, 0, mod(chip, 4))

    class Tables:
        def begin(self, b):
            pass

        def work(self, b):
            col_table(jnp.minimum(2 * b, 11), 0)
            col_table(jnp.minimum(2 * b + 1, 11), 0)
            row_table(jnp.minimum(b, 5), 0)

        def end(self, b):
            pass

    def unit_table(slot, carry):
        m = slot * 2 + chip // 4
        return col_table(2 * m + 1, col_table(2 * m, carry))

    lax.fori_loop(core, 1 + 2 * core, unit_table, 0)
    lax.fori_loop(first_slot, last_slot, own_unit, 0)
    lax.fori_loop(0, 4, fire, 0)
    lax.fori_loop(4, 8, pack_fire, 0)
    lax.fori_loop(first_slot, last_slot, spread_on, 0)
    lax.fori_loop(8, 10, pack_fire, 0)

    @pl.when(core == 0)
    def _():
        lax.fori_loop(0, 4, hand_on, 0)

    @pl.when(core == 1)
    def _():
        lax.fori_loop(0, 4, taken, 0)

    dz = remote(diag.at[y], diag.at[y], dz_s.at[0], dz_r.at[0], p, q_other)

    @pl.when(zl == 0)
    def _():
        diag[y] = cols[0, :, 0:128]
        dz.start()

    @pl.when(zl == 1)
    def _():
        dz.wait_recv()

    def dy(i):
        return remote(diag.at[y], diag.at[y], dy_s.at[i], dy_r.at[y], p, zl * 4 + mod(y + i, 4))

    for i in range(1, 4):
        dy(i).start()


    @pl.when(core == 0)
    def _():
        lax.fori_loop(4, 8, hand_on, 0)
        lax.fori_loop(8, 24, taken, 0)

    @pl.when(core == 1)
    def _():
        lax.fori_loop(8, 24, hand_on, 0)
        lax.fori_loop(4, 8, taken, 0)

    def r1(c):
        return remote(
            cols.at[:, pl.ds(c * 128, 128), pl.ds(pl.multiple_of(ph * 128, 128), 128)],
            rows.at[c], r1_s.at[c], r1_r.at[0], p, zl * 4 + c,
        )

    rz = remote(rows.at[y], rows.at[y], rz_s.at[0], rz_r.at[0], p, q_other)

    def ry(i):
        return remote(rows.at[y], rows.at[y], ry_s.at[i], ry_r.at[y], p, zl * 4 + mod(y + i, 4))

    @pl.when(own)
    def _():
        for c in range(4):
            @pl.when(y != c)
            def _():
                r1(c).start()

            @pl.when(y == c)
            def _():
                rows[c] = cols[:, c * 128 : c * 128 + 128, pl.ds(pl.multiple_of(ph * 128, 128), 128)]


    lax.fori_loop(10, 20, pack_fire, 0)

    holder = zl == pl8 // 4

    @pl.when(holder)
    def _():
        @pl.when(jnp.logical_not(own))
        def _():
            remote(
                rows.at[y], rows.at[y], r1_s.at[0], r1_r.at[0], p, q_other
            ).wait_recv()
        rz.start()

    lax.fori_loop(20, 32, pack_fire, 0)

    for i in range(1, 4):
        src = mod(y + i, 4)
        remote(diag.at[src], diag.at[src], dy_s.at[i], dy_r.at[src], p, q_other).wait_recv()

    for c in range(4):
        work[:, c * 128 : c * 128 + 128] = diag[c]
    full = work[:, 0:SPAN]
    work[:, 0:SPAN] = 0.5 * (full + full.T)
    work[:, SPAN:] = jnp.zeros((SPAN, SPAN), F32)

    lax.fori_loop(0, 8, relay_one, 0)
    factor_block(0, work, pair, Beside(32))

    @pl.when(jnp.logical_not(holder))
    def _():
        rz.wait_recv()

    for i in range(1, 4):
        ry(i).start()

    lax.fori_loop(8, 16, relay_one, 0)
    factor_block(1, work, pair, Beside(40))
    lax.fori_loop(16, 24, relay_one, 0)
    factor_block(2, work, pair, None)
    factor_block(3, work, pair, Tables())

    def sent_unit(slot, carry):
        u = slot * 8 + chip

        cross_copy(u).wait_send()

        def one(dx, c):
            along_copy(u, dx).wait_send()
            along_copy(slot * 8 + mod(chip + 4, 8), dx).wait_send()
            return c

        lax.fori_loop(1, 4, one, 0)
        hand_copy(u).wait_send()
        return carry

    lax.fori_loop(first_slot, last_slot, sent_unit, 0)

    def handed(u, carry):
        @pl.when(mod(u, 8) != chip)
        def _():
            hand_copy(u).wait_send()
        return carry

    @pl.when(core == 0)
    def _():
        lax.fori_loop(0, 8, handed, 0)

    @pl.when(core == 1)
    def _():
        lax.fori_loop(8, 24, handed, 0)

    @pl.when(zl == 0)
    def _():
        dz.wait_send()

    for i in range(1, 4):
        dy(i).wait_send()

    @pl.when(own)
    def _():
        for c in range(4):
            @pl.when(y != c)
            def _():
                r1(c).wait_send()

    @pl.when(holder)
    def _():
        rz.wait_send()

    for i in range(1, 4):
        ry(i).wait_send()

    for i in range(1, 4):
        src = mod(y + i, 4)
        remote(rows.at[src], rows.at[src], ry_s.at[i], ry_r.at[src], p, q_other).wait_recv()

    inverse_h, inverse_l = halves(work[:, SPAN:])
    inv_h[...] = inverse_h
    inv_l[...] = inverse_l

    def solve(block):
        high, low = halves(block)
        total = jnp.dot(inv_h[...], high, preferred_element_type=F32)
        total += jnp.dot(inv_h[...], low, preferred_element_type=F32)
        total += jnp.dot(inv_l[...], high, preferred_element_type=F32)
        return total

    def solve_rows(i, carry):
        parts = [
            jnp.concatenate([rows[c, 2 * i + h] for c in range(4)], axis=0) for h in range(2)
        ]
        turned = solve(jnp.concatenate(parts, axis=1)).T
        at = pl.multiple_of(i * 256, 256)
        high, low = halves(turned)
        rows_h[pl.ds(at, 256), :] = high
        rows_l[pl.ds(at, 256), :] = low
        for c in range(4):
            rows_f[c, pl.ds(at, 256), :] = turned[:, c * 128 : c * 128 + 128]
        return carry

    lax.fori_loop(0, 3, solve_rows, 0)

    def solve_cols(m, carry):
        solved = solve(cols[m])
        high, low = halves(solved)
        cols[m] = solved
        total = jnp.dot(rows_h[...], high, preferred_element_type=F32)
        total += jnp.dot(rows_h[...], low, preferred_element_type=F32)
        total += jnp.dot(rows_l[...], high, preferred_element_type=F32)
        prod[...] = total

        def less(kk, c):
            at = pl.multiple_of(kk * 128, 128)
            for h in range(2):
                where = pl.ds(kk * (128 * COL_BLOCKS) + 2 * m + h, BLOCK, stride=COL_BLOCKS)
                front[where, :] = (
                    front[where, :] - prod[pl.ds(at, 128), h * 128 : h * 128 + 128]
                )
            return c

        lax.fori_loop(0, 6, less, 0)
        return carry

    lax.fori_loop(0, 6, solve_cols, 0)

    def store(kk):
        at = pl.multiple_of(kk * (128 * COL_BLOCKS), 128 * COL_BLOCKS)
        span = pl.ds(at, 128 * COL_BLOCKS)
        return local(front.at[span], out.at[span], s_out.at[kk])

    @pl.when(p < 4)
    def _():
        for l in range(COL_BLOCKS):
            @pl.when(l * 8 + q > p)
            def _():
                front[pl.ds(l, BLOCK, stride=COL_BLOCKS), :] = cols[
                    l // 2, pl.ds(pl.multiple_of(p * 128, 128), 128),
                    (l % 2) * 128 : (l % 2) * 128 + 128,
                ]

    @pl.when(q < 4)
    def _():
        for kk in range(ROW_BLOCKS):
            @pl.when(kk * 16 + p > q)
            def _():
                front[pl.ds(kk * (128 * COL_BLOCKS), BLOCK, stride=COL_BLOCKS), :] = rows_f[
                    q, kk * 128 : kk * 128 + 128, :
                ]

        @pl.when(p == q)
        def _():
            tile = rows_f[q, 0:128, :]
            lower = lax.broadcasted_iota(jnp.int32, (128, 128), 0) >= lax.broadcasted_iota(
                jnp.int32, (128, 128), 1
            )
            front[pl.ds(0, BLOCK, stride=COL_BLOCKS), :] = jnp.where(lower, tile, tile.T)

    def arrived(kk):
        def landed(g, c):
            mine = jnp.logical_and(g == chip, mod(kk, 2) == core)

            @pl.when(jnp.logical_not(mine))
            def _():
                remote(
                    bulk_out.at[0], bulk_in.at[kk * 8 + g], bulk_s.at[0], bulk_r.at[kk * 8 + g],
                    g * 2 + mod(kk, 2), q,
                ).wait_recv()

            @pl.when(mine)
            def _():
                keep_copy(kk // 2).wait()
            return c

        lax.fori_loop(0, 8, landed, 0)

    def early(kk, carry):
        @pl.when(jnp.logical_not(panel_row(kk, p)))
        def _():
            arrived(kk)
            at = pl.multiple_of(kk * 8, 8)
            load = local(bulk_in.at[pl.ds(at, 8)], kids, kids_s.at[0])
            load.start()
            set_pick(pick, row_perms, kk)
            load.wait()

            def one(m, c):
                total = add_pair(m, col_places, lambda g: kids[g, m], pick, wide_buf)
                for h in range(2):
                    where = pl.ds(kk * (128 * COL_BLOCKS) + 2 * m + h, BLOCK, stride=COL_BLOCKS)
                    side = total[:, h * 128 : h * 128 + 128]
                    if h == 0:
                        side = jnp.where(jnp.logical_and(m == 0, q < 4), 0.0, side)
                    front[where, :] = front[where, :] + side
                return c

            lax.fori_loop(0, 6, one, 0)
        store(kk).start()
        return carry

    lax.fori_loop(EARLY, 6, lambda kk, c: (store(kk).start(), c)[1], 0)
    lax.fori_loop(0, EARLY, early, 0)
    lax.fori_loop(EARLY, 6, lambda kk, c: (arrived(kk), c)[1], 0)
    tables = [
        local(row_perms, row_out, tab_s.at[0]), local(col_places, col_out, tab_s.at[1])
    ]
    for copy in tables:
        copy.start()
    for copy in tables:
        copy.wait()

    def sent_bulk(n, carry):
        k, dest = chunk_of(n)

        @pl.when(jnp.logical_not(jnp.logical_or(dest == p, panel_row(2 * k + core, dest))))
        def _():
            bulk_copy(k, dest).wait_send()
        return carry

    lax.fori_loop(0, 48, sent_bulk, 0)

    @pl.when(core == 0)
    def _():
        def one(u, c):
            owner, copy = unit_copy(u)

            @pl.when(owner != p)
            def _():
                copy.wait_send()
            return c

        lax.fori_loop(0, 24, one, 0)

    @pl.when(p < 4)
    def _():
        def one(m, c):
            owner, slot, copy = front_copy(m)

            @pl.when(owner != p)
            def _():
                copy.wait_send()
            return c

        lax.fori_loop(0, 6, one, 0)

    def relayed(i, carry):
        k, way, cs = i // 8, mod(i, 8) // 2, mod(i, 2)
        dest, copy = second_copy(k, way, cs)

        @pl.when(jnp.logical_not(panel_row(2 * k + cs, dest)))
        def _():
            copy.wait_send()
        return carry

    lax.fori_loop(0, 24, relayed, 0)

    def stored(kk, carry):
        store(kk).wait()
        return carry

    lax.fori_loop(0, 6, stored, 0)


def set_pick(pick, row_perms, kk):
    level = lax.broadcasted_iota(jnp.int32, (128, 128), 1)
    for j in range(4):
        order = jnp.broadcast_to(row_perms[kk, j : j + 1, :], (128, 128)).T
        table = jnp.where(order == level, 1.0, 0.0).astype(BF16)
        pick[:, j * 128 : j * 128 + 128] = table
        pick[:, 512 + j * 128 : 640 + j * 128] = table


def add_pair(m, col_places, child_of, pick, wide_buf):
    for g in range(CHILDREN):
        for h in range(2):
            place = jnp.broadcast_to(col_places[2 * m + h, g : g + 1, :], (HALF, 128))
            taken = jnp.take_along_axis(
                child_of(g), jnp.maximum(place, 0), axis=1, mode="promise_in_bounds"
            )
            high, low = halves(jnp.where(place >= 0, taken, 0.0))
            wide_buf[g * 64 : g * 64 + 64, h * 128 : h * 128 + 128] = high
            wide_buf[512 + g * 64 : 576 + g * 64, h * 128 : h * 128 + 128] = low
    return jnp.dot(pick[...], wide_buf[...], preferred_element_type=F32)


EARLY = 4


def add_children(row_perms, col_places, front, children, out, pick, wide_buf):
    kk = mod(pl.program_id(0) + EARLY, ROW_BLOCKS)
    q = lax.axis_index("narrow")

    @pl.when(kk < EARLY)
    def _():
        out[...] = front[...]

    @pl.when(kk >= EARLY)
    def _():
        set_pick(pick, row_perms, kk)

        def one(m, carry):
            total = add_pair(m, col_places, lambda g: children[g, m], pick, wide_buf)
            for h in range(2):
                where = pl.ds(2 * m + h, BLOCK, stride=COL_BLOCKS)
                side = total[:, h * 128 : h * 128 + 128]
                if h == 0:
                    side = jnp.where(jnp.logical_and(m == 0, q < 4), 0.0, side)
                out[where, :] = front[where, :] + side
            return carry

        lax.fori_loop(0, 6, one, 0)


def body(root_front, child_update, child_map):
    child = child_update.reshape(3 * 16 * CHUNK, HALF)
    root = root_front.reshape(ROW_BLOCKS * BLOCK * COL_BLOCKS, BLOCK)
    vmem = lambda *shape: pltpu.VMEM(shape, F32)
    sems = lambda n: pltpu.SemaphoreType.DMA((n,))
    front, children, row_perms, col_places = pl.pallas_call(
        kernel,
        out_shape=[
            jax.ShapeDtypeStruct(root.shape, F32),
            jax.ShapeDtypeStruct((48, 6, HALF, 128), F32),
            jax.ShapeDtypeStruct((8, 4, 128), jnp.int32),
            jax.ShapeDtypeStruct((COL_BLOCKS, CHILDREN, 128), jnp.int32),
        ],
        in_specs=[pl.BlockSpec(memory_space=pl.ANY)] * 3,
        out_specs=[pl.BlockSpec(memory_space=pl.ANY)] * 4,
        scratch_shapes=[
            pltpu.VMEM((CHILDREN, 6144), jnp.int32),
            pltpu.VMEM((8, 4, 128), jnp.int32),
            pltpu.VMEM((COL_BLOCKS, CHILDREN, 128), jnp.int32),
            vmem(4 * CHUNK, HALF),
            vmem(ROW_BLOCKS * BLOCK * COL_BLOCKS, BLOCK),
            vmem(48, 6, HALF, 128),
            vmem(24, HALF, 128),
            vmem(6, BLOCK, 256),
            vmem(3, BLOCK, 256),
            vmem(6, SPAN, 256),
            vmem(4, SPAN, 128),
            vmem(4, 6, BLOCK, BLOCK),
            vmem(SPAN, 2 * SPAN),
            vmem(BLOCK, 2 * BLOCK),
            vmem(4, 768, BLOCK),
            pltpu.VMEM((768, SPAN), BF16),
            pltpu.VMEM((768, SPAN), BF16),
            vmem(768, 256),
            pltpu.VMEM((SPAN, SPAN), BF16),
            pltpu.VMEM((SPAN, SPAN), BF16),
            vmem(24, 6, HALF, 128),
            vmem(CHILDREN, 6, HALF, 128),
            pltpu.VMEM((BLOCK, 1024), BF16),
            pltpu.VMEM((1024, 256), BF16),
            sems(1), sems(3), sems(2), sems(1), sems(4), sems(1), sems(6), sems(24), sems(24), sems(48), sems(48), sems(24), sems(24),
            sems(6), sems(3), sems(24), sems(24), sems(24), sems(1), sems(1), sems(4), sems(4),
            sems(4), sems(1), sems(1), sems(1), sems(4), sems(4),
        ],
        compiler_params=pltpu.CompilerParams(
            collective_id=0, has_side_effects=True, vmem_limit_bytes=60 * 2**20
        ),
    )(child_map, child, root)
    part = pl.BlockSpec((BLOCK * COL_BLOCKS, BLOCK), lambda i: (mod(i + EARLY, ROW_BLOCKS), 0))
    out = pl.pallas_call(
        add_children,
        grid=(ROW_BLOCKS,),
        out_shape=jax.ShapeDtypeStruct(root.shape, F32),
        in_specs=[
            pl.BlockSpec((8, 4, 128), lambda i: (0, 0, 0)),
            pl.BlockSpec((COL_BLOCKS, CHILDREN, 128), lambda i: (0, 0, 0)),
            part,
            pl.BlockSpec(
                (CHILDREN, 6, HALF, 128),
                lambda i: (jnp.minimum(i + EARLY, ROW_BLOCKS - 1), 0, 0, 0),
            ),
        ],
        out_specs=part,
        scratch_shapes=[pltpu.VMEM((BLOCK, 1024), BF16), pltpu.VMEM((1024, 256), BF16)],
        compiler_params=pltpu.CompilerParams(vmem_limit_bytes=60 * 2**20),
    )(row_perms, col_places, front, children)
    return out.reshape(root_front.shape)


def solution(mesh):
    return jax.shard_map(
        body,
        mesh=mesh,
        in_specs=(
            P(None, "wide", None, None, "narrow", None),
            P("wide", None, None, None, None, "narrow", None),
            P(),
        ),
        out_specs=P(None, "wide", None, None, "narrow", None),
        check_vma=False,
    )
```

```python
import functools

import jax
import jax.numpy as jnp
from jax import lax
from jax.experimental import pallas as pl
from jax.experimental.pallas import tpu as pltpu
from jax.sharding import PartitionSpec as P

BLOCK = 128
HALF = 64
ROW_BLOCKS = 6
COL_BLOCKS = 12
CHILDREN = 8
N_WIDE = 16
N_NARROW = 8
SPAN = 512
CHUNK = HALF * COL_BLOCKS
MESH = pl.DeviceIdType.MESH
F32 = jnp.float32
BF16 = jnp.bfloat16


def mod(value, n):
    return lax.rem(value, n)


def shift_of(p, q):
    return p // 8 + (mod(p, 8) > q).astype(jnp.int32)


def halves(value):
    high = value.astype(BF16)
    low = (value - high.astype(F32)).astype(BF16)
    return high, low


def dot_full(a, b, dims):
    return lax.dot_general(
        a, b, (dims, ((), ())), precision=lax.Precision.HIGHEST, preferred_element_type=F32
    )


def thirds(value):
    high = value.astype(BF16).astype(F32)
    rest = value - high
    mid = rest.astype(BF16).astype(F32)
    low = rest - mid
    return high, mid, low


def factor_eight(cols):
    e = {}
    for a in range(8):
        for j in range(a + 1):
            e[a, j] = jnp.broadcast_to(cols[j][a : a + 1, :], (8, 128))
    inv = []
    low = {}
    for j in range(8):
        d = e[j, j]
        r = lax.rsqrt(d)
        r = r * (1.5 - 0.5 * d * r * r)
        inv.append(r)
        for a in range(j + 1, 8):
            low[a, j] = e[a, j] * r
        for a in range(j + 1, 8):
            for c in range(j + 1, a + 1):
                e[a, c] = e[a, c] - low[a, j] * low[c, j]
    return low, inv


def solve_eight(rows, low, inv):
    found = []
    for a in range(8):
        row = jnp.broadcast_to(rows[a : a + 1, :], (8, 128))
        for j in range(a):
            row = row - low[a, j] * found[j]
        found.append(row * inv[a])
    return found


def factor_128(pair, beside):
    lane = lax.broadcasted_iota(jnp.int32, (16, 128), 1)
    sub = lax.broadcasted_iota(jnp.int32, (8, 128), 0)

    def spread(value, j):
        return jnp.broadcast_to(value[:, j : j + 1], (8, 128))

    def gather_rows(found):
        total = found[0]
        for a in range(1, 8):
            total = jnp.where(sub == a, found[a], total)
        return total

    def step(b, carry):
        if beside is not None:
            beside.begin(b)
            beside.work(b)
        first = pl.multiple_of(b * 16, 16)
        rows = pair[pl.ds(first, 16), :]
        back = mod(128 - first, 128)
        top_a, top_b = rows[0:8, :128], rows[0:8, 128:]
        end_a, end_b = rows[8:16, :128], rows[8:16, 128:]
        top_t = pltpu.roll(top_a, back, 1)
        end_t = pltpu.roll(end_a, back, 1)
        low, inv = factor_eight([spread(top_t, j) for j in range(8)])
        ups_t = solve_eight(top_t, low, inv)
        ups_a = solve_eight(top_a, low, inv)
        ups_b = solve_eight(top_b, low, inv)
        link = []
        for a in range(8):
            value = spread(end_t, a)
            for j in range(a):
                value = value - link[j] * low[a, j]
            link.append(value * inv[a])
        for a in range(8):
            end_t = end_t - link[a] * ups_t[a]
            end_a = end_a - link[a] * ups_a[a]
            end_b = end_b - link[a] * ups_b[a]
        low, inv = factor_eight([spread(end_t, 8 + j) for j in range(8)])
        more_a = solve_eight(end_a, low, inv)
        more_b = solve_eight(end_b, low, inv)
        done_a = jnp.concatenate([gather_rows(ups_a), gather_rows(more_a)], axis=0)
        done_b = jnp.concatenate([gather_rows(ups_b), gather_rows(more_b)], axis=0)
        done = jnp.concatenate([done_a, done_b], axis=1)
        pair[pl.ds(first, 16), :] = done
        mult = jnp.where(lane >= first + 16, done_a, 0.0)
        mh, mm, ml = thirds(mult)
        uh, um, ul = thirds(done)
        left = jnp.concatenate([mh, mh, mm, mh, ml, mm], axis=0).astype(BF16)
        right = jnp.concatenate([uh, um, uh, ul, uh, um], axis=0).astype(BF16)
        gone = lax.dot_general(
            left, right, (((0,), (0,)), ((), ())), preferred_element_type=F32
        )
        pair[...] = pair[...] - gone
        if beside is not None:
            beside.end(b)
        return carry

    lax.fori_loop(0, 8, step, 0)


def factor_block(jb, work, pair, beside):
    at = jb * 128
    eye = (
        lax.broadcasted_iota(jnp.int32, (128, 128), 0)
        == lax.broadcasted_iota(jnp.int32, (128, 128), 1)
    ).astype(F32)
    pair[:, 0:128] = work[at : at + 128, at : at + 128]
    pair[:, 128:256] = eye
    factor_128(pair, beside)
    inverse = pair[:, 128:256]
    if jb:
        work[at : at + 128, SPAN : SPAN + at] = dot_full(
            inverse, work[at : at + 128, SPAN : SPAN + at], ((1,), (0,))
        )
    work[at : at + 128, SPAN + at : SPAN + at + 128] = inverse
    if jb < 3:
        rest = at + 128
        above = dot_full(inverse, work[at : at + 128, rest:SPAN], ((1,), (0,)))
        work[rest:SPAN, rest:SPAN] -= dot_full(above, above, ((0,), (0,)))
        work[rest:SPAN, SPAN : SPAN + rest] -= dot_full(
            above, work[at : at + 128, SPAN : SPAN + rest], ((0,), (0,))
        )


def kernel(
    child_map, child, root, out, bulk_in, row_out, col_out,
    marks, row_perms, col_places, chunk_buf, front, bulk_out, unit_in, front_out, front_in, cols, diag, rows, work,
    pair, rows_f, rows_h, rows_l, prod, inv_h, inv_l, relay, kids, pick, wide_buf,
    kids_s, keep_s, tab_s, s_marks, s_chunk, s_front, s_out, relay_s, relay_r, bulk_s, bulk_r, unit_s, unit_r, front_s, front_r,
    cols_s, cols_r, hand_s, dz_s, dz_r, dy_s, dy_r, r1_s, r1_r, rz_s, rz_r, ry_s, ry_r,
):
    p = lax.axis_index("wide")
    q = lax.axis_index("narrow")
    core = mod(p, 2)
    chip = p // 2
    ph = p // 8
    pl8 = mod(p, 8)
    zl = q // 4
    y = mod(q, 4)
    own = pl8 == q
    shift = shift_of(p, q)
    q_other = mod(q + 4, 8)

    def remote(src, dst, ssem, rsem, wide, narrow):
        return pltpu.make_async_remote_copy(
            src_ref=src, dst_ref=dst, send_sem=ssem, recv_sem=rsem,
            device_id=(wide, narrow), device_id_type=MESH,
        )

    def local(src, dst, sem):
        return pltpu.make_async_copy(src, dst, sem)

    def chunk_of(n):
        first = jnp.where(
            ph == 0,
            jnp.where(n < 12, 8 + mod(p + n, 8), 4 + mod(n, 4)),
            jnp.where(n < 8, 4 + mod(p + n, 4), 8 + mod(p + n, 8)),
        )
        first = jnp.where(n < 4, n, first)
        late = n - 16
        k = jnp.where(n < 16, 0, 1 + mod(late // 8, 2))
        side = jnp.where(n < 32, 1 - ph, ph)
        dest = jnp.where(n < 16, first, side * 8 + mod(p + n, 8))
        return k, dest

    def chunk_copy(n):
        k, dest = chunk_of(n)
        at = pl.multiple_of((k * 16 + dest) * CHUNK, CHUNK)
        slot = mod(n, 4)
        to = pl.multiple_of(slot * CHUNK, CHUNK)
        return local(child.at[pl.ds(at, CHUNK)], chunk_buf.at[pl.ds(to, CHUNK)], s_chunk.at[slot])

    for n in range(4):
        chunk_copy(jnp.int32(n)).start()
    marks_load = local(child_map, marks, s_marks.at[0])
    marks_load.start()
    front_load = local(root, front, s_front.at[0])
    front_load.start()

    barrier = pltpu.get_barrier_semaphore()

    def greet(wide, narrow):
        pl.semaphore_signal(barrier, inc=1, device_id=(wide, narrow), device_id_type=MESH)

    def greet_wide(i, carry):
        greet(mod(p + i, 16), q)
        return carry

    lax.fori_loop(1, 16, greet_wide, 0)
    for i in range(1, 4):
        greet(p, zl * 4 + mod(y + i, 4))


    def greet_plane(i, carry):
        greet(i, q_other)
        return carry

    lax.fori_loop(0, 16, greet_plane, 0)
    pl.semaphore_wait(barrier, 34)

    def packed(n, la, lb):
        base = mod(n, 4) * CHUNK
        xa = chunk_buf[pl.ds(base + la, HALF, stride=COL_BLOCKS), :]
        xb = chunk_buf[pl.ds(base + lb, HALF, stride=COL_BLOCKS), :]
        return jnp.concatenate([xa, xb], axis=1)

    def next_chunk(n):
        @pl.when(n + 4 < 48)
        def _():
            chunk_copy(n + 4).start()

    def unit_copy(u):
        slot = u // 8
        owner = mod(u, 8) * 2 + (slot > 0).astype(jnp.int32)
        return owner, remote(
            bulk_out.at[mod(u, 4) * 3, u // 4], unit_in.at[slot * 8 + chip], unit_s.at[u], unit_r.at[slot * 8 + chip],
            owner, q,
        )

    def front_copy(m):
        u = m * 4 + p
        slot = u // 8
        owner = mod(u, 8) * 2 + (slot > 0).astype(jnp.int32)
        return owner, slot, remote(
            front_out.at[m], front_in.at[slot], front_s.at[m], front_r.at[slot], owner, q
        )

    zh = ph
    xs = mod(chip, 4)

    def bulk_copy(k, dest):
        kk = 2 * k + core
        return remote(
            bulk_out.at[dest * 3 + k], bulk_in.at[kk * 8 + chip],
            bulk_s.at[dest * 3 + k], bulk_r.at[kk * 8 + chip], dest, q,
        )

    def keep_copy(k):
        return local(bulk_out.at[p * 3 + k], bulk_in.at[(2 * k + core) * 8 + chip], keep_s.at[k])

    def first_copy(k, dest):
        xd = mod(dest // 2, 4)
        far = mod(xd - xs + 6, 4) == 0
        xi = jnp.where(far, mod(xd + 1, 4), xd)
        gap = mod(xs - xi + 4, 4)
        way = jnp.where(far, 3, jnp.where(gap == 3, 2, gap))
        zi = jnp.where(mod(core + xs + k, 2) == 0, zh, 1 - zh)
        slot = k * 8 + way * 2 + core
        return remote(
            bulk_out.at[dest * 3 + k], relay.at[slot], bulk_s.at[dest * 3 + k],
            relay_r.at[slot], (zi * 4 + xi) * 2 + mod(dest, 2), q_other,
        )

    def second_copy(k, way, cs):
        slot = k * 8 + way * 2 + cs
        side = jnp.where(jnp.logical_or(way == 1, way == 3), 1, jnp.where(way == 2, 3, 0))
        source_x = mod(xs + side, 4)
        dest_x = jnp.where(way == 3, mod(xs + 3, 4), xs)
        source_z = jnp.where(mod(cs + source_x + k, 2) == 0, zh, 1 - zh)
        dest = ((1 - source_z) * 4 + dest_x) * 2 + core
        place = (2 * k + cs) * 8 + source_z * 4 + source_x
        return dest, remote(
            relay.at[slot], bulk_in.at[place], relay_s.at[slot], bulk_r.at[place], dest, q_other
        )

    def relay_one(i, carry):
        k, way, cs = i // 8, mod(i, 8) // 2, mod(i, 2)
        dest, copy = second_copy(k, way, cs)

        @pl.when(jnp.logical_not(panel_row(2 * k + cs, dest)))
        def _():
            remote(
                bulk_out.at[0], relay.at[i], bulk_s.at[0], relay_r.at[i], p, q_other
            ).wait_recv()
            copy.start()
        return carry

    def panel_row(kk, dest):
        return jnp.logical_and(kk == 0, dest < 4)

    def pack(n, carry):
        chunk_copy(n).wait()
        k, dest = chunk_of(n)

        def one(m, c):
            bulk_out[dest * 3 + k, m] = packed(n, 2 * m, 2 * m + 1)
            return c

        lax.fori_loop(0, 6, one, 0)

        @pl.when(panel_row(2 * k + core, dest))
        def _():
            def unit(m, c):
                u = m * 4 + dest
                owner, copy = unit_copy(u)

                @pl.when(owner != p)
                def _():
                    copy.start()

                @pl.when(owner == p)
                def _():
                    unit_in[(u // 8) * 8 + chip] = bulk_out[dest * 3, m]
                return c

            lax.fori_loop(0, 6, unit, 0)
        next_chunk(n)
        return carry

    def fire(n, carry):
        k, dest = chunk_of(n)

        @pl.when(jnp.logical_not(panel_row(2 * k + core, dest)))
        def _():
            crossing = dest // 8 != ph

            @pl.when(crossing)
            def _():
                first_copy(k, dest).start()

            @pl.when(jnp.logical_not(jnp.logical_or(crossing, dest == p)))
            def _():
                bulk_copy(k, dest).start()

            @pl.when(dest == p)
            def _():
                keep_copy(k).start()
        return carry

    def pack_fire(n, carry):
        return fire(n, pack(n, carry))

    class Beside:
        def __init__(self, first):
            self.first = first

        def begin(self, b):
            chunk_copy(self.first + b).wait()

        def work(self, b):
            n = self.first + b
            k, dest = chunk_of(n)
            for m in range(6):
                bulk_out[dest * 3 + k, m] = packed(n, 2 * m, 2 * m + 1)

        def end(self, b):
            next_chunk(self.first + b)
            fire(self.first + b, 0)

    lax.fori_loop(0, 4, pack, 0)
    front_load.wait()

    @pl.when(p < 4)
    def _():
        def one(m, c):
            for h in range(2):
                front_out[m, :, h * 128 : h * 128 + 128] = front[
                    pl.ds(2 * m + h, BLOCK, stride=COL_BLOCKS), :
                ]
            owner, slot, copy = front_copy(m)

            @pl.when(owner != p)
            def _():
                copy.start()

            @pl.when(owner == p)
            def _():
                front_in[slot] = front_out[m]
            return c

        lax.fori_loop(0, 6, one, 0)

    def assemble(source, m, row):
        sides = []
        for h in range(2):
            total = jnp.zeros((BLOCK, BLOCK), F32)
            for pair_id in range(CHILDREN // 2):
                parts = []
                for g in (2 * pair_id, 2 * pair_id + 1):
                    place = jnp.broadcast_to(col_places[2 * m + h, g : g + 1, :], (HALF, 128))
                    taken = jnp.take_along_axis(
                        source(g), jnp.maximum(place, 0), axis=1, mode="promise_in_bounds"
                    )
                    parts.append(jnp.where(place >= 0, taken, 0.0))
                turned = jnp.concatenate(parts, axis=0).T
                order = jnp.broadcast_to(row_perms[row, pair_id : pair_id + 1, :], (BLOCK, BLOCK))
                total += jnp.take_along_axis(turned, order, axis=1, mode="promise_in_bounds")
            sides.append(total.T)
        return sides

    def cols_at(u):
        return cols.at[u // 4, pl.ds(pl.multiple_of(mod(u, 4) * 128, 128), 128), :]

    def cross_copy(u):
        return remote(
            cols_at(u), cols_at(u), cols_s.at[(u // 8) * 8], cols_r.at[u],
            mod(chip + 4, 8) * 2 + core, q,
        )

    def along_copy(u, dx):
        far = jnp.where(mod(u, 8) == chip, 0, 3)
        return remote(
            cols_at(u), cols_at(u), cols_s.at[(u // 8) * 8 + far + dx], cols_r.at[u],
            (ph * 4 + mod(chip + dx, 4)) * 2 + core, q,
        )

    def along(u):
        def send(dx, c):
            along_copy(u, dx).start()
            return c

        lax.fori_loop(1, 4, send, 0)

    def hand_copy(u):
        return remote(cols_at(u), cols_at(u), hand_s.at[u], cols_r.at[u], chip * 2 + 1 - core, q)

    def own_unit(slot, carry):
        u = slot * 8 + chip
        block = mod(u, 4)

        def landed(g, c):
            @pl.when(jnp.logical_or(core == 1, g != chip))
            def _():
                remote(
                    bulk_out.at[0, 0], unit_in.at[slot * 8 + g], unit_s.at[0],
                    unit_r.at[slot * 8 + g], g * 2, q,
                ).wait_recv()
            return c

        lax.fori_loop(0, 8, landed, 0)

        @pl.when(block != p)
        def _():
            remote(
                front_out.at[0], front_in.at[slot], front_s.at[0], front_r.at[slot], block, q
            ).wait_recv()

        sides = assemble(lambda g: unit_in[slot * 8 + g], u // 4, 6)
        cols[u // 4, pl.ds(pl.multiple_of(block * 128, 128), 128), :] = (
            jnp.concatenate(sides, axis=1) + front_in[slot]
        )

        cross_copy(u).start()
        along(u)
        hand_copy(u).start()
        return carry

    def spread_on(slot, carry):
        u = slot * 8 + mod(chip + 4, 8)
        cross_copy(u).wait_recv()
        along(u)
        hand_copy(u).start()
        return carry

    def hand_on(u, carry):
        @pl.when(mod(u - chip + 32, 4) != 0)
        def _():
            cross_copy(u).wait_recv()
            hand_copy(u).start()
        return carry

    def taken(u, carry):
        hand_copy(u).wait_recv()
        return carry

    first_slot = core
    last_slot = 1 + 2 * core

    marks_load.wait()
    ranks = lax.broadcasted_iota(jnp.int32, (HALF, 128), 0)
    spots = lax.broadcasted_iota(jnp.int32, (HALF, 128), 1)

    def places(block):
        at = pl.multiple_of((block // 2) * 128, 128)
        part = marks[:, pl.ds(at, 128)]
        mine = jnp.where(mod(block, 2) == 0, part, pltpu.roll(part, 64, 1)) - block * BLOCK
        tall = mine.T
        found = []
        for g in range(CHILDREN):
            hit = jnp.broadcast_to(tall[0:HALF, g : g + 1], (HALF, 128)) == spots
            found.append(jnp.max(jnp.where(hit, ranks, -1), axis=0, keepdims=True))
        return found

    def row_table(i, carry, block=None):
        found = places(i * 16 + p if block is None else block)
        for j in range(4):
            first, second = found[2 * j], found[2 * j + 1]
            row_perms[i, j : j + 1, :] = jnp.where(first >= 0, first, second + HALF)
        return carry


    def col_table(l, carry):
        found = places(l * 8 + q)
        for g in range(CHILDREN):
            col_places[l, g : g + 1, :] = jnp.where(
                found[g] >= 0, found[g] + mod(l, 2) * HALF, -1
            )
        return carry

    row_table(6, 0, mod(chip, 4))

    class Tables:
        def begin(self, b):
            pass

        def work(self, b):
            col_table(jnp.minimum(2 * b, 11), 0)
            col_table(jnp.minimum(2 * b + 1, 11), 0)
            row_table(jnp.minimum(b, 5), 0)

        def end(self, b):
            pass

    def unit_table(slot, carry):
        m = slot * 2 + chip // 4
        return col_table(2 * m + 1, col_table(2 * m, carry))

    lax.fori_loop(core, 1 + 2 * core, unit_table, 0)
    lax.fori_loop(first_slot, last_slot, own_unit, 0)
    lax.fori_loop(0, 4, fire, 0)
    lax.fori_loop(4, 8, pack_fire, 0)
    lax.fori_loop(first_slot, last_slot, spread_on, 0)
    lax.fori_loop(8, 10, pack_fire, 0)

    @pl.when(core == 0)
    def _():
        lax.fori_loop(0, 4, hand_on, 0)

    @pl.when(core == 1)
    def _():
        lax.fori_loop(0, 4, taken, 0)

    dz = remote(diag.at[y], diag.at[y], dz_s.at[0], dz_r.at[0], p, q_other)

    @pl.when(zl == 0)
    def _():
        diag[y] = cols[0, :, 0:128]
        dz.start()

    @pl.when(zl == 1)
    def _():
        dz.wait_recv()

    def dy(i):
        return remote(diag.at[y], diag.at[y], dy_s.at[i], dy_r.at[y], p, zl * 4 + mod(y + i, 4))

    for i in range(1, 4):
        dy(i).start()


    @pl.when(core == 0)
    def _():
        lax.fori_loop(4, 8, hand_on, 0)
        lax.fori_loop(8, 24, taken, 0)

    @pl.when(core == 1)
    def _():
        lax.fori_loop(8, 24, hand_on, 0)
        lax.fori_loop(4, 8, taken, 0)

    def r1(c):
        return remote(
            cols.at[:, pl.ds(c * 128, 128), pl.ds(pl.multiple_of(ph * 128, 128), 128)],
            rows.at[c], r1_s.at[c], r1_r.at[0], p, zl * 4 + c,
        )

    rz = remote(rows.at[y], rows.at[y], rz_s.at[0], rz_r.at[0], p, q_other)

    def ry(i):
        return remote(rows.at[y], rows.at[y], ry_s.at[i], ry_r.at[y], p, zl * 4 + mod(y + i, 4))

    @pl.when(own)
    def _():
        for c in range(4):
            @pl.when(y != c)
            def _():
                r1(c).start()

            @pl.when(y == c)
            def _():
                rows[c] = cols[:, c * 128 : c * 128 + 128, pl.ds(pl.multiple_of(ph * 128, 128), 128)]


    lax.fori_loop(10, 20, pack_fire, 0)

    holder = zl == pl8 // 4

    @pl.when(holder)
    def _():
        @pl.when(jnp.logical_not(own))
        def _():
            remote(
                rows.at[y], rows.at[y], r1_s.at[0], r1_r.at[0], p, q_other
            ).wait_recv()
        rz.start()

    lax.fori_loop(20, 32, pack_fire, 0)
    lax.fori_loop(0, 8, relay_one, 0)

    for i in range(1, 4):
        src = mod(y + i, 4)
        remote(diag.at[src], diag.at[src], dy_s.at[i], dy_r.at[src], p, q_other).wait_recv()

    for c in range(4):
        work[:, c * 128 : c * 128 + 128] = diag[c]
    full = work[:, 0:SPAN]
    work[:, 0:SPAN] = 0.5 * (full + full.T)
    work[:, SPAN:] = jnp.zeros((SPAN, SPAN), F32)

    lax.fori_loop(8, 16, relay_one, 0)
    factor_block(0, work, pair, Beside(32))

    @pl.when(jnp.logical_not(holder))
    def _():
        rz.wait_recv()

    for i in range(1, 4):
        ry(i).start()

    lax.fori_loop(16, 24, relay_one, 0)
    factor_block(1, work, pair, Beside(40))
    factor_block(2, work, pair, None)
    factor_block(3, work, pair, Tables())

    def sent_unit(slot, carry):
        u = slot * 8 + chip

        cross_copy(u).wait_send()

        def one(dx, c):
            along_copy(u, dx).wait_send()
            along_copy(slot * 8 + mod(chip + 4, 8), dx).wait_send()
            return c

        lax.fori_loop(1, 4, one, 0)
        hand_copy(u).wait_send()
        return carry

    lax.fori_loop(first_slot, last_slot, sent_unit, 0)

    def handed(u, carry):
        @pl.when(mod(u, 8) != chip)
        def _():
            hand_copy(u).wait_send()
        return carry

    @pl.when(core == 0)
    def _():
        lax.fori_loop(0, 8, handed, 0)

    @pl.when(core == 1)
    def _():
        lax.fori_loop(8, 24, handed, 0)

    @pl.when(zl == 0)
    def _():
        dz.wait_send()

    for i in range(1, 4):
        dy(i).wait_send()

    @pl.when(own)
    def _():
        for c in range(4):
            @pl.when(y != c)
            def _():
                r1(c).wait_send()

    @pl.when(holder)
    def _():
        rz.wait_send()

    for i in range(1, 4):
        ry(i).wait_send()

    for i in range(1, 4):
        src = mod(y + i, 4)
        remote(rows.at[src], rows.at[src], ry_s.at[i], ry_r.at[src], p, q_other).wait_recv()

    inverse_h, inverse_l = halves(work[:, SPAN:])
    inv_h[...] = inverse_h
    inv_l[...] = inverse_l

    def solve(block):
        high, low = halves(block)
        total = jnp.dot(inv_h[...], high, preferred_element_type=F32)
        total += jnp.dot(inv_h[...], low, preferred_element_type=F32)
        total += jnp.dot(inv_l[...], high, preferred_element_type=F32)
        return total

    def solve_rows(i, carry):
        parts = [
            jnp.concatenate([rows[c, 2 * i + h] for c in range(4)], axis=0) for h in range(2)
        ]
        turned = solve(jnp.concatenate(parts, axis=1)).T
        at = pl.multiple_of(i * 256, 256)
        high, low = halves(turned)
        rows_h[pl.ds(at, 256), :] = high
        rows_l[pl.ds(at, 256), :] = low
        for c in range(4):
            rows_f[c, pl.ds(at, 256), :] = turned[:, c * 128 : c * 128 + 128]
        return carry

    lax.fori_loop(0, 3, solve_rows, 0)

    def solve_cols(m, carry):
        solved = solve(cols[m])
        high, low = halves(solved)
        cols[m] = solved
        total = jnp.dot(rows_h[...], high, preferred_element_type=F32)
        total += jnp.dot(rows_h[...], low, preferred_element_type=F32)
        total += jnp.dot(rows_l[...], high, preferred_element_type=F32)
        prod[...] = total

        def less(kk, c):
            at = pl.multiple_of(kk * 128, 128)
            for h in range(2):
                where = pl.ds(kk * (128 * COL_BLOCKS) + 2 * m + h, BLOCK, stride=COL_BLOCKS)
                front[where, :] = (
                    front[where, :] - prod[pl.ds(at, 128), h * 128 : h * 128 + 128]
                )
            return c

        lax.fori_loop(0, 6, less, 0)
        return carry

    lax.fori_loop(0, 6, solve_cols, 0)

    def store(kk):
        at = pl.multiple_of(kk * (128 * COL_BLOCKS), 128 * COL_BLOCKS)
        span = pl.ds(at, 128 * COL_BLOCKS)
        return local(front.at[span], out.at[span], s_out.at[kk])

    @pl.when(p < 4)
    def _():
        for l in range(COL_BLOCKS):
            @pl.when(l * 8 + q > p)
            def _():
                front[pl.ds(l, BLOCK, stride=COL_BLOCKS), :] = cols[
                    l // 2, pl.ds(pl.multiple_of(p * 128, 128), 128),
                    (l % 2) * 128 : (l % 2) * 128 + 128,
                ]

    @pl.when(q < 4)
    def _():
        for kk in range(ROW_BLOCKS):
            @pl.when(kk * 16 + p > q)
            def _():
                front[pl.ds(kk * (128 * COL_BLOCKS), BLOCK, stride=COL_BLOCKS), :] = rows_f[
                    q, kk * 128 : kk * 128 + 128, :
                ]

        @pl.when(p == q)
        def _():
            tile = rows_f[q, 0:128, :]
            lower = lax.broadcasted_iota(jnp.int32, (128, 128), 0) >= lax.broadcasted_iota(
                jnp.int32, (128, 128), 1
            )
            front[pl.ds(0, BLOCK, stride=COL_BLOCKS), :] = jnp.where(lower, tile, tile.T)

    def arrived(kk):
        def landed(g, c):
            mine = jnp.logical_and(g == chip, mod(kk, 2) == core)

            @pl.when(jnp.logical_not(mine))
            def _():
                remote(
                    bulk_out.at[0], bulk_in.at[kk * 8 + g], bulk_s.at[0], bulk_r.at[kk * 8 + g],
                    g * 2 + mod(kk, 2), q,
                ).wait_recv()

            @pl.when(mine)
            def _():
                keep_copy(kk // 2).wait()
            return c

        lax.fori_loop(0, 8, landed, 0)

    def early(kk, carry):
        @pl.when(jnp.logical_not(panel_row(kk, p)))
        def _():
            arrived(kk)
            at = pl.multiple_of(kk * 8, 8)
            load = local(bulk_in.at[pl.ds(at, 8)], kids, kids_s.at[0])
            load.start()
            set_pick(pick, row_perms, kk)
            load.wait()

            def one(m, c):
                total = add_pair(m, col_places, lambda g: kids[g, m], pick, wide_buf)
                for h in range(2):
                    where = pl.ds(kk * (128 * COL_BLOCKS) + 2 * m + h, BLOCK, stride=COL_BLOCKS)
                    side = total[:, h * 128 : h * 128 + 128]
                    if h == 0:
                        side = jnp.where(jnp.logical_and(m == 0, q < 4), 0.0, side)
                    front[where, :] = front[where, :] + side
                return c

            lax.fori_loop(0, 6, one, 0)
        store(kk).start()
        return carry

    lax.fori_loop(EARLY, 6, lambda kk, c: (store(kk).start(), c)[1], 0)
    lax.fori_loop(0, EARLY, early, 0)
    lax.fori_loop(EARLY, 6, lambda kk, c: (arrived(kk), c)[1], 0)
    tables = [
        local(row_perms, row_out, tab_s.at[0]), local(col_places, col_out, tab_s.at[1])
    ]
    for copy in tables:
        copy.start()
    for copy in tables:
        copy.wait()

    def sent_bulk(n, carry):
        k, dest = chunk_of(n)

        @pl.when(jnp.logical_not(jnp.logical_or(dest == p, panel_row(2 * k + core, dest))))
        def _():
            bulk_copy(k, dest).wait_send()
        return carry

    lax.fori_loop(0, 48, sent_bulk, 0)

    @pl.when(core == 0)
    def _():
        def one(u, c):
            owner, copy = unit_copy(u)

            @pl.when(owner != p)
            def _():
                copy.wait_send()
            return c

        lax.fori_loop(0, 24, one, 0)

    @pl.when(p < 4)
    def _():
        def one(m, c):
            owner, slot, copy = front_copy(m)

            @pl.when(owner != p)
            def _():
                copy.wait_send()
            return c

        lax.fori_loop(0, 6, one, 0)

    def relayed(i, carry):
        k, way, cs = i // 8, mod(i, 8) // 2, mod(i, 2)
        dest, copy = second_copy(k, way, cs)

        @pl.when(jnp.logical_not(panel_row(2 * k + cs, dest)))
        def _():
            copy.wait_send()
        return carry

    lax.fori_loop(0, 24, relayed, 0)

    def stored(kk, carry):
        store(kk).wait()
        return carry

    lax.fori_loop(0, 6, stored, 0)


def set_pick(pick, row_perms, kk):
    level = lax.broadcasted_iota(jnp.int32, (128, 128), 1)
    for j in range(4):
        order = jnp.broadcast_to(row_perms[kk, j : j + 1, :], (128, 128)).T
        table = jnp.where(order == level, 1.0, 0.0).astype(BF16)
        pick[:, j * 128 : j * 128 + 128] = table
        pick[:, 512 + j * 128 : 640 + j * 128] = table


def add_pair(m, col_places, child_of, pick, wide_buf):
    for g in range(CHILDREN):
        for h in range(2):
            place = jnp.broadcast_to(col_places[2 * m + h, g : g + 1, :], (HALF, 128))
            taken = jnp.take_along_axis(
                child_of(g), jnp.maximum(place, 0), axis=1, mode="promise_in_bounds"
            )
            high, low = halves(jnp.where(place >= 0, taken, 0.0))
            wide_buf[g * 64 : g * 64 + 64, h * 128 : h * 128 + 128] = high
            wide_buf[512 + g * 64 : 576 + g * 64, h * 128 : h * 128 + 128] = low
    return jnp.dot(pick[...], wide_buf[...], preferred_element_type=F32)


EARLY = 4


def add_children(row_perms, col_places, front, children, out, pick, wide_buf):
    kk = mod(pl.program_id(0) + EARLY, ROW_BLOCKS)
    q = lax.axis_index("narrow")

    @pl.when(kk < EARLY)
    def _():
        out[...] = front[...]

    @pl.when(kk >= EARLY)
    def _():
        set_pick(pick, row_perms, kk)

        def one(m, carry):
            total = add_pair(m, col_places, lambda g: children[g, m], pick, wide_buf)
            for h in range(2):
                where = pl.ds(2 * m + h, BLOCK, stride=COL_BLOCKS)
                side = total[:, h * 128 : h * 128 + 128]
                if h == 0:
                    side = jnp.where(jnp.logical_and(m == 0, q < 4), 0.0, side)
                out[where, :] = front[where, :] + side
            return carry

        lax.fori_loop(0, 6, one, 0)


def body(root_front, child_update, child_map):
    child = child_update.reshape(3 * 16 * CHUNK, HALF)
    root = root_front.reshape(ROW_BLOCKS * BLOCK * COL_BLOCKS, BLOCK)
    vmem = lambda *shape: pltpu.VMEM(shape, F32)
    sems = lambda n: pltpu.SemaphoreType.DMA((n,))
    front, children, row_perms, col_places = pl.pallas_call(
        kernel,
        out_shape=[
            jax.ShapeDtypeStruct(root.shape, F32),
            jax.ShapeDtypeStruct((48, 6, HALF, 128), F32),
            jax.ShapeDtypeStruct((8, 4, 128), jnp.int32),
            jax.ShapeDtypeStruct((COL_BLOCKS, CHILDREN, 128), jnp.int32),
        ],
        in_specs=[pl.BlockSpec(memory_space=pl.ANY)] * 3,
        out_specs=[pl.BlockSpec(memory_space=pl.ANY)] * 4,
        scratch_shapes=[
            pltpu.VMEM((CHILDREN, 6144), jnp.int32),
            pltpu.VMEM((8, 4, 128), jnp.int32),
            pltpu.VMEM((COL_BLOCKS, CHILDREN, 128), jnp.int32),
            vmem(4 * CHUNK, HALF),
            vmem(ROW_BLOCKS * BLOCK * COL_BLOCKS, BLOCK),
            vmem(48, 6, HALF, 128),
            vmem(24, HALF, 128),
            vmem(6, BLOCK, 256),
            vmem(3, BLOCK, 256),
            vmem(6, SPAN, 256),
            vmem(4, SPAN, 128),
            vmem(4, 6, BLOCK, BLOCK),
            vmem(SPAN, 2 * SPAN),
            vmem(BLOCK, 2 * BLOCK),
            vmem(4, 768, BLOCK),
            pltpu.VMEM((768, SPAN), BF16),
            pltpu.VMEM((768, SPAN), BF16),
            vmem(768, 256),
            pltpu.VMEM((SPAN, SPAN), BF16),
            pltpu.VMEM((SPAN, SPAN), BF16),
            vmem(24, 6, HALF, 128),
            vmem(CHILDREN, 6, HALF, 128),
            pltpu.VMEM((BLOCK, 1024), BF16),
            pltpu.VMEM((1024, 256), BF16),
            sems(1), sems(3), sems(2), sems(1), sems(4), sems(1), sems(6), sems(24), sems(24), sems(48), sems(48), sems(24), sems(24),
            sems(6), sems(3), sems(24), sems(24), sems(24), sems(1), sems(1), sems(4), sems(4),
            sems(4), sems(1), sems(1), sems(1), sems(4), sems(4),
        ],
        compiler_params=pltpu.CompilerParams(
            collective_id=0, has_side_effects=True, vmem_limit_bytes=60 * 2**20
        ),
    )(child_map, child, root)
    part = pl.BlockSpec((BLOCK * COL_BLOCKS, BLOCK), lambda i: (mod(i + EARLY, ROW_BLOCKS), 0))
    out = pl.pallas_call(
        add_children,
        grid=(ROW_BLOCKS,),
        out_shape=jax.ShapeDtypeStruct(root.shape, F32),
        in_specs=[
            pl.BlockSpec((8, 4, 128), lambda i: (0, 0, 0)),
            pl.BlockSpec((COL_BLOCKS, CHILDREN, 128), lambda i: (0, 0, 0)),
            part,
            pl.BlockSpec(
                (CHILDREN, 6, HALF, 128),
                lambda i: (jnp.minimum(i + EARLY, ROW_BLOCKS - 1), 0, 0, 0),
            ),
        ],
        out_specs=part,
        scratch_shapes=[pltpu.VMEM((BLOCK, 1024), BF16), pltpu.VMEM((1024, 256), BF16)],
        compiler_params=pltpu.CompilerParams(vmem_limit_bytes=60 * 2**20),
    )(row_perms, col_places, front, children)
    return out.reshape(root_front.shape)


def solution(mesh):
    return jax.shard_map(
        body,
        mesh=mesh,
        in_specs=(
            P(None, "wide", None, None, "narrow", None),
            P("wide", None, None, None, None, "narrow", None),
            P(),
        ),
        out_specs=P(None, "wide", None, None, "narrow", None),
        check_vma=False,
    )
```

```python
import functools

import jax
import jax.numpy as jnp
from jax import lax
from jax.experimental import pallas as pl
from jax.experimental.pallas import tpu as pltpu
from jax.sharding import PartitionSpec as P

BLOCK = 128
HALF = 64
ROW_BLOCKS = 6
COL_BLOCKS = 12
CHILDREN = 8
N_WIDE = 16
N_NARROW = 8
SPAN = 512
CHUNK = HALF * COL_BLOCKS
MESH = pl.DeviceIdType.MESH
F32 = jnp.float32
BF16 = jnp.bfloat16


def mod(value, n):
    return lax.rem(value, n)


def shift_of(p, q):
    return p // 8 + (mod(p, 8) > q).astype(jnp.int32)


def halves(value):
    high = value.astype(BF16)
    low = (value - high.astype(F32)).astype(BF16)
    return high, low


def dot_full(a, b, dims):
    return lax.dot_general(
        a, b, (dims, ((), ())), precision=lax.Precision.HIGHEST, preferred_element_type=F32
    )


def thirds(value):
    high = value.astype(BF16).astype(F32)
    rest = value - high
    mid = rest.astype(BF16).astype(F32)
    low = rest - mid
    return high, mid, low


def factor_eight(cols):
    e = {}
    for a in range(8):
        for j in range(a + 1):
            e[a, j] = jnp.broadcast_to(cols[j][a : a + 1, :], (8, 128))
    inv = []
    low = {}
    for j in range(8):
        d = e[j, j]
        r = lax.rsqrt(d)
        r = r * (1.5 - 0.5 * d * r * r)
        inv.append(r)
        for a in range(j + 1, 8):
            low[a, j] = e[a, j] * r
        for a in range(j + 1, 8):
            for c in range(j + 1, a + 1):
                e[a, c] = e[a, c] - low[a, j] * low[c, j]
    return low, inv


def solve_eight(rows, low, inv):
    found = []
    for a in range(8):
        row = jnp.broadcast_to(rows[a : a + 1, :], (8, 128))
        for j in range(a):
            row = row - low[a, j] * found[j]
        found.append(row * inv[a])
    return found


def factor_128(pair, beside):
    lane = lax.broadcasted_iota(jnp.int32, (16, 128), 1)
    sub = lax.broadcasted_iota(jnp.int32, (8, 128), 0)

    def spread(value, j):
        return jnp.broadcast_to(value[:, j : j + 1], (8, 128))

    def gather_rows(found):
        total = found[0]
        for a in range(1, 8):
            total = jnp.where(sub == a, found[a], total)
        return total

    def step(b, carry):
        if beside is not None:
            beside.begin(b)
            beside.work(b)
        first = pl.multiple_of(b * 16, 16)
        rows = pair[pl.ds(first, 16), :]
        back = mod(128 - first, 128)
        top_a, top_b = rows[0:8, :128], rows[0:8, 128:]
        end_a, end_b = rows[8:16, :128], rows[8:16, 128:]
        top_t = pltpu.roll(top_a, back, 1)
        end_t = pltpu.roll(end_a, back, 1)
        low, inv = factor_eight([spread(top_t, j) for j in range(8)])
        ups_t = solve_eight(top_t, low, inv)
        ups_a = solve_eight(top_a, low, inv)
        ups_b = solve_eight(top_b, low, inv)
        link = []
        for a in range(8):
            value = spread(end_t, a)
            for j in range(a):
                value = value - link[j] * low[a, j]
            link.append(value * inv[a])
        for a in range(8):
            end_t = end_t - link[a] * ups_t[a]
            end_a = end_a - link[a] * ups_a[a]
            end_b = end_b - link[a] * ups_b[a]
        low, inv = factor_eight([spread(end_t, 8 + j) for j in range(8)])
        more_a = solve_eight(end_a, low, inv)
        more_b = solve_eight(end_b, low, inv)
        done_a = jnp.concatenate([gather_rows(ups_a), gather_rows(more_a)], axis=0)
        done_b = jnp.concatenate([gather_rows(ups_b), gather_rows(more_b)], axis=0)
        done = jnp.concatenate([done_a, done_b], axis=1)
        pair[pl.ds(first, 16), :] = done
        mult = jnp.where(lane >= first + 16, done_a, 0.0)
        mh, mm, ml = thirds(mult)
        uh, um, ul = thirds(done)
        left = jnp.concatenate([mh, mh, mm, mh, ml, mm], axis=0).astype(BF16)
        right = jnp.concatenate([uh, um, uh, ul, uh, um], axis=0).astype(BF16)
        gone = lax.dot_general(
            left, right, (((0,), (0,)), ((), ())), preferred_element_type=F32
        )
        pair[...] = pair[...] - gone
        if beside is not None:
            beside.end(b)
        return carry

    lax.fori_loop(0, 8, step, 0)


def factor_block(jb, work, pair, beside):
    at = jb * 128
    eye = (
        lax.broadcasted_iota(jnp.int32, (128, 128), 0)
        == lax.broadcasted_iota(jnp.int32, (128, 128), 1)
    ).astype(F32)
    pair[:, 0:128] = work[at : at + 128, at : at + 128]
    pair[:, 128:256] = eye
    factor_128(pair, beside)
    inverse = pair[:, 128:256]
    if jb:
        work[at : at + 128, SPAN : SPAN + at] = dot_full(
            inverse, work[at : at + 128, SPAN : SPAN + at], ((1,), (0,))
        )
    work[at : at + 128, SPAN + at : SPAN + at + 128] = inverse
    if jb < 3:
        rest = at + 128
        above = dot_full(inverse, work[at : at + 128, rest:SPAN], ((1,), (0,)))
        work[rest:SPAN, rest:SPAN] -= dot_full(above, above, ((0,), (0,)))
        work[rest:SPAN, SPAN : SPAN + rest] -= dot_full(
            above, work[at : at + 128, SPAN : SPAN + rest], ((0,), (0,))
        )


def kernel(
    child_map, child, root, out, bulk_in, row_out, col_out,
    marks, row_perms, col_places, chunk_buf, front, bulk_out, unit_in, front_out, front_in, cols, diag, rows, work,
    pair, rows_f, rows_h, rows_l, prod, inv_h, inv_l, relay, kids, pick, wide_buf,
    kids_s, keep_s, tab_s, s_marks, s_chunk, s_front, s_out, relay_s, relay_r, bulk_s, bulk_r, unit_s, unit_r, front_s, front_r,
    cols_s, cols_r, hand_s, dz_s, dz_r, dy_s, dy_r, r1_s, r1_r, rz_s, rz_r, ry_s, ry_r,
):
    p = lax.axis_index("wide")
    q = lax.axis_index("narrow")
    core = mod(p, 2)
    chip = p // 2
    ph = p // 8
    pl8 = mod(p, 8)
    zl = q // 4
    y = mod(q, 4)
    own = pl8 == q
    shift = shift_of(p, q)
    q_other = mod(q + 4, 8)

    def remote(src, dst, ssem, rsem, wide, narrow):
        return pltpu.make_async_remote_copy(
            src_ref=src, dst_ref=dst, send_sem=ssem, recv_sem=rsem,
            device_id=(wide, narrow), device_id_type=MESH,
        )

    def local(src, dst, sem):
        return pltpu.make_async_copy(src, dst, sem)

    def chunk_of(n):
        first = jnp.where(
            ph == 0,
            jnp.where(n < 12, 8 + mod(p + n, 8), 4 + mod(n, 4)),
            jnp.where(n < 8, 4 + mod(p + n, 4), 8 + mod(p + n, 8)),
        )
        first = jnp.where(n < 4, n, first)
        late = n - 16
        k = jnp.where(n < 16, 0, 1 + mod(late // 8, 2))
        side = jnp.where(n < 32, 1 - ph, ph)
        dest = jnp.where(n < 16, first, side * 8 + mod(p + n, 8))
        return k, dest

    def chunk_copy(n):
        k, dest = chunk_of(n)
        at = pl.multiple_of((k * 16 + dest) * CHUNK, CHUNK)
        slot = mod(n, 4)
        to = pl.multiple_of(slot * CHUNK, CHUNK)
        return local(child.at[pl.ds(at, CHUNK)], chunk_buf.at[pl.ds(to, CHUNK)], s_chunk.at[slot])

    for n in range(4):
        chunk_copy(jnp.int32(n)).start()
    marks_load = local(child_map, marks, s_marks.at[0])
    marks_load.start()
    front_load = local(root, front, s_front.at[0])
    front_load.start()

    barrier = pltpu.get_barrier_semaphore()

    def greet(wide, narrow):
        pl.semaphore_signal(barrier, inc=1, device_id=(wide, narrow), device_id_type=MESH)

    def greet_wide(i, carry):
        greet(mod(p + i, 16), q)
        return carry

    lax.fori_loop(1, 16, greet_wide, 0)
    for i in range(1, 4):
        greet(p, zl * 4 + mod(y + i, 4))


    def greet_plane(i, carry):
        greet(i, q_other)
        return carry

    lax.fori_loop(0, 16, greet_plane, 0)
    pl.semaphore_wait(barrier, 34)

    def packed(n, la, lb):
        base = mod(n, 4) * CHUNK
        xa = chunk_buf[pl.ds(base + la, HALF, stride=COL_BLOCKS), :]
        xb = chunk_buf[pl.ds(base + lb, HALF, stride=COL_BLOCKS), :]
        return jnp.concatenate([xa, xb], axis=1)

    def next_chunk(n):
        @pl.when(n + 4 < 48)
        def _():
            chunk_copy(n + 4).start()

    def unit_copy(u):
        slot = u // 8
        owner = mod(u, 8) * 2 + (slot > 0).astype(jnp.int32)
        return owner, remote(
            bulk_out.at[mod(u, 4) * 3, u // 4], unit_in.at[slot * 8 + chip], unit_s.at[u], unit_r.at[slot * 8 + chip],
            owner, q,
        )

    def front_copy(m):
        u = m * 4 + p
        slot = u // 8
        owner = mod(u, 8) * 2 + (slot > 0).astype(jnp.int32)
        return owner, slot, remote(
            front_out.at[m], front_in.at[slot], front_s.at[m], front_r.at[slot], owner, q
        )

    zh = ph
    xs = mod(chip, 4)

    def bulk_copy(k, dest):
        kk = 2 * k + core
        return remote(
            bulk_out.at[dest * 3 + k], bulk_in.at[kk * 8 + chip],
            bulk_s.at[dest * 3 + k], bulk_r.at[kk * 8 + chip], dest, q,
        )

    def keep_copy(k):
        return local(bulk_out.at[p * 3 + k], bulk_in.at[(2 * k + core) * 8 + chip], keep_s.at[k])

    def first_copy(k, dest):
        xd = mod(dest // 2, 4)
        far = mod(xd - xs + 6, 4) == 0
        xi = jnp.where(far, mod(xd + 1, 4), xd)
        gap = mod(xs - xi + 4, 4)
        way = jnp.where(far, 3, jnp.where(gap == 3, 2, gap))
        zi = jnp.where(mod(core + xs + k, 2) == 0, zh, 1 - zh)
        slot = k * 8 + way * 2 + core
        return remote(
            bulk_out.at[dest * 3 + k], relay.at[slot], bulk_s.at[dest * 3 + k],
            relay_r.at[slot], (zi * 4 + xi) * 2 + mod(dest, 2), q_other,
        )

    def second_copy(k, way, cs):
        slot = k * 8 + way * 2 + cs
        side = jnp.where(jnp.logical_or(way == 1, way == 3), 1, jnp.where(way == 2, 3, 0))
        source_x = mod(xs + side, 4)
        dest_x = jnp.where(way == 3, mod(xs + 3, 4), xs)
        source_z = jnp.where(mod(cs + source_x + k, 2) == 0, zh, 1 - zh)
        dest = ((1 - source_z) * 4 + dest_x) * 2 + core
        place = (2 * k + cs) * 8 + source_z * 4 + source_x
        return dest, remote(
            relay.at[slot], bulk_in.at[place], relay_s.at[slot], bulk_r.at[place], dest, q_other
        )

    def relay_one(i, carry):
        k, way, cs = i // 8, mod(i, 8) // 2, mod(i, 2)
        dest, copy = second_copy(k, way, cs)

        @pl.when(jnp.logical_not(panel_row(2 * k + cs, dest)))
        def _():
            remote(
                bulk_out.at[0], relay.at[i], bulk_s.at[0], relay_r.at[i], p, q_other
            ).wait_recv()
            copy.start()
        return carry

    def panel_row(kk, dest):
        return jnp.logical_and(kk == 0, dest < 4)

    def pack(n, carry):
        chunk_copy(n).wait()
        k, dest = chunk_of(n)

        def one(m, c):
            bulk_out[dest * 3 + k, m] = packed(n, 2 * m, 2 * m + 1)
            return c

        lax.fori_loop(0, 6, one, 0)

        @pl.when(panel_row(2 * k + core, dest))
        def _():
            def unit(m, c):
                u = m * 4 + dest
                owner, copy = unit_copy(u)

                @pl.when(owner != p)
                def _():
                    copy.start()

                @pl.when(owner == p)
                def _():
                    unit_in[(u // 8) * 8 + chip] = bulk_out[dest * 3, m]
                return c

            lax.fori_loop(0, 6, unit, 0)
        next_chunk(n)
        return carry

    def fire(n, carry):
        k, dest = chunk_of(n)

        @pl.when(jnp.logical_not(panel_row(2 * k + core, dest)))
        def _():
            crossing = dest // 8 != ph

            @pl.when(crossing)
            def _():
                first_copy(k, dest).start()

            @pl.when(jnp.logical_not(jnp.logical_or(crossing, dest == p)))
            def _():
                bulk_copy(k, dest).start()

            @pl.when(dest == p)
            def _():
                keep_copy(k).start()
        return carry

    def pack_fire(n, carry):
        return fire(n, pack(n, carry))

    class Beside:
        def __init__(self, first):
            self.first = first

        def begin(self, b):
            chunk_copy(self.first + b).wait()

        def work(self, b):
            n = self.first + b
            k, dest = chunk_of(n)
            for m in range(6):
                bulk_out[dest * 3 + k, m] = packed(n, 2 * m, 2 * m + 1)

        def end(self, b):
            next_chunk(self.first + b)
            fire(self.first + b, 0)

    lax.fori_loop(0, 4, pack, 0)
    front_load.wait()

    @pl.when(p < 4)
    def _():
        def one(m, c):
            for h in range(2):
                front_out[m, :, h * 128 : h * 128 + 128] = front[
                    pl.ds(2 * m + h, BLOCK, stride=COL_BLOCKS), :
                ]
            owner, slot, copy = front_copy(m)

            @pl.when(owner != p)
            def _():
                copy.start()

            @pl.when(owner == p)
            def _():
                front_in[slot] = front_out[m]
            return c

        lax.fori_loop(0, 6, one, 0)

    def assemble(source, m, row):
        sides = []
        for h in range(2):
            total = jnp.zeros((BLOCK, BLOCK), F32)
            for pair_id in range(CHILDREN // 2):
                parts = []
                for g in (2 * pair_id, 2 * pair_id + 1):
                    place = jnp.broadcast_to(col_places[2 * m + h, g : g + 1, :], (HALF, 128))
                    taken = jnp.take_along_axis(
                        source(g), jnp.maximum(place, 0), axis=1, mode="promise_in_bounds"
                    )
                    parts.append(jnp.where(place >= 0, taken, 0.0))
                turned = jnp.concatenate(parts, axis=0).T
                order = jnp.broadcast_to(row_perms[row, pair_id : pair_id + 1, :], (BLOCK, BLOCK))
                total += jnp.take_along_axis(turned, order, axis=1, mode="promise_in_bounds")
            sides.append(total.T)
        return sides

    def cols_at(u):
        return cols.at[u // 4, pl.ds(pl.multiple_of(mod(u, 4) * 128, 128), 128), :]

    def cross_copy(u):
        return remote(
            cols_at(u), cols_at(u), cols_s.at[(u // 8) * 8], cols_r.at[u],
            mod(chip + 4, 8) * 2 + core, q,
        )

    def along_copy(u, dx):
        far = jnp.where(mod(u, 8) == chip, 0, 3)
        return remote(
            cols_at(u), cols_at(u), cols_s.at[(u // 8) * 8 + far + dx], cols_r.at[u],
            (ph * 4 + mod(chip + dx, 4)) * 2 + core, q,
        )

    def along(u):
        def send(dx, c):
            along_copy(u, dx).start()
            return c

        lax.fori_loop(1, 4, send, 0)

    def hand_copy(u):
        return remote(cols_at(u), cols_at(u), hand_s.at[u], cols_r.at[u], chip * 2 + 1 - core, q)

    def own_unit(slot, carry):
        u = slot * 8 + chip
        block = mod(u, 4)

        def landed(g, c):
            @pl.when(jnp.logical_or(core == 1, g != chip))
            def _():
                remote(
                    bulk_out.at[0, 0], unit_in.at[slot * 8 + g], unit_s.at[0],
                    unit_r.at[slot * 8 + g], g * 2, q,
                ).wait_recv()
            return c

        lax.fori_loop(0, 8, landed, 0)

        @pl.when(block != p)
        def _():
            remote(
                front_out.at[0], front_in.at[slot], front_s.at[0], front_r.at[slot], block, q
            ).wait_recv()

        sides = assemble(lambda g: unit_in[slot * 8 + g], u // 4, 6)
        cols[u // 4, pl.ds(pl.multiple_of(block * 128, 128), 128), :] = (
            jnp.concatenate(sides, axis=1) + front_in[slot]
        )

        cross_copy(u).start()
        along(u)
        hand_copy(u).start()
        return carry

    def spread_on(slot, carry):
        u = slot * 8 + mod(chip + 4, 8)
        cross_copy(u).wait_recv()
        along(u)
        hand_copy(u).start()
        return carry

    def hand_on(u, carry):
        @pl.when(mod(u - chip + 32, 4) != 0)
        def _():
            cross_copy(u).wait_recv()
            hand_copy(u).start()
        return carry

    def taken(u, carry):
        hand_copy(u).wait_recv()
        return carry

    first_slot = core
    last_slot = 1 + 2 * core

    marks_load.wait()
    ranks = lax.broadcasted_iota(jnp.int32, (HALF, 128), 0)
    spots = lax.broadcasted_iota(jnp.int32, (HALF, 128), 1)

    def places(block):
        at = pl.multiple_of((block // 2) * 128, 128)
        part = marks[:, pl.ds(at, 128)]
        mine = jnp.where(mod(block, 2) == 0, part, pltpu.roll(part, 64, 1)) - block * BLOCK
        tall = mine.T
        found = []
        for g in range(CHILDREN):
            hit = jnp.broadcast_to(tall[0:HALF, g : g + 1], (HALF, 128)) == spots
            found.append(jnp.max(jnp.where(hit, ranks, -1), axis=0, keepdims=True))
        return found

    def row_table(i, carry, block=None):
        found = places(i * 16 + p if block is None else block)
        for j in range(4):
            first, second = found[2 * j], found[2 * j + 1]
            row_perms[i, j : j + 1, :] = jnp.where(first >= 0, first, second + HALF)
        return carry


    def col_table(l, carry):
        found = places(l * 8 + q)
        for g in range(CHILDREN):
            col_places[l, g : g + 1, :] = jnp.where(
                found[g] >= 0, found[g] + mod(l, 2) * HALF, -1
            )
        return carry

    row_table(6, 0, mod(chip, 4))

    class Tables:
        def begin(self, b):
            pass

        def work(self, b):
            col_table(jnp.minimum(2 * b, 11), 0)
            col_table(jnp.minimum(2 * b + 1, 11), 0)
            row_table(jnp.minimum(b, 5), 0)

        def end(self, b):
            pass

    def unit_table(slot, carry):
        m = slot * 2 + chip // 4
        return col_table(2 * m + 1, col_table(2 * m, carry))

    lax.fori_loop(core, 1 + 2 * core, unit_table, 0)
    lax.fori_loop(first_slot, last_slot, own_unit, 0)
    lax.fori_loop(4, 8, pack, 0)
    lax.fori_loop(first_slot, last_slot, spread_on, 0)
    lax.fori_loop(8, 10, pack, 0)

    @pl.when(core == 0)
    def _():
        lax.fori_loop(0, 4, hand_on, 0)

    @pl.when(core == 1)
    def _():
        lax.fori_loop(0, 4, taken, 0)

    dz = remote(diag.at[y], diag.at[y], dz_s.at[0], dz_r.at[0], p, q_other)

    @pl.when(zl == 0)
    def _():
        diag[y] = cols[0, :, 0:128]
        dz.start()

    @pl.when(zl == 1)
    def _():
        dz.wait_recv()

    def dy(i):
        return remote(diag.at[y], diag.at[y], dy_s.at[i], dy_r.at[y], p, zl * 4 + mod(y + i, 4))

    for i in range(1, 4):
        dy(i).start()


    @pl.when(core == 0)
    def _():
        lax.fori_loop(4, 8, hand_on, 0)
        lax.fori_loop(8, 24, taken, 0)

    @pl.when(core == 1)
    def _():
        lax.fori_loop(8, 24, hand_on, 0)
        lax.fori_loop(4, 8, taken, 0)

    def r1(c):
        return remote(
            cols.at[:, pl.ds(c * 128, 128), pl.ds(pl.multiple_of(ph * 128, 128), 128)],
            rows.at[c], r1_s.at[c], r1_r.at[0], p, zl * 4 + c,
        )

    rz = remote(rows.at[y], rows.at[y], rz_s.at[0], rz_r.at[0], p, q_other)

    def ry(i):
        return remote(rows.at[y], rows.at[y], ry_s.at[i], ry_r.at[y], p, zl * 4 + mod(y + i, 4))

    @pl.when(own)
    def _():
        for c in range(4):
            @pl.when(y != c)
            def _():
                r1(c).start()

            @pl.when(y == c)
            def _():
                rows[c] = cols[:, c * 128 : c * 128 + 128, pl.ds(pl.multiple_of(ph * 128, 128), 128)]


    lax.fori_loop(0, 8, fire, 0)
    lax.fori_loop(10, 20, pack, 0)

    holder = zl == pl8 // 4

    @pl.when(holder)
    def _():
        @pl.when(jnp.logical_not(own))
        def _():
            remote(
                rows.at[y], rows.at[y], r1_s.at[0], r1_r.at[0], p, q_other
            ).wait_recv()
        rz.start()

    lax.fori_loop(8, 12, fire, 0)
    lax.fori_loop(20, 26, pack, 0)

    @pl.when(jnp.logical_not(holder))
    def _():
        rz.wait_recv()

    for i in range(1, 4):
        ry(i).start()

    lax.fori_loop(12, 26, fire, 0)
    lax.fori_loop(26, 32, pack_fire, 0)

    for i in range(1, 4):
        src = mod(y + i, 4)
        remote(diag.at[src], diag.at[src], dy_s.at[i], dy_r.at[src], p, q_other).wait_recv()

    for c in range(4):
        work[:, c * 128 : c * 128 + 128] = diag[c]
    full = work[:, 0:SPAN]
    work[:, 0:SPAN] = 0.5 * (full + full.T)
    work[:, SPAN:] = jnp.zeros((SPAN, SPAN), F32)

    lax.fori_loop(0, 8, relay_one, 0)
    factor_block(0, work, pair, Beside(32))

    lax.fori_loop(8, 16, relay_one, 0)
    factor_block(1, work, pair, Beside(40))
    lax.fori_loop(16, 24, relay_one, 0)
    factor_block(2, work, pair, None)
    factor_block(3, work, pair, Tables())

    def sent_unit(slot, carry):
        u = slot * 8 + chip

        cross_copy(u).wait_send()

        def one(dx, c):
            along_copy(u, dx).wait_send()
            along_copy(slot * 8 + mod(chip + 4, 8), dx).wait_send()
            return c

        lax.fori_loop(1, 4, one, 0)
        hand_copy(u).wait_send()
        return carry

    lax.fori_loop(first_slot, last_slot, sent_unit, 0)

    def handed(u, carry):
        @pl.when(mod(u, 8) != chip)
        def _():
            hand_copy(u).wait_send()
        return carry

    @pl.when(core == 0)
    def _():
        lax.fori_loop(0, 8, handed, 0)

    @pl.when(core == 1)
    def _():
        lax.fori_loop(8, 24, handed, 0)

    @pl.when(zl == 0)
    def _():
        dz.wait_send()

    for i in range(1, 4):
        dy(i).wait_send()

    @pl.when(own)
    def _():
        for c in range(4):
            @pl.when(y != c)
            def _():
                r1(c).wait_send()

    @pl.when(holder)
    def _():
        rz.wait_send()

    for i in range(1, 4):
        ry(i).wait_send()

    for i in range(1, 4):
        src = mod(y + i, 4)
        remote(rows.at[src], rows.at[src], ry_s.at[i], ry_r.at[src], p, q_other).wait_recv()

    inverse_h, inverse_l = halves(work[:, SPAN:])
    inv_h[...] = inverse_h
    inv_l[...] = inverse_l

    def solve(block):
        high, low = halves(block)
        total = jnp.dot(inv_h[...], high, preferred_element_type=F32)
        total += jnp.dot(inv_h[...], low, preferred_element_type=F32)
        total += jnp.dot(inv_l[...], high, preferred_element_type=F32)
        return total

    def solve_rows(i, carry):
        parts = [
            jnp.concatenate([rows[c, 2 * i + h] for c in range(4)], axis=0) for h in range(2)
        ]
        turned = solve(jnp.concatenate(parts, axis=1)).T
        at = pl.multiple_of(i * 256, 256)
        high, low = halves(turned)
        rows_h[pl.ds(at, 256), :] = high
        rows_l[pl.ds(at, 256), :] = low
        for c in range(4):
            rows_f[c, pl.ds(at, 256), :] = turned[:, c * 128 : c * 128 + 128]
        return carry

    lax.fori_loop(0, 3, solve_rows, 0)

    def solve_cols(m, carry):
        solved = solve(cols[m])
        high, low = halves(solved)
        cols[m] = solved
        total = jnp.dot(rows_h[...], high, preferred_element_type=F32)
        total += jnp.dot(rows_h[...], low, preferred_element_type=F32)
        total += jnp.dot(rows_l[...], high, preferred_element_type=F32)
        prod[...] = total

        def less(kk, c):
            at = pl.multiple_of(kk * 128, 128)
            for h in range(2):
                where = pl.ds(kk * (128 * COL_BLOCKS) + 2 * m + h, BLOCK, stride=COL_BLOCKS)
                front[where, :] = (
                    front[where, :] - prod[pl.ds(at, 128), h * 128 : h * 128 + 128]
                )
            return c

        lax.fori_loop(0, 6, less, 0)
        return carry

    lax.fori_loop(0, 6, solve_cols, 0)

    def store(kk):
        at = pl.multiple_of(kk * (128 * COL_BLOCKS), 128 * COL_BLOCKS)
        span = pl.ds(at, 128 * COL_BLOCKS)
        return local(front.at[span], out.at[span], s_out.at[kk])

    @pl.when(p < 4)
    def _():
        for l in range(COL_BLOCKS):
            @pl.when(l * 8 + q > p)
            def _():
                front[pl.ds(l, BLOCK, stride=COL_BLOCKS), :] = cols[
                    l // 2, pl.ds(pl.multiple_of(p * 128, 128), 128),
                    (l % 2) * 128 : (l % 2) * 128 + 128,
                ]

    @pl.when(q < 4)
    def _():
        for kk in range(ROW_BLOCKS):
            @pl.when(kk * 16 + p > q)
            def _():
                front[pl.ds(kk * (128 * COL_BLOCKS), BLOCK, stride=COL_BLOCKS), :] = rows_f[
                    q, kk * 128 : kk * 128 + 128, :
                ]

        @pl.when(p == q)
        def _():
            tile = rows_f[q, 0:128, :]
            lower = lax.broadcasted_iota(jnp.int32, (128, 128), 0) >= lax.broadcasted_iota(
                jnp.int32, (128, 128), 1
            )
            front[pl.ds(0, BLOCK, stride=COL_BLOCKS), :] = jnp.where(lower, tile, tile.T)

    def arrived(kk):
        def landed(g, c):
            mine = jnp.logical_and(g == chip, mod(kk, 2) == core)

            @pl.when(jnp.logical_not(mine))
            def _():
                remote(
                    bulk_out.at[0], bulk_in.at[kk * 8 + g], bulk_s.at[0], bulk_r.at[kk * 8 + g],
                    g * 2 + mod(kk, 2), q,
                ).wait_recv()

            @pl.when(mine)
            def _():
                keep_copy(kk // 2).wait()
            return c

        lax.fori_loop(0, 8, landed, 0)

    def early(kk, carry):
        @pl.when(jnp.logical_not(panel_row(kk, p)))
        def _():
            arrived(kk)
            at = pl.multiple_of(kk * 8, 8)
            load = local(bulk_in.at[pl.ds(at, 8)], kids, kids_s.at[0])
            load.start()
            set_pick(pick, row_perms, kk)
            load.wait()

            def one(m, c):
                total = add_pair(m, col_places, lambda g: kids[g, m], pick, wide_buf)
                for h in range(2):
                    where = pl.ds(kk * (128 * COL_BLOCKS) + 2 * m + h, BLOCK, stride=COL_BLOCKS)
                    side = total[:, h * 128 : h * 128 + 128]
                    if h == 0:
                        side = jnp.where(jnp.logical_and(m == 0, q < 4), 0.0, side)
                    front[where, :] = front[where, :] + side
                return c

            lax.fori_loop(0, 6, one, 0)
        store(kk).start()
        return carry

    lax.fori_loop(EARLY, 6, lambda kk, c: (store(kk).start(), c)[1], 0)
    lax.fori_loop(0, EARLY, early, 0)
    lax.fori_loop(EARLY, 6, lambda kk, c: (arrived(kk), c)[1], 0)
    tables = [
        local(row_perms, row_out, tab_s.at[0]), local(col_places, col_out, tab_s.at[1])
    ]
    for copy in tables:
        copy.start()
    for copy in tables:
        copy.wait()

    def sent_bulk(n, carry):
        k, dest = chunk_of(n)

        @pl.when(jnp.logical_not(jnp.logical_or(dest == p, panel_row(2 * k + core, dest))))
        def _():
            bulk_copy(k, dest).wait_send()
        return carry

    lax.fori_loop(0, 48, sent_bulk, 0)

    @pl.when(core == 0)
    def _():
        def one(u, c):
            owner, copy = unit_copy(u)

            @pl.when(owner != p)
            def _():
                copy.wait_send()
            return c

        lax.fori_loop(0, 24, one, 0)

    @pl.when(p < 4)
    def _():
        def one(m, c):
            owner, slot, copy = front_copy(m)

            @pl.when(owner != p)
            def _():
                copy.wait_send()
            return c

        lax.fori_loop(0, 6, one, 0)

    def relayed(i, carry):
        k, way, cs = i // 8, mod(i, 8) // 2, mod(i, 2)
        dest, copy = second_copy(k, way, cs)

        @pl.when(jnp.logical_not(panel_row(2 * k + cs, dest)))
        def _():
            copy.wait_send()
        return carry

    lax.fori_loop(0, 24, relayed, 0)

    def stored(kk, carry):
        store(kk).wait()
        return carry

    lax.fori_loop(0, 6, stored, 0)


def set_pick(pick, row_perms, kk):
    level = lax.broadcasted_iota(jnp.int32, (128, 128), 1)
    for j in range(4):
        order = jnp.broadcast_to(row_perms[kk, j : j + 1, :], (128, 128)).T
        table = jnp.where(order == level, 1.0, 0.0).astype(BF16)
        pick[:, j * 128 : j * 128 + 128] = table
        pick[:, 512 + j * 128 : 640 + j * 128] = table


def add_pair(m, col_places, child_of, pick, wide_buf):
    for g in range(CHILDREN):
        for h in range(2):
            place = jnp.broadcast_to(col_places[2 * m + h, g : g + 1, :], (HALF, 128))
            taken = jnp.take_along_axis(
                child_of(g), jnp.maximum(place, 0), axis=1, mode="promise_in_bounds"
            )
            high, low = halves(jnp.where(place >= 0, taken, 0.0))
            wide_buf[g * 64 : g * 64 + 64, h * 128 : h * 128 + 128] = high
            wide_buf[512 + g * 64 : 576 + g * 64, h * 128 : h * 128 + 128] = low
    return jnp.dot(pick[...], wide_buf[...], preferred_element_type=F32)


EARLY = 4


def add_children(row_perms, col_places, front, children, out, pick, wide_buf):
    kk = mod(pl.program_id(0) + EARLY, ROW_BLOCKS)
    q = lax.axis_index("narrow")

    @pl.when(kk < EARLY)
    def _():
        out[...] = front[...]

    @pl.when(kk >= EARLY)
    def _():
        set_pick(pick, row_perms, kk)

        def one(m, carry):
            total = add_pair(m, col_places, lambda g: children[g, m], pick, wide_buf)
            for h in range(2):
                where = pl.ds(2 * m + h, BLOCK, stride=COL_BLOCKS)
                side = total[:, h * 128 : h * 128 + 128]
                if h == 0:
                    side = jnp.where(jnp.logical_and(m == 0, q < 4), 0.0, side)
                out[where, :] = front[where, :] + side
            return carry

        lax.fori_loop(0, 6, one, 0)


def body(root_front, child_update, child_map):
    child = child_update.reshape(3 * 16 * CHUNK, HALF)
    root = root_front.reshape(ROW_BLOCKS * BLOCK * COL_BLOCKS, BLOCK)
    vmem = lambda *shape: pltpu.VMEM(shape, F32)
    sems = lambda n: pltpu.SemaphoreType.DMA((n,))
    front, children, row_perms, col_places = pl.pallas_call(
        kernel,
        out_shape=[
            jax.ShapeDtypeStruct(root.shape, F32),
            jax.ShapeDtypeStruct((48, 6, HALF, 128), F32),
            jax.ShapeDtypeStruct((8, 4, 128), jnp.int32),
            jax.ShapeDtypeStruct((COL_BLOCKS, CHILDREN, 128), jnp.int32),
        ],
        in_specs=[pl.BlockSpec(memory_space=pl.ANY)] * 3,
        out_specs=[pl.BlockSpec(memory_space=pl.ANY)] * 4,
        scratch_shapes=[
            pltpu.VMEM((CHILDREN, 6144), jnp.int32),
            pltpu.VMEM((8, 4, 128), jnp.int32),
            pltpu.VMEM((COL_BLOCKS, CHILDREN, 128), jnp.int32),
            vmem(4 * CHUNK, HALF),
            vmem(ROW_BLOCKS * BLOCK * COL_BLOCKS, BLOCK),
            vmem(48, 6, HALF, 128),
            vmem(24, HALF, 128),
            vmem(6, BLOCK, 256),
            vmem(3, BLOCK, 256),
            vmem(6, SPAN, 256),
            vmem(4, SPAN, 128),
            vmem(4, 6, BLOCK, BLOCK),
            vmem(SPAN, 2 * SPAN),
            vmem(BLOCK, 2 * BLOCK),
            vmem(4, 768, BLOCK),
            pltpu.VMEM((768, SPAN), BF16),
            pltpu.VMEM((768, SPAN), BF16),
            vmem(768, 256),
            pltpu.VMEM((SPAN, SPAN), BF16),
            pltpu.VMEM((SPAN, SPAN), BF16),
            vmem(24, 6, HALF, 128),
            vmem(CHILDREN, 6, HALF, 128),
            pltpu.VMEM((BLOCK, 1024), BF16),
            pltpu.VMEM((1024, 256), BF16),
            sems(1), sems(3), sems(2), sems(1), sems(4), sems(1), sems(6), sems(24), sems(24), sems(48), sems(48), sems(24), sems(24),
            sems(6), sems(3), sems(24), sems(24), sems(24), sems(1), sems(1), sems(4), sems(4),
            sems(4), sems(1), sems(1), sems(1), sems(4), sems(4),
        ],
        compiler_params=pltpu.CompilerParams(
            collective_id=0, has_side_effects=True, vmem_limit_bytes=60 * 2**20
        ),
    )(child_map, child, root)
    part = pl.BlockSpec((BLOCK * COL_BLOCKS, BLOCK), lambda i: (mod(i + EARLY, ROW_BLOCKS), 0))
    out = pl.pallas_call(
        add_children,
        grid=(ROW_BLOCKS,),
        out_shape=jax.ShapeDtypeStruct(root.shape, F32),
        in_specs=[
            pl.BlockSpec((8, 4, 128), lambda i: (0, 0, 0)),
            pl.BlockSpec((COL_BLOCKS, CHILDREN, 128), lambda i: (0, 0, 0)),
            part,
            pl.BlockSpec(
                (CHILDREN, 6, HALF, 128),
                lambda i: (jnp.minimum(i + EARLY, ROW_BLOCKS - 1), 0, 0, 0),
            ),
        ],
        out_specs=part,
        scratch_shapes=[pltpu.VMEM((BLOCK, 1024), BF16), pltpu.VMEM((1024, 256), BF16)],
        compiler_params=pltpu.CompilerParams(vmem_limit_bytes=60 * 2**20),
    )(row_perms, col_places, front, children)
    return out.reshape(root_front.shape)


def solution(mesh):
    return jax.shard_map(
        body,
        mesh=mesh,
        in_specs=(
            P(None, "wide", None, None, "narrow", None),
            P("wide", None, None, None, None, "narrow", None),
            P(),
        ),
        out_specs=P(None, "wide", None, None, "narrow", None),
        check_vma=False,
    )
```

```python
import functools

import jax
import jax.numpy as jnp
from jax import lax
from jax.experimental import pallas as pl
from jax.experimental.pallas import tpu as pltpu
from jax.sharding import PartitionSpec as P

BLOCK = 128
HALF = 64
ROW_BLOCKS = 6
COL_BLOCKS = 12
CHILDREN = 8
N_WIDE = 16
N_NARROW = 8
SPAN = 512
CHUNK = HALF * COL_BLOCKS
MESH = pl.DeviceIdType.MESH
F32 = jnp.float32
BF16 = jnp.bfloat16


def mod(value, n):
    return lax.rem(value, n)


def shift_of(p, q):
    return p // 8 + (mod(p, 8) > q).astype(jnp.int32)


def halves(value):
    high = value.astype(BF16)
    low = (value - high.astype(F32)).astype(BF16)
    return high, low


def dot_full(a, b, dims):
    return lax.dot_general(
        a, b, (dims, ((), ())), precision=lax.Precision.HIGHEST, preferred_element_type=F32
    )


def thirds(value):
    high = value.astype(BF16).astype(F32)
    rest = value - high
    mid = rest.astype(BF16).astype(F32)
    low = rest - mid
    return high, mid, low


def factor_eight(cols):
    e = {}
    for a in range(8):
        for j in range(a + 1):
            e[a, j] = jnp.broadcast_to(cols[j][a : a + 1, :], (8, 128))
    inv = []
    low = {}
    for j in range(8):
        d = e[j, j]
        r = lax.rsqrt(d)
        r = r * (1.5 - 0.5 * d * r * r)
        inv.append(r)
        for a in range(j + 1, 8):
            low[a, j] = e[a, j] * r
        for a in range(j + 1, 8):
            for c in range(j + 1, a + 1):
                e[a, c] = e[a, c] - low[a, j] * low[c, j]
    return low, inv


def solve_eight(rows, low, inv):
    found = []
    for a in range(8):
        row = jnp.broadcast_to(rows[a : a + 1, :], (8, 128))
        for j in range(a):
            row = row - low[a, j] * found[j]
        found.append(row * inv[a])
    return found


def factor_128(pair, beside):
    lane = lax.broadcasted_iota(jnp.int32, (16, 128), 1)
    sub = lax.broadcasted_iota(jnp.int32, (8, 128), 0)

    def spread(value, j):
        return jnp.broadcast_to(value[:, j : j + 1], (8, 128))

    def gather_rows(found):
        total = found[0]
        for a in range(1, 8):
            total = jnp.where(sub == a, found[a], total)
        return total

    def step(b, carry):
        if beside is not None:
            beside.begin(b)
            beside.work(b)
        first = pl.multiple_of(b * 16, 16)
        rows = pair[pl.ds(first, 16), :]
        back = mod(128 - first, 128)
        top_a, top_b = rows[0:8, :128], rows[0:8, 128:]
        end_a, end_b = rows[8:16, :128], rows[8:16, 128:]
        top_t = pltpu.roll(top_a, back, 1)
        end_t = pltpu.roll(end_a, back, 1)
        low, inv = factor_eight([spread(top_t, j) for j in range(8)])
        ups_t = solve_eight(top_t, low, inv)
        ups_a = solve_eight(top_a, low, inv)
        ups_b = solve_eight(top_b, low, inv)
        link = []
        for a in range(8):
            value = spread(end_t, a)
            for j in range(a):
                value = value - link[j] * low[a, j]
            link.append(value * inv[a])
        for a in range(8):
            end_t = end_t - link[a] * ups_t[a]
            end_a = end_a - link[a] * ups_a[a]
            end_b = end_b - link[a] * ups_b[a]
        low, inv = factor_eight([spread(end_t, 8 + j) for j in range(8)])
        more_a = solve_eight(end_a, low, inv)
        more_b = solve_eight(end_b, low, inv)
        done_a = jnp.concatenate([gather_rows(ups_a), gather_rows(more_a)], axis=0)
        done_b = jnp.concatenate([gather_rows(ups_b), gather_rows(more_b)], axis=0)
        done = jnp.concatenate([done_a, done_b], axis=1)
        pair[pl.ds(first, 16), :] = done
        mult = jnp.where(lane >= first + 16, done_a, 0.0)
        mh, mm, ml = thirds(mult)
        uh, um, ul = thirds(done)
        left = jnp.concatenate([mh, mh, mm, mh, ml, mm], axis=0).astype(BF16)
        right = jnp.concatenate([uh, um, uh, ul, uh, um], axis=0).astype(BF16)
        gone = lax.dot_general(
            left, right, (((0,), (0,)), ((), ())), preferred_element_type=F32
        )
        pair[...] = pair[...] - gone
        if beside is not None:
            beside.end(b)
        return carry

    lax.fori_loop(0, 8, step, 0)


def factor_block(jb, work, pair, beside):
    at = jb * 128
    eye = (
        lax.broadcasted_iota(jnp.int32, (128, 128), 0)
        == lax.broadcasted_iota(jnp.int32, (128, 128), 1)
    ).astype(F32)
    pair[:, 0:128] = work[at : at + 128, at : at + 128]
    pair[:, 128:256] = eye
    factor_128(pair, beside)
    inverse = pair[:, 128:256]
    if jb:
        work[at : at + 128, SPAN : SPAN + at] = dot_full(
            inverse, work[at : at + 128, SPAN : SPAN + at], ((1,), (0,))
        )
    work[at : at + 128, SPAN + at : SPAN + at + 128] = inverse
    if jb < 3:
        rest = at + 128
        above = dot_full(inverse, work[at : at + 128, rest:SPAN], ((1,), (0,)))
        work[rest:SPAN, rest:SPAN] -= dot_full(above, above, ((0,), (0,)))
        work[rest:SPAN, SPAN : SPAN + rest] -= dot_full(
            above, work[at : at + 128, SPAN : SPAN + rest], ((0,), (0,))
        )


def kernel(
    child_map, child, root, out, bulk_in, row_out, col_out,
    marks, row_perms, col_places, chunk_buf, front, bulk_out, unit_in, front_out, front_in, cols, diag, rows, work,
    pair, rows_f, rows_h, rows_l, prod, inv_h, inv_l, kids, pick, wide_buf,
    kids_s, keep_s, tab_s, s_marks, s_chunk, s_front, s_out, bulk_s, bulk_r, unit_s, unit_r, front_s, front_r,
    cols_s, cols_r, hand_s, dz_s, dz_r, dy_s, dy_r, r1_s, r1_r, rz_s, rz_r, ry_s, ry_r,
):
    p = lax.axis_index("wide")
    q = lax.axis_index("narrow")
    core = mod(p, 2)
    chip = p // 2
    ph = p // 8
    pl8 = mod(p, 8)
    zl = q // 4
    y = mod(q, 4)
    own = pl8 == q
    shift = shift_of(p, q)
    q_other = mod(q + 4, 8)

    def remote(src, dst, ssem, rsem, wide, narrow):
        return pltpu.make_async_remote_copy(
            src_ref=src, dst_ref=dst, send_sem=ssem, recv_sem=rsem,
            device_id=(wide, narrow), device_id_type=MESH,
        )

    def local(src, dst, sem):
        return pltpu.make_async_copy(src, dst, sem)

    def chunk_of(n):
        first = jnp.where(
            ph == 0,
            jnp.where(n < 12, 8 + mod(p + n, 8), 4 + mod(n, 4)),
            jnp.where(n < 8, 4 + mod(p + n, 4), 8 + mod(p + n, 8)),
        )
        first = jnp.where(n < 4, n, first)
        late = n - 16
        k = jnp.where(n < 16, 0, 1 + mod(late // 8, 2))
        side = jnp.where(n < 32, 1 - ph, ph)
        dest = jnp.where(n < 16, first, side * 8 + mod(p + n, 8))
        return k, dest

    def chunk_copy(n):
        k, dest = chunk_of(n)
        at = pl.multiple_of((k * 16 + dest) * CHUNK, CHUNK)
        slot = mod(n, 4)
        to = pl.multiple_of(slot * CHUNK, CHUNK)
        return local(child.at[pl.ds(at, CHUNK)], chunk_buf.at[pl.ds(to, CHUNK)], s_chunk.at[slot])

    for n in range(4):
        chunk_copy(jnp.int32(n)).start()
    marks_load = local(child_map, marks, s_marks.at[0])
    marks_load.start()
    front_load = local(root, front, s_front.at[0])
    front_load.start()

    barrier = pltpu.get_barrier_semaphore()

    def greet(wide, narrow):
        pl.semaphore_signal(barrier, inc=1, device_id=(wide, narrow), device_id_type=MESH)

    def greet_wide(i, carry):
        greet(mod(p + i, 16), q)
        return carry

    lax.fori_loop(1, 16, greet_wide, 0)
    for i in range(1, 4):
        greet(p, zl * 4 + mod(y + i, 4))


    greet(p, q_other)
    pl.semaphore_wait(barrier, 19)

    def packed(n, la, lb):
        base = mod(n, 4) * CHUNK
        xa = chunk_buf[pl.ds(base + la, HALF, stride=COL_BLOCKS), :]
        xb = chunk_buf[pl.ds(base + lb, HALF, stride=COL_BLOCKS), :]
        return jnp.concatenate([xa, xb], axis=1)

    def next_chunk(n):
        @pl.when(n + 4 < 48)
        def _():
            chunk_copy(n + 4).start()

    def unit_copy(u):
        slot = u // 8
        owner = mod(u, 8) * 2 + (slot > 0).astype(jnp.int32)
        return owner, remote(
            bulk_out.at[mod(u, 4) * 3, u // 4], unit_in.at[slot * 8 + chip], unit_s.at[u], unit_r.at[slot * 8 + chip],
            owner, q,
        )

    def front_copy(m):
        u = m * 4 + p
        slot = u // 8
        owner = mod(u, 8) * 2 + (slot > 0).astype(jnp.int32)
        return owner, slot, remote(
            front_out.at[m], front_in.at[slot], front_s.at[m], front_r.at[slot], owner, q
        )

    def bulk_copy(k, dest):
        kk = 2 * k + core
        return remote(
            bulk_out.at[dest * 3 + k], bulk_in.at[kk * 8 + chip],
            bulk_s.at[dest * 3 + k], bulk_r.at[kk * 8 + chip], dest, q,
        )

    def keep_copy(k):
        return local(bulk_out.at[p * 3 + k], bulk_in.at[(2 * k + core) * 8 + chip], keep_s.at[k])

    def panel_row(kk, dest):
        return jnp.logical_and(kk == 0, dest < 4)

    def pack(n, carry):
        chunk_copy(n).wait()
        k, dest = chunk_of(n)

        def one(m, c):
            bulk_out[dest * 3 + k, m] = packed(n, 2 * m, 2 * m + 1)
            return c

        lax.fori_loop(0, 6, one, 0)

        @pl.when(panel_row(2 * k + core, dest))
        def _():
            def unit(m, c):
                u = m * 4 + dest
                owner, copy = unit_copy(u)

                @pl.when(owner != p)
                def _():
                    copy.start()

                @pl.when(owner == p)
                def _():
                    unit_in[(u // 8) * 8 + chip] = bulk_out[dest * 3, m]
                return c

            lax.fori_loop(0, 6, unit, 0)
        next_chunk(n)
        return carry

    def fire(n, carry):
        k, dest = chunk_of(n)

        @pl.when(jnp.logical_not(panel_row(2 * k + core, dest)))
        def _():
            @pl.when(dest != p)
            def _():
                bulk_copy(k, dest).start()

            @pl.when(dest == p)
            def _():
                keep_copy(k).start()
        return carry

    def pack_fire(n, carry):
        return fire(n, pack(n, carry))

    class Beside:
        def __init__(self, first):
            self.first = first

        def begin(self, b):
            chunk_copy(self.first + b).wait()

        def work(self, b):
            n = self.first + b
            k, dest = chunk_of(n)
            for m in range(6):
                bulk_out[dest * 3 + k, m] = packed(n, 2 * m, 2 * m + 1)

        def end(self, b):
            next_chunk(self.first + b)
            fire(self.first + b, 0)

    lax.fori_loop(0, 4, pack, 0)
    front_load.wait()

    @pl.when(p < 4)
    def _():
        def one(m, c):
            for h in range(2):
                front_out[m, :, h * 128 : h * 128 + 128] = front[
                    pl.ds(2 * m + h, BLOCK, stride=COL_BLOCKS), :
                ]
            owner, slot, copy = front_copy(m)

            @pl.when(owner != p)
            def _():
                copy.start()

            @pl.when(owner == p)
            def _():
                front_in[slot] = front_out[m]
            return c

        lax.fori_loop(0, 6, one, 0)

    def assemble(source, m, row):
        sides = []
        for h in range(2):
            total = jnp.zeros((BLOCK, BLOCK), F32)
            for pair_id in range(CHILDREN // 2):
                parts = []
                for g in (2 * pair_id, 2 * pair_id + 1):
                    place = jnp.broadcast_to(col_places[2 * m + h, g : g + 1, :], (HALF, 128))
                    taken = jnp.take_along_axis(
                        source(g), jnp.maximum(place, 0), axis=1, mode="promise_in_bounds"
                    )
                    parts.append(jnp.where(place >= 0, taken, 0.0))
                turned = jnp.concatenate(parts, axis=0).T
                order = jnp.broadcast_to(row_perms[row, pair_id : pair_id + 1, :], (BLOCK, BLOCK))
                total += jnp.take_along_axis(turned, order, axis=1, mode="promise_in_bounds")
            sides.append(total.T)
        return sides

    def cols_at(u):
        return cols.at[u // 4, pl.ds(pl.multiple_of(mod(u, 4) * 128, 128), 128), :]

    def cross_copy(u):
        return remote(
            cols_at(u), cols_at(u), cols_s.at[(u // 8) * 8], cols_r.at[u],
            mod(chip + 4, 8) * 2 + core, q,
        )

    def along_copy(u, dx):
        far = jnp.where(mod(u, 8) == chip, 0, 3)
        return remote(
            cols_at(u), cols_at(u), cols_s.at[(u // 8) * 8 + far + dx], cols_r.at[u],
            (ph * 4 + mod(chip + dx, 4)) * 2 + core, q,
        )

    def along(u):
        def send(dx, c):
            along_copy(u, dx).start()
            return c

        lax.fori_loop(1, 4, send, 0)

    def hand_copy(u):
        return remote(cols_at(u), cols_at(u), hand_s.at[u], cols_r.at[u], chip * 2 + 1 - core, q)

    def own_unit(slot, carry):
        u = slot * 8 + chip
        block = mod(u, 4)

        def landed(g, c):
            @pl.when(jnp.logical_or(core == 1, g != chip))
            def _():
                remote(
                    bulk_out.at[0, 0], unit_in.at[slot * 8 + g], unit_s.at[0],
                    unit_r.at[slot * 8 + g], g * 2, q,
                ).wait_recv()
            return c

        lax.fori_loop(0, 8, landed, 0)

        @pl.when(block != p)
        def _():
            remote(
                front_out.at[0], front_in.at[slot], front_s.at[0], front_r.at[slot], block, q
            ).wait_recv()

        sides = assemble(lambda g: unit_in[slot * 8 + g], u // 4, 6)
        cols[u // 4, pl.ds(pl.multiple_of(block * 128, 128), 128), :] = (
            jnp.concatenate(sides, axis=1) + front_in[slot]
        )

        cross_copy(u).start()
        along(u)
        hand_copy(u).start()
        return carry

    def spread_on(slot, carry):
        u = slot * 8 + mod(chip + 4, 8)
        cross_copy(u).wait_recv()
        along(u)
        hand_copy(u).start()
        return carry

    def hand_on(u, carry):
        @pl.when(mod(u - chip + 32, 4) != 0)
        def _():
            cross_copy(u).wait_recv()
            hand_copy(u).start()
        return carry

    def taken(u, carry):
        hand_copy(u).wait_recv()
        return carry

    first_slot = core
    last_slot = 1 + 2 * core

    marks_load.wait()
    ranks = lax.broadcasted_iota(jnp.int32, (HALF, 128), 0)
    spots = lax.broadcasted_iota(jnp.int32, (HALF, 128), 1)

    def places(block):
        at = pl.multiple_of((block // 2) * 128, 128)
        part = marks[:, pl.ds(at, 128)]
        mine = jnp.where(mod(block, 2) == 0, part, pltpu.roll(part, 64, 1)) - block * BLOCK
        tall = mine.T
        found = []
        for g in range(CHILDREN):
            hit = jnp.broadcast_to(tall[0:HALF, g : g + 1], (HALF, 128)) == spots
            found.append(jnp.max(jnp.where(hit, ranks, -1), axis=0, keepdims=True))
        return found

    def row_table(i, carry, block=None):
        found = places(i * 16 + p if block is None else block)
        for j in range(4):
            first, second = found[2 * j], found[2 * j + 1]
            row_perms[i, j : j + 1, :] = jnp.where(first >= 0, first, second + HALF)
        return carry


    def col_table(l, carry):
        found = places(l * 8 + q)
        for g in range(CHILDREN):
            col_places[l, g : g + 1, :] = jnp.where(
                found[g] >= 0, found[g] + mod(l, 2) * HALF, -1
            )
        return carry

    row_table(6, 0, mod(chip, 4))

    class Tables:
        def begin(self, b):
            pass

        def work(self, b):
            col_table(jnp.minimum(2 * b, 11), 0)
            col_table(jnp.minimum(2 * b + 1, 11), 0)
            row_table(jnp.minimum(b, 5), 0)

        def end(self, b):
            pass

    def unit_table(slot, carry):
        m = slot * 2 + chip // 4
        return col_table(2 * m + 1, col_table(2 * m, carry))

    lax.fori_loop(core, 1 + 2 * core, unit_table, 0)
    lax.fori_loop(first_slot, last_slot, own_unit, 0)
    lax.fori_loop(0, 4, fire, 0)
    lax.fori_loop(4, 8, pack_fire, 0)
    lax.fori_loop(first_slot, last_slot, spread_on, 0)
    lax.fori_loop(8, 10, pack_fire, 0)

    @pl.when(core == 0)
    def _():
        lax.fori_loop(0, 4, hand_on, 0)

    @pl.when(core == 1)
    def _():
        lax.fori_loop(0, 4, taken, 0)

    dz = remote(diag.at[y], diag.at[y], dz_s.at[0], dz_r.at[0], p, q_other)

    @pl.when(zl == 0)
    def _():
        diag[y] = cols[0, :, 0:128]
        dz.start()

    @pl.when(zl == 1)
    def _():
        dz.wait_recv()

    def dy(i):
        return remote(diag.at[y], diag.at[y], dy_s.at[i], dy_r.at[y], p, zl * 4 + mod(y + i, 4))

    for i in range(1, 4):
        dy(i).start()


    @pl.when(core == 0)
    def _():
        lax.fori_loop(4, 8, hand_on, 0)
        lax.fori_loop(8, 24, taken, 0)

    @pl.when(core == 1)
    def _():
        lax.fori_loop(8, 24, hand_on, 0)
        lax.fori_loop(4, 8, taken, 0)

    def r1(c):
        return remote(
            cols.at[:, pl.ds(c * 128, 128), pl.ds(pl.multiple_of(ph * 128, 128), 128)],
            rows.at[c], r1_s.at[c], r1_r.at[0], p, zl * 4 + c,
        )

    rz = remote(rows.at[y], rows.at[y], rz_s.at[0], rz_r.at[0], p, q_other)

    def ry(i):
        return remote(rows.at[y], rows.at[y], ry_s.at[i], ry_r.at[y], p, zl * 4 + mod(y + i, 4))

    @pl.when(own)
    def _():
        for c in range(4):
            @pl.when(y != c)
            def _():
                r1(c).start()

            @pl.when(y == c)
            def _():
                rows[c] = cols[:, c * 128 : c * 128 + 128, pl.ds(pl.multiple_of(ph * 128, 128), 128)]


    lax.fori_loop(10, 20, pack_fire, 0)

    holder = zl == pl8 // 4

    @pl.when(holder)
    def _():
        @pl.when(jnp.logical_not(own))
        def _():
            remote(
                rows.at[y], rows.at[y], r1_s.at[0], r1_r.at[0], p, q_other
            ).wait_recv()
        rz.start()

    lax.fori_loop(20, 32, pack_fire, 0)

    for i in range(1, 4):
        src = mod(y + i, 4)
        remote(diag.at[src], diag.at[src], dy_s.at[i], dy_r.at[src], p, q_other).wait_recv()

    for c in range(4):
        work[:, c * 128 : c * 128 + 128] = diag[c]
    full = work[:, 0:SPAN]
    work[:, 0:SPAN] = 0.5 * (full + full.T)
    work[:, SPAN:] = jnp.zeros((SPAN, SPAN), F32)

    factor_block(0, work, pair, Beside(32))

    @pl.when(jnp.logical_not(holder))
    def _():
        rz.wait_recv()

    for i in range(1, 4):
        ry(i).start()

    factor_block(1, work, pair, Beside(40))
    factor_block(2, work, pair, None)
    factor_block(3, work, pair, Tables())

    def sent_unit(slot, carry):
        u = slot * 8 + chip

        cross_copy(u).wait_send()

        def one(dx, c):
            along_copy(u, dx).wait_send()
            along_copy(slot * 8 + mod(chip + 4, 8), dx).wait_send()
            return c

        lax.fori_loop(1, 4, one, 0)
        hand_copy(u).wait_send()
        return carry

    lax.fori_loop(first_slot, last_slot, sent_unit, 0)

    def handed(u, carry):
        @pl.when(mod(u, 8) != chip)
        def _():
            hand_copy(u).wait_send()
        return carry

    @pl.when(core == 0)
    def _():
        lax.fori_loop(0, 8, handed, 0)

    @pl.when(core == 1)
    def _():
        lax.fori_loop(8, 24, handed, 0)

    @pl.when(zl == 0)
    def _():
        dz.wait_send()

    for i in range(1, 4):
        dy(i).wait_send()

    @pl.when(own)
    def _():
        for c in range(4):
            @pl.when(y != c)
            def _():
                r1(c).wait_send()

    @pl.when(holder)
    def _():
        rz.wait_send()

    for i in range(1, 4):
        ry(i).wait_send()

    for i in range(1, 4):
        src = mod(y + i, 4)
        remote(rows.at[src], rows.at[src], ry_s.at[i], ry_r.at[src], p, q_other).wait_recv()

    inverse_h, inverse_l = halves(work[:, SPAN:])
    inv_h[...] = inverse_h
    inv_l[...] = inverse_l

    def solve(block):
        high, low = halves(block)
        total = jnp.dot(inv_h[...], high, preferred_element_type=F32)
        total += jnp.dot(inv_h[...], low, preferred_element_type=F32)
        total += jnp.dot(inv_l[...], high, preferred_element_type=F32)
        return total

    def solve_rows(i, carry):
        parts = [
            jnp.concatenate([rows[c, 2 * i + h] for c in range(4)], axis=0) for h in range(2)
        ]
        turned = solve(jnp.concatenate(parts, axis=1)).T
        at = pl.multiple_of(i * 256, 256)
        high, low = halves(turned)
        rows_h[pl.ds(at, 256), :] = high
        rows_l[pl.ds(at, 256), :] = low
        for c in range(4):
            rows_f[c, pl.ds(at, 256), :] = turned[:, c * 128 : c * 128 + 128]
        return carry

    lax.fori_loop(0, 3, solve_rows, 0)

    def solve_cols(m, carry):
        solved = solve(cols[m])
        high, low = halves(solved)
        cols[m] = solved
        total = jnp.dot(rows_h[...], high, preferred_element_type=F32)
        total += jnp.dot(rows_h[...], low, preferred_element_type=F32)
        total += jnp.dot(rows_l[...], high, preferred_element_type=F32)
        prod[...] = total

        def less(kk, c):
            at = pl.multiple_of(kk * 128, 128)
            for h in range(2):
                where = pl.ds(kk * (128 * COL_BLOCKS) + 2 * m + h, BLOCK, stride=COL_BLOCKS)
                front[where, :] = (
                    front[where, :] - prod[pl.ds(at, 128), h * 128 : h * 128 + 128]
                )
            return c

        lax.fori_loop(0, 6, less, 0)
        return carry

    lax.fori_loop(0, 6, solve_cols, 0)

    def store(kk):
        at = pl.multiple_of(kk * (128 * COL_BLOCKS), 128 * COL_BLOCKS)
        span = pl.ds(at, 128 * COL_BLOCKS)
        return local(front.at[span], out.at[span], s_out.at[kk])

    @pl.when(p < 4)
    def _():
        for l in range(COL_BLOCKS):
            @pl.when(l * 8 + q > p)
            def _():
                front[pl.ds(l, BLOCK, stride=COL_BLOCKS), :] = cols[
                    l // 2, pl.ds(pl.multiple_of(p * 128, 128), 128),
                    (l % 2) * 128 : (l % 2) * 128 + 128,
                ]

    @pl.when(q < 4)
    def _():
        for kk in range(ROW_BLOCKS):
            @pl.when(kk * 16 + p > q)
            def _():
                front[pl.ds(kk * (128 * COL_BLOCKS), BLOCK, stride=COL_BLOCKS), :] = rows_f[
                    q, kk * 128 : kk * 128 + 128, :
                ]

        @pl.when(p == q)
        def _():
            tile = rows_f[q, 0:128, :]
            lower = lax.broadcasted_iota(jnp.int32, (128, 128), 0) >= lax.broadcasted_iota(
                jnp.int32, (128, 128), 1
            )
            front[pl.ds(0, BLOCK, stride=COL_BLOCKS), :] = jnp.where(lower, tile, tile.T)

    def arrived(kk):
        def landed(g, c):
            mine = jnp.logical_and(g == chip, mod(kk, 2) == core)

            @pl.when(jnp.logical_not(mine))
            def _():
                remote(
                    bulk_out.at[0], bulk_in.at[kk * 8 + g], bulk_s.at[0], bulk_r.at[kk * 8 + g],
                    g * 2 + mod(kk, 2), q,
                ).wait_recv()

            @pl.when(mine)
            def _():
                keep_copy(kk // 2).wait()
            return c

        lax.fori_loop(0, 8, landed, 0)

    def early(kk, carry):
        @pl.when(jnp.logical_not(panel_row(kk, p)))
        def _():
            arrived(kk)
            at = pl.multiple_of(kk * 8, 8)
            load = local(bulk_in.at[pl.ds(at, 8)], kids, kids_s.at[0])
            load.start()
            set_pick(pick, row_perms, kk)
            load.wait()

            def one(m, c):
                total = add_pair(m, col_places, lambda g: kids[g, m], pick, wide_buf)
                for h in range(2):
                    where = pl.ds(kk * (128 * COL_BLOCKS) + 2 * m + h, BLOCK, stride=COL_BLOCKS)
                    side = total[:, h * 128 : h * 128 + 128]
                    if h == 0:
                        side = jnp.where(jnp.logical_and(m == 0, q < 4), 0.0, side)
                    front[where, :] = front[where, :] + side
                return c

            lax.fori_loop(0, 6, one, 0)
        store(kk).start()
        return carry

    lax.fori_loop(EARLY, 6, lambda kk, c: (store(kk).start(), c)[1], 0)
    lax.fori_loop(0, EARLY, early, 0)
    lax.fori_loop(EARLY, 6, lambda kk, c: (arrived(kk), c)[1], 0)
    tables = [
        local(row_perms, row_out, tab_s.at[0]), local(col_places, col_out, tab_s.at[1])
    ]
    for copy in tables:
        copy.start()
    for copy in tables:
        copy.wait()

    def sent_bulk(n, carry):
        k, dest = chunk_of(n)

        @pl.when(jnp.logical_not(jnp.logical_or(dest == p, panel_row(2 * k + core, dest))))
        def _():
            bulk_copy(k, dest).wait_send()
        return carry

    lax.fori_loop(0, 48, sent_bulk, 0)

    @pl.when(core == 0)
    def _():
        def one(u, c):
            owner, copy = unit_copy(u)

            @pl.when(owner != p)
            def _():
                copy.wait_send()
            return c

        lax.fori_loop(0, 24, one, 0)

    @pl.when(p < 4)
    def _():
        def one(m, c):
            owner, slot, copy = front_copy(m)

            @pl.when(owner != p)
            def _():
                copy.wait_send()
            return c

        lax.fori_loop(0, 6, one, 0)

    def stored(kk, carry):
        store(kk).wait()
        return carry

    lax.fori_loop(0, 6, stored, 0)


def set_pick(pick, row_perms, kk):
    level = lax.broadcasted_iota(jnp.int32, (128, 128), 1)
    for j in range(4):
        order = jnp.broadcast_to(row_perms[kk, j : j + 1, :], (128, 128)).T
        table = jnp.where(order == level, 1.0, 0.0).astype(BF16)
        pick[:, j * 128 : j * 128 + 128] = table
        pick[:, 512 + j * 128 : 640 + j * 128] = table


def add_pair(m, col_places, child_of, pick, wide_buf):
    for g in range(CHILDREN):
        for h in range(2):
            place = jnp.broadcast_to(col_places[2 * m + h, g : g + 1, :], (HALF, 128))
            taken = jnp.take_along_axis(
                child_of(g), jnp.maximum(place, 0), axis=1, mode="promise_in_bounds"
            )
            high, low = halves(jnp.where(place >= 0, taken, 0.0))
            wide_buf[g * 64 : g * 64 + 64, h * 128 : h * 128 + 128] = high
            wide_buf[512 + g * 64 : 576 + g * 64, h * 128 : h * 128 + 128] = low
    return jnp.dot(pick[...], wide_buf[...], preferred_element_type=F32)


EARLY = 4


def add_children(row_perms, col_places, front, children, out, pick, wide_buf):
    kk = mod(pl.program_id(0) + EARLY, ROW_BLOCKS)
    q = lax.axis_index("narrow")

    @pl.when(kk < EARLY)
    def _():
        out[...] = front[...]

    @pl.when(kk >= EARLY)
    def _():
        set_pick(pick, row_perms, kk)

        def one(m, carry):
            total = add_pair(m, col_places, lambda g: children[g, m], pick, wide_buf)
            for h in range(2):
                where = pl.ds(2 * m + h, BLOCK, stride=COL_BLOCKS)
                side = total[:, h * 128 : h * 128 + 128]
                if h == 0:
                    side = jnp.where(jnp.logical_and(m == 0, q < 4), 0.0, side)
                out[where, :] = front[where, :] + side
            return carry

        lax.fori_loop(0, 6, one, 0)


def body(root_front, child_update, child_map):
    child = child_update.reshape(3 * 16 * CHUNK, HALF)
    root = root_front.reshape(ROW_BLOCKS * BLOCK * COL_BLOCKS, BLOCK)
    vmem = lambda *shape: pltpu.VMEM(shape, F32)
    sems = lambda n: pltpu.SemaphoreType.DMA((n,))
    front, children, row_perms, col_places = pl.pallas_call(
        kernel,
        out_shape=[
            jax.ShapeDtypeStruct(root.shape, F32),
            jax.ShapeDtypeStruct((48, 6, HALF, 128), F32),
            jax.ShapeDtypeStruct((8, 4, 128), jnp.int32),
            jax.ShapeDtypeStruct((COL_BLOCKS, CHILDREN, 128), jnp.int32),
        ],
        in_specs=[pl.BlockSpec(memory_space=pl.ANY)] * 3,
        out_specs=[pl.BlockSpec(memory_space=pl.ANY)] * 4,
        scratch_shapes=[
            pltpu.VMEM((CHILDREN, 6144), jnp.int32),
            pltpu.VMEM((8, 4, 128), jnp.int32),
            pltpu.VMEM((COL_BLOCKS, CHILDREN, 128), jnp.int32),
            vmem(4 * CHUNK, HALF),
            vmem(ROW_BLOCKS * BLOCK * COL_BLOCKS, BLOCK),
            vmem(48, 6, HALF, 128),
            vmem(24, HALF, 128),
            vmem(6, BLOCK, 256),
            vmem(3, BLOCK, 256),
            vmem(6, SPAN, 256),
            vmem(4, SPAN, 128),
            vmem(4, 6, BLOCK, BLOCK),
            vmem(SPAN, 2 * SPAN),
            vmem(BLOCK, 2 * BLOCK),
            vmem(4, 768, BLOCK),
            pltpu.VMEM((768, SPAN), BF16),
            pltpu.VMEM((768, SPAN), BF16),
            vmem(768, 256),
            pltpu.VMEM((SPAN, SPAN), BF16),
            pltpu.VMEM((SPAN, SPAN), BF16),
            vmem(CHILDREN, 6, HALF, 128),
            pltpu.VMEM((BLOCK, 1024), BF16),
            pltpu.VMEM((1024, 256), BF16),
            sems(1), sems(3), sems(2), sems(1), sems(4), sems(1), sems(6), sems(48), sems(48), sems(24), sems(24),
            sems(6), sems(3), sems(24), sems(24), sems(24), sems(1), sems(1), sems(4), sems(4),
            sems(4), sems(1), sems(1), sems(1), sems(4), sems(4),
        ],
        compiler_params=pltpu.CompilerParams(
            collective_id=0, has_side_effects=True, vmem_limit_bytes=60 * 2**20
        ),
    )(child_map, child, root)
    part = pl.BlockSpec((BLOCK * COL_BLOCKS, BLOCK), lambda i: (mod(i + EARLY, ROW_BLOCKS), 0))
    out = pl.pallas_call(
        add_children,
        grid=(ROW_BLOCKS,),
        out_shape=jax.ShapeDtypeStruct(root.shape, F32),
        in_specs=[
            pl.BlockSpec((8, 4, 128), lambda i: (0, 0, 0)),
            pl.BlockSpec((COL_BLOCKS, CHILDREN, 128), lambda i: (0, 0, 0)),
            part,
            pl.BlockSpec(
                (CHILDREN, 6, HALF, 128),
                lambda i: (jnp.minimum(i + EARLY, ROW_BLOCKS - 1), 0, 0, 0),
            ),
        ],
        out_specs=part,
        scratch_shapes=[pltpu.VMEM((BLOCK, 1024), BF16), pltpu.VMEM((1024, 256), BF16)],
        compiler_params=pltpu.CompilerParams(vmem_limit_bytes=60 * 2**20),
    )(row_perms, col_places, front, children)
    return out.reshape(root_front.shape)


def solution(mesh):
    return jax.shard_map(
        body,
        mesh=mesh,
        in_specs=(
            P(None, "wide", None, None, "narrow", None),
            P("wide", None, None, None, None, "narrow", None),
            P(),
        ),
        out_specs=P(None, "wide", None, None, "narrow", None),
        check_vma=False,
    )
```

```python
import functools

import jax
import jax.numpy as jnp
from jax import lax
from jax.experimental import pallas as pl
from jax.experimental.pallas import tpu as pltpu
from jax.sharding import PartitionSpec as P

BLOCK = 128
HALF = 64
ROW_BLOCKS = 6
COL_BLOCKS = 12
CHILDREN = 8
N_WIDE = 16
N_NARROW = 8
SPAN = 512
CHUNK = HALF * COL_BLOCKS
MESH = pl.DeviceIdType.MESH
F32 = jnp.float32
BF16 = jnp.bfloat16


def mod(value, n):
    return lax.rem(value, n)


def shift_of(p, q):
    return p // 8 + (mod(p, 8) > q).astype(jnp.int32)


def halves(value):
    high = value.astype(BF16)
    low = (value - high.astype(F32)).astype(BF16)
    return high, low


def dot_full(a, b, dims):
    return lax.dot_general(
        a, b, (dims, ((), ())), precision=lax.Precision.HIGHEST, preferred_element_type=F32
    )


def thirds(value):
    high = value.astype(BF16).astype(F32)
    rest = value - high
    mid = rest.astype(BF16).astype(F32)
    low = rest - mid
    return high, mid, low


def factor_eight(cols):
    e = {}
    for a in range(8):
        for j in range(a + 1):
            e[a, j] = jnp.broadcast_to(cols[j][a : a + 1, :], (8, 128))
    inv = []
    low = {}
    for j in range(8):
        d = e[j, j]
        r = lax.rsqrt(d)
        r = r * (1.5 - 0.5 * d * r * r)
        inv.append(r)
        for a in range(j + 1, 8):
            low[a, j] = e[a, j] * r
        for a in range(j + 1, 8):
            for c in range(j + 1, a + 1):
                e[a, c] = e[a, c] - low[a, j] * low[c, j]
    return low, inv


def solve_eight(rows, low, inv):
    found = []
    for a in range(8):
        row = jnp.broadcast_to(rows[a : a + 1, :], (8, 128))
        for j in range(a):
            row = row - low[a, j] * found[j]
        found.append(row * inv[a])
    return found


def factor_128(pair, beside):
    lane = lax.broadcasted_iota(jnp.int32, (16, 128), 1)
    sub = lax.broadcasted_iota(jnp.int32, (8, 128), 0)

    def spread(value, j):
        return jnp.broadcast_to(value[:, j : j + 1], (8, 128))

    def gather_rows(found):
        total = found[0]
        for a in range(1, 8):
            total = jnp.where(sub == a, found[a], total)
        return total

    def step(b, carry):
        if beside is not None:
            beside.begin(b)
            beside.work(b)
        first = pl.multiple_of(b * 16, 16)
        rows = pair[pl.ds(first, 16), :]
        back = mod(128 - first, 128)
        top_a, top_b = rows[0:8, :128], rows[0:8, 128:]
        end_a, end_b = rows[8:16, :128], rows[8:16, 128:]
        top_t = pltpu.roll(top_a, back, 1)
        end_t = pltpu.roll(end_a, back, 1)
        low, inv = factor_eight([spread(top_t, j) for j in range(8)])
        ups_t = solve_eight(top_t, low, inv)
        ups_a = solve_eight(top_a, low, inv)
        ups_b = solve_eight(top_b, low, inv)
        link = []
        for a in range(8):
            value = spread(end_t, a)
            for j in range(a):
                value = value - link[j] * low[a, j]
            link.append(value * inv[a])
        for a in range(8):
            end_t = end_t - link[a] * ups_t[a]
            end_a = end_a - link[a] * ups_a[a]
            end_b = end_b - link[a] * ups_b[a]
        low, inv = factor_eight([spread(end_t, 8 + j) for j in range(8)])
        more_a = solve_eight(end_a, low, inv)
        more_b = solve_eight(end_b, low, inv)
        done_a = jnp.concatenate([gather_rows(ups_a), gather_rows(more_a)], axis=0)
        done_b = jnp.concatenate([gather_rows(ups_b), gather_rows(more_b)], axis=0)
        done = jnp.concatenate([done_a, done_b], axis=1)
        pair[pl.ds(first, 16), :] = done
        mult = jnp.where(lane >= first + 16, done_a, 0.0)
        mh, mm, ml = thirds(mult)
        uh, um, ul = thirds(done)
        left = jnp.concatenate([mh, mh, mm, mh, ml, mm], axis=0).astype(BF16)
        right = jnp.concatenate([uh, um, uh, ul, uh, um], axis=0).astype(BF16)
        gone = lax.dot_general(
            left, right, (((0,), (0,)), ((), ())), preferred_element_type=F32
        )
        pair[...] = pair[...] - gone
        if beside is not None:
            beside.end(b)
        return carry

    lax.fori_loop(0, 8, step, 0)


def factor_block(jb, work, pair, beside):
    at = jb * 128
    eye = (
        lax.broadcasted_iota(jnp.int32, (128, 128), 0)
        == lax.broadcasted_iota(jnp.int32, (128, 128), 1)
    ).astype(F32)
    pair[:, 0:128] = work[at : at + 128, at : at + 128]
    pair[:, 128:256] = eye
    factor_128(pair, beside)
    inverse = pair[:, 128:256]
    if jb:
        work[at : at + 128, SPAN : SPAN + at] = dot_full(
            inverse, work[at : at + 128, SPAN : SPAN + at], ((1,), (0,))
        )
    work[at : at + 128, SPAN + at : SPAN + at + 128] = inverse
    if jb < 3:
        rest = at + 128
        above = dot_full(inverse, work[at : at + 128, rest:SPAN], ((1,), (0,)))
        work[rest:SPAN, rest:SPAN] -= dot_full(above, above, ((0,), (0,)))
        work[rest:SPAN, SPAN : SPAN + rest] -= dot_full(
            above, work[at : at + 128, SPAN : SPAN + rest], ((0,), (0,))
        )


def kernel(
    child_map, child, root, out, bulk_in, row_out, col_out,
    marks, row_perms, col_places, chunk_buf, front, bulk_out, unit_in, front_out, front_in, cols, diag, rows, work,
    pair, rows_f, rows_h, rows_l, prod, inv_h, inv_l, relay, kids, pick, wide_buf,
    kids_s, keep_s, tab_s, s_marks, s_chunk, s_front, s_out, relay_s, relay_r, bulk_s, bulk_r, unit_s, unit_r, front_s, front_r,
    cols_s, cols_r, hand_s, dz_s, dz_r, dy_s, dy_r, r1_s, r1_r, rz_s, rz_r, ry_s, ry_r,
):
    p = lax.axis_index("wide")
    q = lax.axis_index("narrow")
    core = mod(p, 2)
    chip = p // 2
    ph = p // 8
    pl8 = mod(p, 8)
    zl = q // 4
    y = mod(q, 4)
    own = pl8 == q
    shift = shift_of(p, q)
    q_other = mod(q + 4, 8)

    def remote(src, dst, ssem, rsem, wide, narrow):
        return pltpu.make_async_remote_copy(
            src_ref=src, dst_ref=dst, send_sem=ssem, recv_sem=rsem,
            device_id=(wide, narrow), device_id_type=MESH,
        )

    def local(src, dst, sem):
        return pltpu.make_async_copy(src, dst, sem)

    def chunk_of(n):
        first = jnp.where(
            ph == 0,
            jnp.where(n < 12, 8 + mod(p + n, 8), 4 + mod(n, 4)),
            jnp.where(n < 8, 4 + mod(p + n, 4), 8 + mod(p + n, 8)),
        )
        first = jnp.where(n < 4, n, first)
        late = n - 16
        k = jnp.where(n < 16, 0, 1 + mod(late // 8, 2))
        side = jnp.where(n < 32, 1 - ph, ph)
        dest = jnp.where(n < 16, first, side * 8 + mod(p + n, 8))
        return k, dest

    def chunk_copy(n):
        k, dest = chunk_of(n)
        at = pl.multiple_of((k * 16 + dest) * CHUNK, CHUNK)
        slot = mod(n, 4)
        to = pl.multiple_of(slot * CHUNK, CHUNK)
        return local(child.at[pl.ds(at, CHUNK)], chunk_buf.at[pl.ds(to, CHUNK)], s_chunk.at[slot])

    for n in range(4):
        chunk_copy(jnp.int32(n)).start()
    marks_load = local(child_map, marks, s_marks.at[0])
    marks_load.start()
    front_load = local(root, front, s_front.at[0])
    front_load.start()

    barrier = pltpu.get_barrier_semaphore()

    def greet(wide, narrow):
        pl.semaphore_signal(barrier, inc=1, device_id=(wide, narrow), device_id_type=MESH)

    def greet_wide(i, carry):
        greet(mod(p + i, 16), q)
        return carry

    lax.fori_loop(1, 16, greet_wide, 0)
    for i in range(1, 4):
        greet(p, zl * 4 + mod(y + i, 4))


    def greet_plane(i, carry):
        greet(i, q_other)
        return carry

    lax.fori_loop(0, 16, greet_plane, 0)
    pl.semaphore_wait(barrier, 34)

    def packed(n, la, lb):
        base = mod(n, 4) * CHUNK
        xa = chunk_buf[pl.ds(base + la, HALF, stride=COL_BLOCKS), :]
        xb = chunk_buf[pl.ds(base + lb, HALF, stride=COL_BLOCKS), :]
        return jnp.concatenate([xa, xb], axis=1)

    def next_chunk(n):
        @pl.when(n + 4 < 48)
        def _():
            chunk_copy(n + 4).start()

    def unit_copy(u):
        slot = u // 8
        owner = mod(u, 8) * 2 + (slot > 0).astype(jnp.int32)
        return owner, remote(
            bulk_out.at[mod(u, 4) * 3, u // 4], unit_in.at[slot * 8 + chip], unit_s.at[u], unit_r.at[slot * 8 + chip],
            owner, q,
        )

    def front_copy(m):
        u = m * 4 + p
        slot = u // 8
        owner = mod(u, 8) * 2 + (slot > 0).astype(jnp.int32)
        return owner, slot, remote(
            front_out.at[m], front_in.at[slot], front_s.at[m], front_r.at[slot], owner, q
        )

    zh = ph
    xs = mod(chip, 4)

    def bulk_copy(k, dest):
        kk = 2 * k + core
        return remote(
            bulk_out.at[dest * 3 + k], bulk_in.at[kk * 8 + chip],
            bulk_s.at[dest * 3 + k], bulk_r.at[kk * 8 + chip], dest, q,
        )

    def keep_copy(k):
        return local(bulk_out.at[p * 3 + k], bulk_in.at[(2 * k + core) * 8 + chip], keep_s.at[k])

    def first_copy(k, dest):
        xd = mod(dest // 2, 4)
        far = mod(xd - xs + 6, 4) == 0
        xi = jnp.where(far, mod(xd + 1, 4), xd)
        gap = mod(xs - xi + 4, 4)
        way = jnp.where(far, 3, jnp.where(gap == 3, 2, gap))
        zi = jnp.where(mod(core + xs + k, 2) == 0, zh, 1 - zh)
        slot = k * 8 + way * 2 + core
        return remote(
            bulk_out.at[dest * 3 + k], relay.at[slot], bulk_s.at[dest * 3 + k],
            relay_r.at[slot], (zi * 4 + xi) * 2 + mod(dest, 2), q_other,
        )

    def second_copy(k, way, cs):
        slot = k * 8 + way * 2 + cs
        side = jnp.where(jnp.logical_or(way == 1, way == 3), 1, jnp.where(way == 2, 3, 0))
        source_x = mod(xs + side, 4)
        dest_x = jnp.where(way == 3, mod(xs + 3, 4), xs)
        source_z = jnp.where(mod(cs + source_x + k, 2) == 0, zh, 1 - zh)
        dest = ((1 - source_z) * 4 + dest_x) * 2 + core
        place = (2 * k + cs) * 8 + source_z * 4 + source_x
        return dest, remote(
            relay.at[slot], bulk_in.at[place], relay_s.at[slot], bulk_r.at[place], dest, q_other
        )

    def relay_one(i, carry):
        k, way, cs = i // 8, mod(i, 8) // 2, mod(i, 2)
        dest, copy = second_copy(k, way, cs)

        @pl.when(jnp.logical_not(panel_row(2 * k + cs, dest)))
        def _():
            remote(
                bulk_out.at[0], relay.at[i], bulk_s.at[0], relay_r.at[i], p, q_other
            ).wait_recv()
            copy.start()
        return carry

    def panel_row(kk, dest):
        return jnp.logical_and(kk == 0, dest < 4)

    def pack(n, carry):
        chunk_copy(n).wait()
        k, dest = chunk_of(n)

        def one(m, c):
            bulk_out[dest * 3 + k, m] = packed(n, 2 * m, 2 * m + 1)
            return c

        lax.fori_loop(0, 6, one, 0)

        @pl.when(panel_row(2 * k + core, dest))
        def _():
            def unit(m, c):
                u = m * 4 + dest
                owner, copy = unit_copy(u)

                @pl.when(owner != p)
                def _():
                    copy.start()

                @pl.when(owner == p)
                def _():
                    unit_in[(u // 8) * 8 + chip] = bulk_out[dest * 3, m]
                return c

            lax.fori_loop(0, 6, unit, 0)
        next_chunk(n)
        return carry

    def fire(n, carry):
        k, dest = chunk_of(n)

        @pl.when(jnp.logical_not(panel_row(2 * k + core, dest)))
        def _():
            crossing = dest // 8 != ph

            @pl.when(crossing)
            def _():
                first_copy(k, dest).start()

            @pl.when(jnp.logical_not(jnp.logical_or(crossing, dest == p)))
            def _():
                bulk_copy(k, dest).start()

            @pl.when(dest == p)
            def _():
                keep_copy(k).start()
        return carry

    def pack_fire(n, carry):
        return fire(n, pack(n, carry))

    class Beside:
        def __init__(self, first):
            self.first = first

        def begin(self, b):
            chunk_copy(self.first + b).wait()

        def work(self, b):
            n = self.first + b
            k, dest = chunk_of(n)
            for m in range(6):
                bulk_out[dest * 3 + k, m] = packed(n, 2 * m, 2 * m + 1)

        def end(self, b):
            next_chunk(self.first + b)
            fire(self.first + b, 0)

    lax.fori_loop(0, 4, pack, 0)
    front_load.wait()

    @pl.when(p < 4)
    def _():
        def one(m, c):
            for h in range(2):
                front_out[m, :, h * 128 : h * 128 + 128] = front[
                    pl.ds(2 * m + h, BLOCK, stride=COL_BLOCKS), :
                ]
            owner, slot, copy = front_copy(m)

            @pl.when(owner != p)
            def _():
                copy.start()

            @pl.when(owner == p)
            def _():
                front_in[slot] = front_out[m]
            return c

        lax.fori_loop(0, 6, one, 0)

    def assemble(source, m, row):
        sides = []
        for h in range(2):
            total = jnp.zeros((BLOCK, BLOCK), F32)
            for pair_id in range(CHILDREN // 2):
                parts = []
                for g in (2 * pair_id, 2 * pair_id + 1):
                    place = jnp.broadcast_to(col_places[2 * m + h, g : g + 1, :], (HALF, 128))
                    taken = jnp.take_along_axis(
                        source(g), jnp.maximum(place, 0), axis=1, mode="promise_in_bounds"
                    )
                    parts.append(jnp.where(place >= 0, taken, 0.0))
                turned = jnp.concatenate(parts, axis=0).T
                order = jnp.broadcast_to(row_perms[row, pair_id : pair_id + 1, :], (BLOCK, BLOCK))
                total += jnp.take_along_axis(turned, order, axis=1, mode="promise_in_bounds")
            sides.append(total.T)
        return sides

    def cols_at(u):
        return cols.at[u // 4, pl.ds(pl.multiple_of(mod(u, 4) * 128, 128), 128), :]

    def cross_copy(u):
        return remote(
            cols_at(u), cols_at(u), cols_s.at[(u // 8) * 8], cols_r.at[u],
            mod(chip + 4, 8) * 2 + core, q,
        )

    def along_copy(u, dx):
        far = jnp.where(mod(u, 8) == chip, 0, 3)
        return remote(
            cols_at(u), cols_at(u), cols_s.at[(u // 8) * 8 + far + dx], cols_r.at[u],
            (ph * 4 + mod(chip + dx, 4)) * 2 + core, q,
        )

    def along(u):
        def send(dx, c):
            along_copy(u, dx).start()
            return c

        lax.fori_loop(1, 4, send, 0)

    def hand_copy(u):
        return remote(cols_at(u), cols_at(u), hand_s.at[u], cols_r.at[u], chip * 2 + 1 - core, q)

    def own_unit(slot, carry):
        u = slot * 8 + chip
        block = mod(u, 4)

        def landed(g, c):
            @pl.when(jnp.logical_or(core == 1, g != chip))
            def _():
                remote(
                    bulk_out.at[0, 0], unit_in.at[slot * 8 + g], unit_s.at[0],
                    unit_r.at[slot * 8 + g], g * 2, q,
                ).wait_recv()
            return c

        lax.fori_loop(0, 8, landed, 0)

        @pl.when(block != p)
        def _():
            remote(
                front_out.at[0], front_in.at[slot], front_s.at[0], front_r.at[slot], block, q
            ).wait_recv()

        sides = assemble(lambda g: unit_in[slot * 8 + g], u // 4, 6)
        cols[u // 4, pl.ds(pl.multiple_of(block * 128, 128), 128), :] = (
            jnp.concatenate(sides, axis=1) + front_in[slot]
        )

        cross_copy(u).start()
        along(u)
        hand_copy(u).start()
        return carry

    def spread_on(slot, carry):
        u = slot * 8 + mod(chip + 4, 8)
        cross_copy(u).wait_recv()
        along(u)
        hand_copy(u).start()
        return carry

    def hand_on(u, carry):
        @pl.when(mod(u - chip + 32, 4) != 0)
        def _():
            cross_copy(u).wait_recv()
            hand_copy(u).start()
        return carry

    def taken(u, carry):
        hand_copy(u).wait_recv()
        return carry

    first_slot = core
    last_slot = 1 + 2 * core

    lax.fori_loop(0, 4, fire, 0)
    lax.fori_loop(4, 8, pack_fire, 0)

    marks_load.wait()
    ranks = lax.broadcasted_iota(jnp.int32, (HALF, 128), 0)
    spots = lax.broadcasted_iota(jnp.int32, (HALF, 128), 1)

    def places(block):
        at = pl.multiple_of((block // 2) * 128, 128)
        part = marks[:, pl.ds(at, 128)]
        mine = jnp.where(mod(block, 2) == 0, part, pltpu.roll(part, 64, 1)) - block * BLOCK
        tall = mine.T
        found = []
        for g in range(CHILDREN):
            hit = jnp.broadcast_to(tall[0:HALF, g : g + 1], (HALF, 128)) == spots
            found.append(jnp.max(jnp.where(hit, ranks, -1), axis=0, keepdims=True))
        return found

    def row_table(i, carry, block=None):
        found = places(i * 16 + p if block is None else block)
        for j in range(4):
            first, second = found[2 * j], found[2 * j + 1]
            row_perms[i, j : j + 1, :] = jnp.where(first >= 0, first, second + HALF)
        return carry


    def col_table(l, carry):
        found = places(l * 8 + q)
        for g in range(CHILDREN):
            col_places[l, g : g + 1, :] = jnp.where(
                found[g] >= 0, found[g] + mod(l, 2) * HALF, -1
            )
        return carry

    row_table(6, 0, mod(chip, 4))

    class Tables:
        def begin(self, b):
            pass

        def work(self, b):
            col_table(jnp.minimum(2 * b, 11), 0)
            col_table(jnp.minimum(2 * b + 1, 11), 0)
            row_table(jnp.minimum(b, 5), 0)

        def end(self, b):
            pass

    def unit_table(slot, carry):
        m = slot * 2 + chip // 4
        return col_table(2 * m + 1, col_table(2 * m, carry))

    lax.fori_loop(core, 1 + 2 * core, unit_table, 0)
    lax.fori_loop(first_slot, last_slot, own_unit, 0)
    lax.fori_loop(first_slot, last_slot, spread_on, 0)
    lax.fori_loop(8, 10, pack_fire, 0)

    @pl.when(core == 0)
    def _():
        lax.fori_loop(0, 4, hand_on, 0)

    @pl.when(core == 1)
    def _():
        lax.fori_loop(0, 4, taken, 0)

    dz = remote(diag.at[y], diag.at[y], dz_s.at[0], dz_r.at[0], p, q_other)

    @pl.when(zl == 0)
    def _():
        diag[y] = cols[0, :, 0:128]
        dz.start()

    @pl.when(zl == 1)
    def _():
        dz.wait_recv()

    def dy(i):
        return remote(diag.at[y], diag.at[y], dy_s.at[i], dy_r.at[y], p, zl * 4 + mod(y + i, 4))

    for i in range(1, 4):
        dy(i).start()


    @pl.when(core == 0)
    def _():
        lax.fori_loop(4, 8, hand_on, 0)
        lax.fori_loop(8, 24, taken, 0)

    @pl.when(core == 1)
    def _():
        lax.fori_loop(8, 24, hand_on, 0)
        lax.fori_loop(4, 8, taken, 0)

    def r1(c):
        return remote(
            cols.at[:, pl.ds(c * 128, 128), pl.ds(pl.multiple_of(ph * 128, 128), 128)],
            rows.at[c], r1_s.at[c], r1_r.at[0], p, zl * 4 + c,
        )

    rz = remote(rows.at[y], rows.at[y], rz_s.at[0], rz_r.at[0], p, q_other)

    def ry(i):
        return remote(rows.at[y], rows.at[y], ry_s.at[i], ry_r.at[y], p, zl * 4 + mod(y + i, 4))

    @pl.when(own)
    def _():
        for c in range(4):
            @pl.when(y != c)
            def _():
                r1(c).start()

            @pl.when(y == c)
            def _():
                rows[c] = cols[:, c * 128 : c * 128 + 128, pl.ds(pl.multiple_of(ph * 128, 128), 128)]


    lax.fori_loop(10, 20, pack_fire, 0)

    holder = zl == pl8 // 4

    @pl.when(holder)
    def _():
        @pl.when(jnp.logical_not(own))
        def _():
            remote(
                rows.at[y], rows.at[y], r1_s.at[0], r1_r.at[0], p, q_other
            ).wait_recv()
        rz.start()

    lax.fori_loop(20, 32, pack_fire, 0)

    for i in range(1, 4):
        src = mod(y + i, 4)
        remote(diag.at[src], diag.at[src], dy_s.at[i], dy_r.at[src], p, q_other).wait_recv()

    for c in range(4):
        work[:, c * 128 : c * 128 + 128] = diag[c]
    full = work[:, 0:SPAN]
    work[:, 0:SPAN] = 0.5 * (full + full.T)
    work[:, SPAN:] = jnp.zeros((SPAN, SPAN), F32)

    lax.fori_loop(0, 8, relay_one, 0)
    factor_block(0, work, pair, Beside(32))

    @pl.when(jnp.logical_not(holder))
    def _():
        rz.wait_recv()

    for i in range(1, 4):
        ry(i).start()

    lax.fori_loop(8, 16, relay_one, 0)
    factor_block(1, work, pair, Beside(40))
    lax.fori_loop(16, 24, relay_one, 0)
    factor_block(2, work, pair, None)
    factor_block(3, work, pair, Tables())

    def sent_unit(slot, carry):
        u = slot * 8 + chip

        cross_copy(u).wait_send()

        def one(dx, c):
            along_copy(u, dx).wait_send()
            along_copy(slot * 8 + mod(chip + 4, 8), dx).wait_send()
            return c

        lax.fori_loop(1, 4, one, 0)
        hand_copy(u).wait_send()
        return carry

    lax.fori_loop(first_slot, last_slot, sent_unit, 0)

    def handed(u, carry):
        @pl.when(mod(u, 8) != chip)
        def _():
            hand_copy(u).wait_send()
        return carry

    @pl.when(core == 0)
    def _():
        lax.fori_loop(0, 8, handed, 0)

    @pl.when(core == 1)
    def _():
        lax.fori_loop(8, 24, handed, 0)

    @pl.when(zl == 0)
    def _():
        dz.wait_send()

    for i in range(1, 4):
        dy(i).wait_send()

    @pl.when(own)
    def _():
        for c in range(4):
            @pl.when(y != c)
            def _():
                r1(c).wait_send()

    @pl.when(holder)
    def _():
        rz.wait_send()

    for i in range(1, 4):
        ry(i).wait_send()

    for i in range(1, 4):
        src = mod(y + i, 4)
        remote(rows.at[src], rows.at[src], ry_s.at[i], ry_r.at[src], p, q_other).wait_recv()

    inverse_h, inverse_l = halves(work[:, SPAN:])
    inv_h[...] = inverse_h
    inv_l[...] = inverse_l

    def solve(block):
        high, low = halves(block)
        total = jnp.dot(inv_h[...], high, preferred_element_type=F32)
        total += jnp.dot(inv_h[...], low, preferred_element_type=F32)
        total += jnp.dot(inv_l[...], high, preferred_element_type=F32)
        return total

    def solve_rows(i, carry):
        parts = [
            jnp.concatenate([rows[c, 2 * i + h] for c in range(4)], axis=0) for h in range(2)
        ]
        turned = solve(jnp.concatenate(parts, axis=1)).T
        at = pl.multiple_of(i * 256, 256)
        high, low = halves(turned)
        rows_h[pl.ds(at, 256), :] = high
        rows_l[pl.ds(at, 256), :] = low
        for c in range(4):
            rows_f[c, pl.ds(at, 256), :] = turned[:, c * 128 : c * 128 + 128]
        return carry

    lax.fori_loop(0, 3, solve_rows, 0)

    def solve_cols(m, carry):
        solved = solve(cols[m])
        high, low = halves(solved)
        cols[m] = solved
        total = jnp.dot(rows_h[...], high, preferred_element_type=F32)
        total += jnp.dot(rows_h[...], low, preferred_element_type=F32)
        total += jnp.dot(rows_l[...], high, preferred_element_type=F32)
        prod[...] = total

        def less(kk, c):
            at = pl.multiple_of(kk * 128, 128)
            for h in range(2):
                where = pl.ds(kk * (128 * COL_BLOCKS) + 2 * m + h, BLOCK, stride=COL_BLOCKS)
                front[where, :] = (
                    front[where, :] - prod[pl.ds(at, 128), h * 128 : h * 128 + 128]
                )
            return c

        lax.fori_loop(0, 6, less, 0)
        return carry

    lax.fori_loop(0, 6, solve_cols, 0)

    def store(kk):
        at = pl.multiple_of(kk * (128 * COL_BLOCKS), 128 * COL_BLOCKS)
        span = pl.ds(at, 128 * COL_BLOCKS)
        return local(front.at[span], out.at[span], s_out.at[kk])

    @pl.when(p < 4)
    def _():
        for l in range(COL_BLOCKS):
            @pl.when(l * 8 + q > p)
            def _():
                front[pl.ds(l, BLOCK, stride=COL_BLOCKS), :] = cols[
                    l // 2, pl.ds(pl.multiple_of(p * 128, 128), 128),
                    (l % 2) * 128 : (l % 2) * 128 + 128,
                ]

    @pl.when(q < 4)
    def _():
        for kk in range(ROW_BLOCKS):
            @pl.when(kk * 16 + p > q)
            def _():
                front[pl.ds(kk * (128 * COL_BLOCKS), BLOCK, stride=COL_BLOCKS), :] = rows_f[
                    q, kk * 128 : kk * 128 + 128, :
                ]

        @pl.when(p == q)
        def _():
            tile = rows_f[q, 0:128, :]
            lower = lax.broadcasted_iota(jnp.int32, (128, 128), 0) >= lax.broadcasted_iota(
                jnp.int32, (128, 128), 1
            )
            front[pl.ds(0, BLOCK, stride=COL_BLOCKS), :] = jnp.where(lower, tile, tile.T)

    def arrived(kk):
        def landed(g, c):
            mine = jnp.logical_and(g == chip, mod(kk, 2) == core)

            @pl.when(jnp.logical_not(mine))
            def _():
                remote(
                    bulk_out.at[0], bulk_in.at[kk * 8 + g], bulk_s.at[0], bulk_r.at[kk * 8 + g],
                    g * 2 + mod(kk, 2), q,
                ).wait_recv()

            @pl.when(mine)
            def _():
                keep_copy(kk // 2).wait()
            return c

        lax.fori_loop(0, 8, landed, 0)

    def early(kk, carry):
        @pl.when(jnp.logical_not(panel_row(kk, p)))
        def _():
            arrived(kk)
            at = pl.multiple_of(kk * 8, 8)
            load = local(bulk_in.at[pl.ds(at, 8)], kids, kids_s.at[0])
            load.start()
            set_pick(pick, row_perms, kk)
            load.wait()

            def one(m, c):
                total = add_pair(m, col_places, lambda g: kids[g, m], pick, wide_buf)
                for h in range(2):
                    where = pl.ds(kk * (128 * COL_BLOCKS) + 2 * m + h, BLOCK, stride=COL_BLOCKS)
                    side = total[:, h * 128 : h * 128 + 128]
                    if h == 0:
                        side = jnp.where(jnp.logical_and(m == 0, q < 4), 0.0, side)
                    front[where, :] = front[where, :] + side
                return c

            lax.fori_loop(0, 6, one, 0)
        store(kk).start()
        return carry

    lax.fori_loop(EARLY, 6, lambda kk, c: (store(kk).start(), c)[1], 0)
    lax.fori_loop(0, EARLY, early, 0)
    lax.fori_loop(EARLY, 6, lambda kk, c: (arrived(kk), c)[1], 0)
    tables = [
        local(row_perms, row_out, tab_s.at[0]), local(col_places, col_out, tab_s.at[1])
    ]
    for copy in tables:
        copy.start()
    for copy in tables:
        copy.wait()

    def sent_bulk(n, carry):
        k, dest = chunk_of(n)

        @pl.when(jnp.logical_not(jnp.logical_or(dest == p, panel_row(2 * k + core, dest))))
        def _():
            bulk_copy(k, dest).wait_send()
        return carry

    lax.fori_loop(0, 48, sent_bulk, 0)

    @pl.when(core == 0)
    def _():
        def one(u, c):
            owner, copy = unit_copy(u)

            @pl.when(owner != p)
            def _():
                copy.wait_send()
            return c

        lax.fori_loop(0, 24, one, 0)

    @pl.when(p < 4)
    def _():
        def one(m, c):
            owner, slot, copy = front_copy(m)

            @pl.when(owner != p)
            def _():
                copy.wait_send()
            return c

        lax.fori_loop(0, 6, one, 0)

    def relayed(i, carry):
        k, way, cs = i // 8, mod(i, 8) // 2, mod(i, 2)
        dest, copy = second_copy(k, way, cs)

        @pl.when(jnp.logical_not(panel_row(2 * k + cs, dest)))
        def _():
            copy.wait_send()
        return carry

    lax.fori_loop(0, 24, relayed, 0)

    def stored(kk, carry):
        store(kk).wait()
        return carry

    lax.fori_loop(0, 6, stored, 0)


def set_pick(pick, row_perms, kk):
    level = lax.broadcasted_iota(jnp.int32, (128, 128), 1)
    for j in range(4):
        order = jnp.broadcast_to(row_perms[kk, j : j + 1, :], (128, 128)).T
        table = jnp.where(order == level, 1.0, 0.0).astype(BF16)
        pick[:, j * 128 : j * 128 + 128] = table
        pick[:, 512 + j * 128 : 640 + j * 128] = table


def add_pair(m, col_places, child_of, pick, wide_buf):
    for g in range(CHILDREN):
        for h in range(2):
            place = jnp.broadcast_to(col_places[2 * m + h, g : g + 1, :], (HALF, 128))
            taken = jnp.take_along_axis(
                child_of(g), jnp.maximum(place, 0), axis=1, mode="promise_in_bounds"
            )
            high, low = halves(jnp.where(place >= 0, taken, 0.0))
            wide_buf[g * 64 : g * 64 + 64, h * 128 : h * 128 + 128] = high
            wide_buf[512 + g * 64 : 576 + g * 64, h * 128 : h * 128 + 128] = low
    return jnp.dot(pick[...], wide_buf[...], preferred_element_type=F32)


EARLY = 4


def add_children(row_perms, col_places, front, children, out, pick, wide_buf):
    kk = mod(pl.program_id(0) + EARLY, ROW_BLOCKS)
    q = lax.axis_index("narrow")

    @pl.when(kk < EARLY)
    def _():
        out[...] = front[...]

    @pl.when(kk >= EARLY)
    def _():
        set_pick(pick, row_perms, kk)

        def one(m, carry):
            total = add_pair(m, col_places, lambda g: children[g, m], pick, wide_buf)
            for h in range(2):
                where = pl.ds(2 * m + h, BLOCK, stride=COL_BLOCKS)
                side = total[:, h * 128 : h * 128 + 128]
                if h == 0:
                    side = jnp.where(jnp.logical_and(m == 0, q < 4), 0.0, side)
                out[where, :] = front[where, :] + side
            return carry

        lax.fori_loop(0, 6, one, 0)


def body(root_front, child_update, child_map):
    child = child_update.reshape(3 * 16 * CHUNK, HALF)
    root = root_front.reshape(ROW_BLOCKS * BLOCK * COL_BLOCKS, BLOCK)
    vmem = lambda *shape: pltpu.VMEM(shape, F32)
    sems = lambda n: pltpu.SemaphoreType.DMA((n,))
    front, children, row_perms, col_places = pl.pallas_call(
        kernel,
        out_shape=[
            jax.ShapeDtypeStruct(root.shape, F32),
            jax.ShapeDtypeStruct((48, 6, HALF, 128), F32),
            jax.ShapeDtypeStruct((8, 4, 128), jnp.int32),
            jax.ShapeDtypeStruct((COL_BLOCKS, CHILDREN, 128), jnp.int32),
        ],
        in_specs=[pl.BlockSpec(memory_space=pl.ANY)] * 3,
        out_specs=[pl.BlockSpec(memory_space=pl.ANY)] * 4,
        scratch_shapes=[
            pltpu.VMEM((CHILDREN, 6144), jnp.int32),
            pltpu.VMEM((8, 4, 128), jnp.int32),
            pltpu.VMEM((COL_BLOCKS, CHILDREN, 128), jnp.int32),
            vmem(4 * CHUNK, HALF),
            vmem(ROW_BLOCKS * BLOCK * COL_BLOCKS, BLOCK),
            vmem(48, 6, HALF, 128),
            vmem(24, HALF, 128),
            vmem(6, BLOCK, 256),
            vmem(3, BLOCK, 256),
            vmem(6, SPAN, 256),
            vmem(4, SPAN, 128),
            vmem(4, 6, BLOCK, BLOCK),
            vmem(SPAN, 2 * SPAN),
            vmem(BLOCK, 2 * BLOCK),
            vmem(4, 768, BLOCK),
            pltpu.VMEM((768, SPAN), BF16),
            pltpu.VMEM((768, SPAN), BF16),
            vmem(768, 256),
            pltpu.VMEM((SPAN, SPAN), BF16),
            pltpu.VMEM((SPAN, SPAN), BF16),
            vmem(24, 6, HALF, 128),
            vmem(CHILDREN, 6, HALF, 128),
            pltpu.VMEM((BLOCK, 1024), BF16),
            pltpu.VMEM((1024, 256), BF16),
            sems(1), sems(3), sems(2), sems(1), sems(4), sems(1), sems(6), sems(24), sems(24), sems(48), sems(48), sems(24), sems(24),
            sems(6), sems(3), sems(24), sems(24), sems(24), sems(1), sems(1), sems(4), sems(4),
            sems(4), sems(1), sems(1), sems(1), sems(4), sems(4),
        ],
        compiler_params=pltpu.CompilerParams(
            collective_id=0, has_side_effects=True, vmem_limit_bytes=60 * 2**20
        ),
    )(child_map, child, root)
    part = pl.BlockSpec((BLOCK * COL_BLOCKS, BLOCK), lambda i: (mod(i + EARLY, ROW_BLOCKS), 0))
    out = pl.pallas_call(
        add_children,
        grid=(ROW_BLOCKS,),
        out_shape=jax.ShapeDtypeStruct(root.shape, F32),
        in_specs=[
            pl.BlockSpec((8, 4, 128), lambda i: (0, 0, 0)),
            pl.BlockSpec((COL_BLOCKS, CHILDREN, 128), lambda i: (0, 0, 0)),
            part,
            pl.BlockSpec(
                (CHILDREN, 6, HALF, 128),
                lambda i: (jnp.minimum(i + EARLY, ROW_BLOCKS - 1), 0, 0, 0),
            ),
        ],
        out_specs=part,
        scratch_shapes=[pltpu.VMEM((BLOCK, 1024), BF16), pltpu.VMEM((1024, 256), BF16)],
        compiler_params=pltpu.CompilerParams(vmem_limit_bytes=60 * 2**20),
    )(row_perms, col_places, front, children)
    return out.reshape(root_front.shape)


def solution(mesh):
    return jax.shard_map(
        body,
        mesh=mesh,
        in_specs=(
            P(None, "wide", None, None, "narrow", None),
            P("wide", None, None, None, None, "narrow", None),
            P(),
        ),
        out_specs=P(None, "wide", None, None, "narrow", None),
        check_vma=False,
    )
```
